32 devices in a mesh: wide: 8 (over z, x), narrow: 4 (over y, core).
Axes of the slice: x: 2, y: 2, z: 4, core: 2. Of those that a mesh axis runs over, the one named last changes fastest.
Arguments:
- table: bfloat16 [6291456, 16], P(('wide', 'narrow')), may hold values from -6 to 6
- dense: float32 [16384, 16], P(('wide', 'narrow')), may hold values from -400 to 400
- domains: int32 [16384], P(('wide', 'narrow')), may hold values from 0 to 1, as said below
- lengths: int32 [32, 512], P(('wide', 'narrow')), may hold values from 1 to 200, 32768 in all within a row
- requests: int32 [32, 32, 256], P(('wide', 'narrow')), may hold values from 0 to 196607, as said below
- counts: int32 [32, 32], P(('wide', 'narrow')), may hold values from 64 to 256
- field_slots: int32 [16384, 38], P(('wide', 'narrow')), may hold values from 0 to 8191, as said below
- behave_slots: int32 [32, 32768], P(('wide', 'narrow')), may hold values from 0 to 8191, as said below
- proj_w: bfloat16 [640, 512], replicated, may hold values from -0.25 to 0.25
- proj_b: float32 [512], replicated, may hold values from -3 to 3
- inter_gain: float32 [512], replicated, may hold values from 0.5 to 1.5
- inter_bias: float32 [512], replicated, may hold values from -3 to 3
- w_in: bfloat16 [4, 512, 1024], replicated, may hold values from -0.25 to 0.25
- b_in: float32 [4, 1024], replicated, may hold values from -3 to 3
- w_out: bfloat16 [4, 1024, 512], replicated, may hold values from -0.1875 to 0.1875
- b_out: float32 [4, 512], replicated, may hold values from -3 to 3
- expert_gain: float32 [4, 512], replicated, may hold values from 0.5 to 1.5
- expert_bias: float32 [4, 512], replicated, may hold values from -3 to 3
- shared_gate: bfloat16 [512, 2], replicated, may hold values from -0.25 to 0.25
- group_gate: bfloat16 [2, 512, 2], replicated, may hold values from -0.25 to 0.25
- tower_in: bfloat16 [2, 512, 256], replicated, may hold values from -0.25 to 0.25
- tower_in_bias: float32 [2, 256], replicated, may hold values from -3 to 3
- tower_out: float32 [2, 256], replicated, may hold values from -0.375 to 0.375
- tower_out_bias: float32 [2], replicated, may hold values from -3 to 3
- pred_cotangent: float32 [16384], P(('wide', 'narrow')), may hold values from -6 to 6
Outputs:
- pred: float32 [16384], P(('wide', 'narrow'))
- dense_grad: float32 [16384, 16], P(('wide', 'narrow'))
- table_grad: float32 [6291456, 16], P(('wide', 'narrow'))
- proj_w_grad: float32 [640, 512], replicated
- proj_b_grad: float32 [512], replicated
- inter_gain_grad: float32 [512], replicated
- inter_bias_grad: float32 [512], replicated
- w_in_grad: float32 [4, 512, 1024], replicated
- b_in_grad: float32 [4, 1024], replicated
- w_out_grad: float32 [4, 1024, 512], replicated
- b_out_grad: float32 [4, 512], replicated
- expert_gain_grad: float32 [4, 512], replicated
- expert_bias_grad: float32 [4, 512], replicated
- shared_gate_grad: float32 [512, 2], replicated
- group_gate_grad: float32 [2, 512, 2], replicated
- tower_in_grad: float32 [2, 512, 256], replicated
- tower_in_bias_grad: float32 [2, 256], replicated
- tower_out_grad: float32 [2, 256], replicated
- tower_out_bias_grad: float32 [2], replicated
The draws below stay inside these ranges and needn't reach their ends.
Inputs may be any that keep to these rules, and one draw needn't show every extreme that they name: Within one block of 256 requests from one device to one owner the rows are distinct; slots at or past the block's count are padding. `field_slots`: each entry is o * 256 + j for an owner o and a live slot j of the event's device. `behave_slots`: each entry is o * 256 + j for an owner o and a live slot j of that device. `domains`: every device holds events of every domain. Each device's lengths sum to 32768.
All inputs are finite; a program needn't handle non-finite values.
Results may differ from the reference program's by a relative error of at most 0.011.
Values may be sent and summed in bfloat16 or wider, within the bound.
A program may use at most 320 MiB of HBM per device.

```python
import math
from functools import partial
import jax
import jax.numpy as jnp
import numpy as np
from jax import lax

EMB = 16
NCAT = 38
INPUT = 640
D = 512
EXPERT_UNITS = 1024
TOWER = 256
SHARED = 2
DOMAINS = 2
EXPERTS = 4
ROWS_DEV = 196608
TABLE_ROWS = 6291456
EV_DEV = 512
EVENTS = 16384
SEQ_MAX = 200
PACK_DEV = 32768
CAP = 256
N_WIDE = 8
N_NARROW = 4


def owner_counts(key):
    devices = N_WIDE * N_NARROW
    levels = jax.random.randint(jax.random.fold_in(key, 101), (devices, devices), 0, 3)
    counts = jnp.right_shift(jnp.full((devices, devices), CAP, jnp.int32), levels)
    busiest = jax.random.randint(jax.random.fold_in(key, 102), (), 0, devices)
    owners = jnp.arange(devices, dtype=jnp.int32)
    full = jnp.logical_or(owners[None, :] == busiest, owners[None, :] == devices - 1)
    return jnp.where(full, CAP, counts).astype(jnp.int32)


def pick_slots(key, counts, source):
    devices = N_WIDE * N_NARROW
    owner = jax.random.randint(jax.random.fold_in(key, 11), source.shape, 0, devices)
    spread = jax.random.randint(jax.random.fold_in(key, 12), source.shape, 0, 1 << 30)
    live = counts[source, owner]
    slots = (owner * CAP + spread % live).astype(jnp.int32).reshape(-1)
    slots = slots.at[0].set(devices * CAP - 1).at[1].set(0)
    return slots.reshape(source.shape).astype(jnp.int32)


def draw_counts(key, part):
    return owner_counts(key)


def draw_requests(key, part):
    key = jax.random.fold_in(key, 2)
    devices = N_WIDE * N_NARROW
    stride = ROWS_DEV // CAP
    scores = jax.random.randint(jax.random.fold_in(key, 1), (devices, devices, CAP), 0, 1 << 20) * CAP + jnp.arange(CAP, dtype=jnp.int32)
    order = jnp.argsort(scores, axis=-1).astype(jnp.int32)
    offset = jax.random.randint(jax.random.fold_in(key, 4), (devices, devices, CAP), 0, stride)
    offset = jnp.where(order == CAP - 1, stride - 1, offset)
    offset = jnp.where(order == 0, 0, offset)
    return (order * stride + offset).astype(jnp.int32)


def draw_field_slots(key, part):
    counts = owner_counts(key)
    key = jax.random.fold_in(key, 3)
    source = jnp.broadcast_to((jnp.arange(EVENTS, dtype=jnp.int32) // EV_DEV)[:, None], (EVENTS, NCAT))
    return pick_slots(key, counts, source)


def draw_behave_slots(key, part):
    counts = owner_counts(key)
    key = jax.random.fold_in(key, 7)
    devices = N_WIDE * N_NARROW
    source = jnp.broadcast_to(jnp.arange(devices, dtype=jnp.int32)[:, None], (devices, PACK_DEV))
    return pick_slots(key, counts, source)


def draw_domains(key, part):
    key = jax.random.fold_in(key, 5)
    devices = N_WIDE * N_NARROW
    labels = jax.random.randint(jax.random.fold_in(key, 1), (EVENTS,), 0, DOMAINS)
    shift = jax.random.randint(jax.random.fold_in(key, 2), (devices,), 0, EV_DEV)
    place = jnp.arange(EVENTS, dtype=jnp.int32) % EV_DEV
    owner = jnp.arange(EVENTS, dtype=jnp.int32) // EV_DEV
    spot = (place - shift[owner]) % EV_DEV
    return jnp.where(spot < DOMAINS, spot, labels).astype(jnp.int32)


def draw_dense(key, part):
    key = jax.random.fold_in(key, 6)
    rows = jnp.arange(EVENTS, dtype=jnp.float32)[:, None] / max(EVENTS - 1, 1)
    columns = jnp.exp(jax.random.uniform(jax.random.fold_in(key, 1), (1, EMB)) * jnp.log(10.0))
    base = jax.random.truncated_normal(jax.random.fold_in(key, 2), -4.0, 4.0, (EVENTS, EMB))
    values = base * jnp.exp(rows * jnp.log(3.0)) * columns
    return jnp.clip(values, -400.0, 400.0).astype(jnp.float32)


def block_scale(own_key, dims, pieces, low, largest):
    def one(position, parts):
        draws = jax.random.uniform(jax.random.fold_in(jax.random.fold_in(own_key, 6), position), (parts,), jnp.float32, low / len(pieces), largest / len(pieces))
        return jnp.repeat(jnp.exp(draws), dims[position] // parts).reshape((-1,) + (1,) * (len(dims) - position - 1))

    factor_of = one(*pieces[0])
    for cut in pieces[1:]:
        factor_of = factor_of * one(*cut)
    return factor_of


def length_profile(amount, total, bound, lean):
    loads = [(1 << 20) // math.isqrt(grade ** lean) + 1 for grade in range(2, amount + 1)]
    spare, given = total - bound - (amount - 1), [1] * (amount - 1)
    while spare > 0:
        movable = [i for i in range(amount - 1) if given[i] < bound]
        whole, remaining = sum([loads[i] for i in movable]), spare
        for i in movable:
            addition = min(bound - given[i], max(1, remaining * loads[i] // whole), spare)
            given[i] = given[i] + addition
            spare = spare - addition
    return np.array([bound] + given)


def uneven_parts(own_key, number_of, total, bound, lean):
    if number_of == 2:
        one = jax.random.randint(own_key, (), max(1, total - bound), min(bound, total - 1) + 1)
        return jnp.stack([one, total - one])
    sizes = jnp.asarray(length_profile(number_of, total, bound, lean), jnp.int32)
    twos = (number_of - 1) // 2
    donor, taker = sizes[1:1 + 2 * twos:2], sizes[2:2 + 2 * twos:2]
    margin = jnp.minimum(donor - 1, bound - taker)
    moved = jax.random.randint(jax.random.fold_in(own_key, 1), (twos,), 0, 1 << 20) % (margin + 1)
    sizes = sizes.at[1:1 + 2 * twos:2].set(donor - moved).at[2:2 + 2 * twos:2].set(taker + moved)
    return sizes[jax.random.permutation(jax.random.fold_in(own_key, 2), number_of)]


def noise(rng, shape, scale, reach, shards=(), kind=jnp.bfloat16):
    loudness = block_scale(rng, shape, shards, -0.22, 0.18) if shards else 1.0
    entries = jax.random.normal(rng, shape, jnp.float32) * scale * loudness
    return jnp.minimum(jnp.maximum(entries, -reach), reach).astype(kind)


def setup_inputs(seed: int = 0) -> dict:
    key_of = jax.random.split(jax.random.key(seed), 26)
    table = noise(key_of[0], (TABLE_ROWS, EMB), 1.0, 6.0, ((0, 32),))
    dense = draw_dense(jax.random.fold_in(key_of[25], 71), 0)
    domains = draw_domains(jax.random.fold_in(key_of[25], 71), 0)
    lengths = jax.vmap(lambda own: uneven_parts(own, EV_DEV, PACK_DEV, SEQ_MAX, 2))(jax.random.split(key_of[3], (N_WIDE * N_NARROW))).reshape((N_WIDE * N_NARROW, EV_DEV)).astype(jnp.int32)
    requests = draw_requests(jax.random.fold_in(key_of[25], 71), 0)
    counts = draw_counts(jax.random.fold_in(key_of[25], 71), 0)
    field_slots = draw_field_slots(jax.random.fold_in(key_of[25], 71), 0)
    behave_slots = draw_behave_slots(jax.random.fold_in(key_of[25], 71), 0)
    proj_w = noise(key_of[8], (INPUT, D), INPUT ** -0.5, 0.25)
    proj_b = noise(key_of[9], (D,), 0.5, 3.0, (), jnp.float32)
    inter_gain = jnp.clip(1.0 + 0.1 * jax.random.normal(key_of[10], (D,), jnp.float32), 0.5, 1.5)
    inter_bias = noise(key_of[11], (D,), 0.5, 3.0, (), jnp.float32)
    w_in = noise(key_of[12], (EXPERTS, D, EXPERT_UNITS), D ** -0.5, 0.25)
    b_in = noise(key_of[13], (EXPERTS, EXPERT_UNITS), 0.5, 3.0, (), jnp.float32)
    w_out = noise(key_of[14], (EXPERTS, EXPERT_UNITS, D), EXPERT_UNITS ** -0.5, 0.1875)
    b_out = noise(key_of[15], (EXPERTS, D), 0.5, 3.0, (), jnp.float32)
    expert_gain = jnp.clip(1.0 + 0.1 * jax.random.normal(key_of[16], (EXPERTS, D), jnp.float32), 0.5, 1.5)
    expert_bias = noise(key_of[17], (EXPERTS, D), 0.5, 3.0, (), jnp.float32)
    shared_gate = noise(key_of[18], (D, SHARED), D ** -0.5, 0.25)
    group_gate = noise(key_of[19], (DOMAINS, D, 2), D ** -0.5, 0.25)
    tower_in = noise(key_of[20], (DOMAINS, D, TOWER), D ** -0.5, 0.25)
    tower_in_bias = noise(key_of[21], (DOMAINS, TOWER), 0.5, 3.0, (), jnp.float32)
    tower_out = noise(key_of[22], (DOMAINS, TOWER), TOWER ** -0.5, 0.375, (), jnp.float32)
    tower_out_bias = noise(key_of[23], (DOMAINS,), 1.0, 3.0, (), jnp.float32)
    pred_cotangent = noise(key_of[24], (EVENTS,), 1.0, 6.0, ((0, 32),), jnp.float32)
    return {"table": table, "dense": dense, "domains": domains, "lengths": lengths, "requests": requests, "counts": counts, "field_slots": field_slots, "behave_slots": behave_slots, "proj_w": proj_w, "proj_b": proj_b, "inter_gain": inter_gain, "inter_bias": inter_bias, "w_in": w_in, "b_in": b_in, "w_out": w_out, "b_out": b_out, "expert_gain": expert_gain, "expert_bias": expert_bias, "shared_gate": shared_gate, "group_gate": group_gate, "tower_in": tower_in, "tower_in_bias": tower_in_bias, "tower_out": tower_out, "tower_out_bias": tower_out_bias, "pred_cotangent": pred_cotangent}


EPSILON = 1e-05

@jax.custom_vjp
def low(v):
    return lax.optimization_barrier(v.astype(jnp.bfloat16)).astype(jnp.float32)

@jax.custom_vjp
def low_back(v):
    return v

def low_keep(v):
    return (low(v), None)

def low_pass(kept, grad):
    return (grad,)

def back_keep(v):
    return (v, None)

def back_low(kept, grad):
    return (low(grad),)
low.defvjp(low_keep, low_pass)
low_back.defvjp(back_keep, back_low)

def layer_norm(values, gain, shift):
    center = values - lax.optimization_barrier(jnp.mean(values, axis=-1, keepdims=True))
    spread = lax.optimization_barrier(jnp.mean(center * center, axis=-1, keepdims=True))
    return center * lax.rsqrt(spread + EPSILON) * gain + shift

def gelu_norm(pre, gain, shift):
    return layer_norm(jax.nn.gelu(pre), gain, shift)

def mixture(shared_logits, group_logits, outputs, onehot):
    shared_weights = jax.nn.softmax(shared_logits, axis=-1)
    shared_mix = lax.optimization_barrier(jnp.sum(shared_weights.T[:, :, None] * outputs[:SHARED], axis=0))
    picked = lax.optimization_barrier(jnp.sum(onehot[:, :, None] * group_logits, axis=1))
    group_weights = jax.nn.softmax(picked, axis=-1)
    domain_out = lax.optimization_barrier(jnp.sum(onehot.T[:, :, None] * outputs[SHARED:], axis=0))
    return group_weights[:, 0:1] * shared_mix + group_weights[:, 1:2] * domain_out

def tower_head(pre_stack, tower_out, tower_out_bias, onehot):
    hidden = jax.nn.gelu(pre_stack)
    logits = lax.optimization_barrier(jnp.sum(hidden * tower_out[:, None, :], axis=-1)) + tower_out_bias[:, None]
    return jax.nn.sigmoid(lax.optimization_barrier(jnp.sum(onehot.T * logits, axis=0)))

def matmul(left, right):
    return jnp.dot(left, right, precision=lax.Precision.HIGHEST)

def pick_rows(rows, index):
    return jnp.take(rows, index, axis=0)

def reference(table, dense, domains, lengths, requests, counts, field_slots, behave_slots, proj_w, proj_b, inter_gain, inter_bias, w_in, b_in, w_out, b_out, expert_gain, expert_bias, shared_gate, group_gate, tower_in, tower_in_bias, tower_out, tower_out_bias, pred_cotangent):
    devices = N_WIDE * N_NARROW
    onehot = (domains[:, None] == jnp.arange(DOMAINS, dtype=jnp.int32)[None, :]).astype(jnp.float32)
    live = (jnp.arange(CAP, dtype=jnp.int32)[None, None, :] < counts[:, :, None]).reshape(devices, devices * CAP, 1)
    global_rows = (jnp.arange(devices, dtype=jnp.int32)[None, :, None] * ROWS_DEV + requests).astype(jnp.int32).reshape(-1)
    ends = jnp.cumsum(lengths, axis=1).astype(jnp.int32)
    positions = jnp.arange(PACK_DEV, dtype=jnp.int32)

    def locate(row_ends):
        return jnp.searchsorted(row_ends, positions, side='right').astype(jnp.int32)
    owner_event = jax.vmap(locate)(ends)
    seq_len = lengths.astype(jnp.float32)[:, :, None]
    field_index = field_slots.reshape(devices, EV_DEV * NCAT)

    def forward(table_f, dense_f, proj_wf, proj_bf, inter_gf, inter_bf, w_inf, b_inf, w_outf, b_outf, expert_gf, expert_bf, shared_gf, group_gf, tower_inf, tower_ibf, tower_outf, tower_obf):
        gathered = jnp.take(table_f, global_rows, axis=0).reshape(devices, devices * CAP, EMB)
        slot_rows = jnp.where(live, gathered, jnp.zeros_like(gathered))
        fields = jax.vmap(pick_rows)(slot_rows, field_index).reshape(EVENTS, NCAT * EMB)
        behave = jax.vmap(pick_rows)(slot_rows, behave_slots)
        pooled = jax.vmap(partial(jax.ops.segment_sum, num_segments=EV_DEV))(behave, owner_event) / seq_len
        pooled = low(pooled.reshape(EVENTS, EMB))
        count = lax.optimization_barrier(jnp.sum(onehot, axis=0))[:, None]
        mean = matmul(onehot.T, dense_f) / count
        variance = matmul(onehot.T, dense_f * dense_f) / count - mean * mean
        inverse = lax.rsqrt(variance + EPSILON)
        centered = low((dense_f - matmul(onehot, mean)) * matmul(onehot, inverse))
        joined = jnp.concatenate([fields, pooled, centered], axis=1)
        pre_proj = low_back(matmul(joined, proj_wf) + proj_bf)
        state = gelu_norm(pre_proj, inter_gf, inter_bf)
        state_low = low(state)
        outputs = []
        for expert in range(EXPERTS):
            pre_in = low_back(matmul(state_low, w_inf[expert]) + b_inf[expert])
            active = low(jax.nn.gelu(pre_in))
            pre_out = low_back(matmul(active, w_outf[expert]) + b_outf[expert])
            outputs.append(layer_norm(pre_out, expert_gf[expert], expert_bf[expert]))
        outputs = jnp.stack(outputs)
        shared_logits = matmul(state_low, shared_gf)
        group_logits = jnp.einsum('ek,dkg->edg', state_low, group_gf, precision=lax.Precision.HIGHEST)
        after = state + mixture(shared_logits, group_logits, outputs, onehot)
        after_low = low(after)
        tower_pre = low_back(jnp.einsum('ek,dkj->dej', after_low, tower_inf, precision=lax.Precision.HIGHEST) + tower_ibf[:, None, :])
        return tower_head(tower_pre, tower_outf, tower_obf, onehot)
    floats = (table.astype(jnp.float32), dense, proj_w.astype(jnp.float32), proj_b, inter_gain, inter_bias, w_in.astype(jnp.float32), b_in, w_out.astype(jnp.float32), b_out, expert_gain, expert_bias, shared_gate.astype(jnp.float32), group_gate.astype(jnp.float32), tower_in.astype(jnp.float32), tower_in_bias, tower_out, tower_out_bias)
    pred, backward = jax.vjp(forward, *floats)
    grads = backward(pred_cotangent)
    return (pred, grads[1], grads[0], grads[2], grads[3], grads[4], grads[5], grads[6], grads[7], grads[8], grads[9], grads[10], grads[11], grads[12], grads[13], grads[14], grads[15], grads[16], grads[17])
```

```python
import functools
import math

import jax
import jax.numpy as jnp
from jax import lax
from jax.experimental import pallas as pl
from jax.experimental.pallas import tpu as pltpu
from jax.sharding import PartitionSpec as P

SHARED = 2
DOMAINS = 2


EPSILON = 1e-05
f32=jnp.float32; bf16=jnp.bfloat16
VM=60*1024*1024
NT=(((1,),(1,)),((),()))

def gather_kernel(asked_s, asked_v, tab, out, lines, got):
    step=pl.program_id(0); n=pl.num_programs(0)
    cols=tab.shape[1]; per=cols//1024
    eye=(lax.broadcasted_iota(jnp.int32,(128,128),0)==lax.broadcasted_iota(jnp.int32,(128,128),1)).astype(bf16)
    for c in range(per):
        stack=jnp.concatenate([tab[:,c*1024+g*128:c*1024+(g+1)*128] for g in range(8)],axis=0)
        lines[pl.ds(pl.multiple_of(step*(per*128),128)+c*128,128),:]=lax.dot_general(eye,stack,NT,preferred_element_type=f32)
    @pl.when(step==n-1)
    def _():
        blocks,cap=asked_v.shape[0],asked_v.shape[2]
        def one(s,carry):
            def inner(u,carry):
                for k in range(32):
                    j=u*32+k
                    r=asked_s[s*cap+j]
                    line=lax.shift_left(lax.shift_right_logical(r,10),7)+lax.bitwise_and(r,127)
                    got[pl.ds(j,1),:]=lines[pl.ds(line,1),:]
                return carry
            lax.fori_loop(0,cap//32,inner,0)
            t=lax.dot_general(eye,got[...].astype(bf16),NT,preferred_element_type=f32)
            grp=lax.bitwise_and(lax.shift_right_logical(asked_v[s],7),7)
            acc=jnp.zeros((16,cap),f32)
            for g in range(8):
                acc=jnp.where(grp==g,t[g*16:(g+1)*16],acc)
            out[s]=acc.astype(bf16)
            return carry
        lax.fori_loop(0,blocks,one,0)

def table_gather(tab_t, asked):
    width,rows=tab_t.shape; blocks,cap=asked.shape
    cols=8192
    return pl.pallas_call(gather_kernel,grid=(rows//cols,),
        in_specs=[pl.BlockSpec(memory_space=pltpu.SMEM),
                  pl.BlockSpec((blocks,1,cap),lambda i:(0,0,0)),
                  pl.BlockSpec((width,cols),lambda i:(0,i))],
        out_specs=pl.BlockSpec((blocks,width,cap),lambda i:(0,0,0)),
        out_shape=jax.ShapeDtypeStruct((blocks,width,cap),bf16),
        scratch_shapes=[pltpu.VMEM((rows//8,128),f32),pltpu.VMEM((cap,128),f32)],
        compiler_params=pltpu.CompilerParams(vmem_limit_bytes=VM),name="table_gather")(asked.reshape(-1),asked.reshape(blocks,1,cap),tab_t)

U=32
def scatter_kernel(asked_s, asked_v, ret, out, lines, vals):
    step=pl.program_id(0)
    cols=out.shape[1]; per=cols//1024
    @pl.when(step==0)
    def _():
        blocks,cap=asked_v.shape[0],asked_v.shape[2]
        def zero(i,carry):
            lines[pl.ds(pl.multiple_of(i*1024,1024),1024),:]=jnp.zeros((1024,128),f32)
            return carry
        lax.fori_loop(0,lines.shape[0]//1024,zero,0)
        near=lax.shift_right_logical(lax.broadcasted_iota(jnp.int32,(cap,cap),0),5)==lax.shift_right_logical(lax.broadcasted_iota(jnp.int32,(cap,cap),1),5)
        def one(s,carry):
            r=asked_v[s]
            grp=lax.bitwise_and(lax.shift_right_logical(r,7),7)
            line=lax.shift_left(lax.shift_right_logical(r,10),7)+lax.bitwise_and(r,127)
            own=ret[s].astype(f32)
            wide=jnp.concatenate([jnp.where(grp==g,own,0.0) for g in range(8)],axis=0).astype(bf16)
            across=jnp.broadcast_to(line.astype(f32),(cap,cap))
            same=jnp.where(jnp.logical_and(across==across.T,near),1.0,0.0).astype(bf16)
            vals[...]=lax.dot_general(same,wide,NT,preferred_element_type=f32)
            def inner(u,carry):
                where=[]; news=[]
                for k in range(U):
                    j=u*U+k
                    q=asked_s[s*cap+j]
                    at=lax.shift_left(lax.shift_right_logical(q,10),7)+lax.bitwise_and(q,127)
                    where.append(at)
                    news.append(lines[pl.ds(at,1),:]+vals[pl.ds(j,1),:])
                for at,new in zip(where,news):
                    lines[pl.ds(at,1),:]=new
                return carry
            lax.fori_loop(0,cap//U,inner,0)
            return carry
        lax.fori_loop(0,blocks,one,0)
    for c in range(per):
        t=lines[pl.ds(pl.multiple_of(step*(per*128),128)+c*128,128),:].T
        for g in range(8):
            out[:,c*1024+g*128:c*1024+(g+1)*128]=t[g*16:(g+1)*16]

def table_scatter(asked, ret, rows):
    blocks,cap=asked.shape; width=ret.shape[1]
    cols=8192
    return pl.pallas_call(scatter_kernel,grid=(rows//cols,),
        in_specs=[pl.BlockSpec(memory_space=pltpu.SMEM),
                  pl.BlockSpec((blocks,1,cap),lambda i:(0,0,0)),
                  pl.BlockSpec((blocks,width,cap),lambda i:(0,0,0))],
        out_specs=pl.BlockSpec((width,cols),lambda i:(0,i)),
        out_shape=jax.ShapeDtypeStruct((width,rows),f32),
        scratch_shapes=[pltpu.VMEM((rows//8,128),f32),pltpu.VMEM((cap,128),f32)],
        compiler_params=pltpu.CompilerParams(vmem_limit_bytes=VM),name="table_scatter")(asked.reshape(-1),asked.reshape(blocks,1,cap),ret)

PB=256
def slots_kernel(starts, rows, live, field, behave, joined, pooled_out, counts_out):
    owners,width,cap=rows.shape
    nf,events=field.shape
    a=jnp.concatenate([jnp.where(lax.broadcasted_iota(jnp.int32,(width,cap),1)<live[o],rows[o].astype(f32),0.0).astype(bf16) for o in range(owners)],axis=0)
    shift=cap.bit_length()-1
    column=lax.broadcasted_iota(jnp.int32,(cap,events),0)
    def one(f,carry):
        slot=field[pl.ds(f,1),:]
        low=lax.bitwise_and(slot,cap-1); high=lax.shift_right_logical(slot,shift)
        hot=jnp.where(column==low,1.0,0.0).astype(bf16)
        got=jnp.dot(a,hot,preferred_element_type=f32)
        acc=got[:width]
        for o in range(1,owners):
            acc=jnp.where(high==o,got[o*width:(o+1)*width],acc)
        joined[pl.ds(pl.multiple_of(f*width,width),width),:]=acc.astype(bf16)
        return carry
    lax.fori_loop(0,nf,one,0)
    G=8
    key_row=lax.broadcasted_iota(jnp.int32,(owners*G,PB),0)
    low_row=lax.broadcasted_iota(jnp.int32,(cap,PB),0)
    place=lax.broadcasted_iota(jnp.int32,(1,PB),1)
    def group(e0):
        first=starts[e0]; last=starts[e0+G]
        cuts=[starts[e0+k] for k in range(1,G)]
        def block(b,acc):
            slot=behave[b]
            p=place+b*PB
            ev=jnp.zeros((1,PB),jnp.int32)
            for c in cuts: ev=ev+jnp.where(p>=c,1,0)
            key=lax.shift_right_logical(slot,shift)*G+ev
            key=jnp.where(jnp.logical_and(p>=first,p<last),key,-1)
            left=jnp.where(key_row==key,1.0,0.0).astype(bf16)
            right=jnp.where(low_row==lax.bitwise_and(slot,cap-1),1.0,0.0).astype(bf16)
            return acc+lax.dot_general(left,right,NT,preferred_element_type=f32)
        return lax.fori_loop(lax.div(first,PB),lax.div(last-1,PB)+1,block,jnp.zeros((owners*G,cap),f32))
    def pair(g,carry):
        x=group(g*16); y=group(g*16+8)
        for o in range(owners):
            counts_out[o,pl.ds(pl.multiple_of(g*16,16),16),:]=jnp.concatenate([x[o*G:(o+1)*G],y[o*G:(o+1)*G]],axis=0).astype(bf16)
        return carry
    lax.fori_loop(0,events//16,pair,0)
    pooled=jnp.zeros((width,events),f32)
    for o in range(owners):
        pooled=pooled+lax.dot_general(a[o*width:(o+1)*width],counts_out[o],NT,preferred_element_type=f32)
    pooled_out[...]=pooled

def slots_forward(starts,rows,live,field_t,behave):
    owners,width,cap=rows.shape; nf,events=field_t.shape
    vm=pl.BlockSpec(memory_space=pltpu.VMEM); sm=pl.BlockSpec(memory_space=pltpu.SMEM)
    return pl.pallas_call(slots_kernel,in_specs=[sm,vm,sm,vm,vm],out_specs=[vm,vm,vm],
        out_shape=[jax.ShapeDtypeStruct((nf*width,events),bf16),jax.ShapeDtypeStruct((width,events),f32),jax.ShapeDtypeStruct((owners,events,cap),bf16)],
        compiler_params=pltpu.CompilerParams(vmem_limit_bytes=VM),name="slots_forward")(starts,rows,live,field_t,behave.reshape(-1,1,PB))

def slots_back_kernel(field,dj,counts,out,e):
    owners,width,cap=out.shape
    nf,events=field.shape
    shift=cap.bit_length()-1
    column=lax.broadcasted_iota(jnp.int32,(cap,events),0)
    zero=jnp.zeros((width,events),bf16)
    def one(f,carry):
        slot=field[pl.ds(f,1),:]
        low=lax.bitwise_and(slot,cap-1); high=jnp.broadcast_to(lax.shift_right_logical(slot,shift),(width,events))
        hot=jnp.where(column==low,1.0,0.0).astype(bf16)
        d=dj[pl.ds(pl.multiple_of(f*width,width),width),:].astype(f32)
        wide=jnp.concatenate([jnp.where(high==o,d,0.0).astype(bf16) for o in range(owners)],axis=0)
        e[...]+=lax.dot_general(wide,hot,NT,preferred_element_type=f32)
        return carry
    e[...]=jnp.zeros(e.shape,f32)
    lax.fori_loop(0,nf,one,0)
    pooled=dj[nf*width:(nf+1)*width,:].astype(bf16)
    for o in range(owners):
        out[o]=(e[o*width:(o+1)*width]+jnp.dot(pooled,counts[o],preferred_element_type=f32)).astype(bf16)

def slots_back(field_t,dj,counts):
    owners,events,cap=counts.shape; width=16
    vm=pl.BlockSpec(memory_space=pltpu.VMEM)
    return pl.pallas_call(slots_back_kernel,in_specs=[vm,vm,vm],out_specs=vm,
        out_shape=jax.ShapeDtypeStruct((owners,width,cap),bf16),scratch_shapes=[pltpu.VMEM((owners*width,cap),f32)],
        compiler_params=pltpu.CompilerParams(vmem_limit_bytes=VM),name="slots_back")(field_t,dj,counts)


def layer_norm(values, gain, shift):
    center = values - jnp.mean(values, axis=-1, keepdims=True)
    spread = jnp.mean(center * center, axis=-1, keepdims=True)
    return center * lax.rsqrt(spread + EPSILON) * gain + shift


def gelu_norm(pre, gain, shift):
    return layer_norm(jax.nn.gelu(pre), gain, shift)


def mixture(shared_logits, group_logits, outputs, onehot):
    shared_weights = jax.nn.softmax(shared_logits, axis=-1)
    shared_mix = jnp.sum(shared_weights.T[:, :, None] * outputs[:SHARED], axis=0)
    picked = jnp.sum(onehot[:, :, None] * group_logits, axis=1)
    group_weights = jax.nn.softmax(picked, axis=-1)
    domain_out = jnp.sum(onehot.T[:, :, None] * outputs[SHARED:], axis=0)
    return group_weights[:, 0:1] * shared_mix + group_weights[:, 1:2] * domain_out


def tower_head(pre_stack, tower_out, tower_out_bias, onehot):
    hidden = jax.nn.gelu(pre_stack)
    logits = jnp.sum(hidden * tower_out[:, None, :], axis=-1) + tower_out_bias[:, None]
    return jax.nn.sigmoid(jnp.sum(onehot.T * logits, axis=0))


def exact_dot(left, right):
    return jnp.dot(left, right, precision=lax.Precision.HIGHEST)


def local(
    table,
    dense,
    domains,
    lengths,
    requests,
    counts,
    field_slots,
    behave_slots,
    proj_w,
    proj_b,
    inter_gain,
    inter_bias,
    w_in,
    b_in,
    w_out,
    b_out,
    expert_gain,
    expert_bias,
    shared_gate,
    group_gate,
    tower_in,
    tower_in_bias,
    tower_out,
    tower_out_bias,
    pred_cotangent,
):
    f32 = jnp.float32
    bf16 = jnp.bfloat16
    n_wide = lax.axis_size("wide")
    n_narrow = lax.axis_size("narrow")
    devices = n_wide * n_narrow
    capacity = requests.shape[2]
    events = dense.shape[0]
    width = table.shape[1]
    asked = lax.all_to_all(requests, ("wide", "narrow"), split_axis=1, concat_axis=1, tiled=True)
    asked = asked.reshape(devices, capacity)
    found = table_gather(table.T, asked)
    rows = lax.all_to_all(found, ("wide", "narrow"), split_axis=0, concat_axis=0, tiled=True)
    sizes_seq = lengths.reshape(-1)
    starts = jnp.concatenate([jnp.zeros((1,), jnp.int32), jnp.cumsum(sizes_seq)])
    field_t = field_slots.T
    seq_len = sizes_seq.astype(f32)
    joined_t, pooled_sum, spread = slots_forward(starts, rows, counts.reshape(-1), field_t, behave_slots)
    field_width = field_t.shape[0] * width
    onehot = (domains[:, None] == jnp.arange(DOMAINS, dtype=jnp.int32)[None, :]).astype(f32)
    totals, squares, count = lax.psum(
        (exact_dot(onehot.T, dense), exact_dot(onehot.T, dense * dense), jnp.sum(onehot, axis=0)),
        ("wide", "narrow"),
    )
    count = count[:, None]
    mean = totals / count
    variance = squares / count - mean * mean
    inverse = lax.rsqrt(variance + EPSILON)
    event_inverse = exact_dot(onehot, inverse)
    centered = (dense - exact_dot(onehot, mean)) * event_inverse
    centered_low = centered.astype(bf16)
    pooled_t = (pooled_sum / seq_len[None, :]).astype(bf16)
    joined = jnp.concatenate([joined_t, pooled_t, centered_low.T], axis=0).T
    pre_proj = jnp.dot(joined, proj_w, preferred_element_type=f32) + proj_b
    state = gelu_norm(pre_proj, inter_gain, inter_bias)
    state_low = state.astype(bf16)
    kept = []
    outputs = []
    for expert in range(w_in.shape[0]):
        pre_in = jnp.dot(state_low, w_in[expert], preferred_element_type=f32) + b_in[expert]
        active = jax.nn.gelu(pre_in).astype(bf16)
        pre_out = jnp.dot(active, w_out[expert], preferred_element_type=f32) + b_out[expert]
        outputs.append(layer_norm(pre_out, expert_gain[expert], expert_bias[expert]))
        kept.append((pre_in, active, pre_out))
    outputs = jnp.stack(outputs)
    shared_logits = jnp.dot(state_low, shared_gate, preferred_element_type=f32)
    group_logits = jnp.einsum("ek,dkg->edg", state_low, group_gate, preferred_element_type=f32)

    def mixing(shared_part, group_part, expert_part):
        return mixture(shared_part, group_part, expert_part, onehot)

    mixed, mixing_back = jax.vjp(mixing, shared_logits, group_logits, outputs)
    after = state + mixed
    after_low = after.astype(bf16)
    tower_pre = (
        jnp.einsum("ek,dkj->dej", after_low, tower_in, preferred_element_type=f32)
        + tower_in_bias[:, None, :]
    )

    def heading(pre_part, out_part, bias_part):
        return tower_head(pre_part, out_part, bias_part, onehot)

    pred, heading_back = jax.vjp(heading, tower_pre, tower_out, tower_out_bias)
    d_tower_pre, d_tower_out, d_tower_out_bias = heading_back(pred_cotangent)
    d_tower_low = d_tower_pre.astype(bf16)
    d_tower_in = jnp.einsum("ek,dej->dkj", after_low, d_tower_low, preferred_element_type=f32)
    d_tower_in_bias = jnp.sum(d_tower_low.astype(f32), axis=1)
    d_after = jnp.einsum("dej,dkj->ek", d_tower_low, tower_in, preferred_element_type=f32)
    d_shared_logits, d_group_logits, d_outputs = mixing_back(d_after)
    state_wide = state_low.astype(f32)
    d_shared_gate = jnp.einsum(
        "ek,es->ks", state_wide, d_shared_logits, precision=lax.Precision.HIGHEST
    )
    d_group_gate = jnp.einsum(
        "ek,edg->dkg", state_wide, d_group_logits, precision=lax.Precision.HIGHEST
    )
    d_low = jnp.einsum(
        "es,ks->ek", d_shared_logits, shared_gate.astype(f32), precision=lax.Precision.HIGHEST
    )
    d_low = d_low + jnp.einsum(
        "edg,dkg->ek", d_group_logits, group_gate.astype(f32), precision=lax.Precision.HIGHEST
    )
    grads_w_in, grads_b_in, grads_w_out, grads_b_out, grads_gain, grads_bias = (
        [],
        [],
        [],
        [],
        [],
        [],
    )
    for expert in range(w_in.shape[0]):
        pre_in, active, pre_out = kept[expert]
        norm_back = jax.vjp(layer_norm, pre_out, expert_gain[expert], expert_bias[expert])[1]
        d_pre_out, d_gain_one, d_bias_one = norm_back(d_outputs[expert])
        d_out_low = d_pre_out.astype(bf16)
        grads_b_out.append(jnp.sum(d_out_low.astype(f32), axis=0))
        grads_w_out.append(jnp.einsum("ej,ek->jk", active, d_out_low, preferred_element_type=f32))
        d_active = jnp.einsum("ek,jk->ej", d_out_low, w_out[expert], preferred_element_type=f32)
        d_pre_in = jax.vjp(jax.nn.gelu, pre_in)[1](d_active)[0]
        d_in_low = d_pre_in.astype(bf16)
        grads_b_in.append(jnp.sum(d_in_low.astype(f32), axis=0))
        grads_w_in.append(jnp.einsum("ek,ej->kj", state_low, d_in_low, preferred_element_type=f32))
        d_low = d_low + jnp.einsum("ej,kj->ek", d_in_low, w_in[expert], preferred_element_type=f32)
        grads_gain.append(d_gain_one)
        grads_bias.append(d_bias_one)
    mixture_terms = (
        jnp.stack(grads_w_in),
        jnp.stack(grads_b_in),
        jnp.stack(grads_w_out),
        jnp.stack(grads_b_out),
        jnp.stack(grads_gain),
        jnp.stack(grads_bias),
        d_shared_gate,
        d_group_gate,
        d_tower_in,
        d_tower_in_bias,
        d_tower_out,
        d_tower_out_bias,
    )
    d_state = d_after + d_low
    d_pre_proj, d_inter_gain, d_inter_bias = jax.vjp(gelu_norm, pre_proj, inter_gain, inter_bias)[
        1
    ](d_state)
    d_proj_low = d_pre_proj.astype(bf16)
    d_proj_b = jnp.sum(d_proj_low.astype(f32), axis=0)
    d_proj_w = jnp.einsum("ef,ek->fk", joined, d_proj_low, preferred_element_type=f32)
    interaction_terms = (d_proj_w, d_proj_b, d_inter_gain, d_inter_bias)
    terms = mixture_terms + interaction_terms
    large = [i for i, term in enumerate(terms) if term.size > 100000]
    small = [i for i in range(len(terms)) if i not in large]
    large_sums = lax.psum(tuple(terms[i].astype(bf16) for i in large), ("wide", "narrow"))
    small_sums = lax.psum(tuple(terms[i] for i in small), ("wide", "narrow"))
    summed = [None] * len(terms)
    for i, value in zip(large, large_sums):
        summed[i] = value.astype(f32)
    for i, value in zip(small, small_sums):
        summed[i] = value
    mixture_terms = summed[:12]
    interaction_terms = summed[12:]
    d_joined = jnp.einsum("ek,fk->ef", d_proj_low, proj_w, preferred_element_type=f32)
    d_fields = d_joined[:, :field_width]
    d_pooled = d_joined[:, field_width : field_width + width]
    d_centered = d_joined[:, field_width + width :]
    sum_grad, sum_cross = lax.psum(
        (exact_dot(onehot.T, d_centered), exact_dot(onehot.T, d_centered * centered)),
        ("wide", "narrow"),
    )
    d_dense = event_inverse * (
        d_centered
        - exact_dot(onehot, sum_grad / count)
        - centered * exact_dot(onehot, sum_cross / count)
    )
    d_joined_t = d_joined.T
    scaled_t = d_joined_t[field_width : field_width + width] / seq_len[None, :]
    slot_grad = slots_back(
        field_t, jnp.concatenate([d_joined_t[:field_width], scaled_t], axis=0), spread
    )
    returned = lax.all_to_all(slot_grad, ("wide", "narrow"), split_axis=0, concat_axis=0, tiled=True)
    d_table = table_scatter(asked, returned, table.shape[0]).T
    return (
        pred,
        d_dense,
        d_table,
        interaction_terms[0],
        interaction_terms[1],
        interaction_terms[2],
        interaction_terms[3],
        mixture_terms[0],
        mixture_terms[1],
        mixture_terms[2],
        mixture_terms[3],
        mixture_terms[4],
        mixture_terms[5],
        mixture_terms[6],
        mixture_terms[7],
        mixture_terms[8],
        mixture_terms[9],
        mixture_terms[10],
        mixture_terms[11],
    )


def solution(mesh):
    placed = (
        P(("wide", "narrow"), None),
        P(("wide", "narrow"), None),
        P(("wide", "narrow")),
        P(("wide", "narrow"), None),
        P(("wide", "narrow"), None, None),
        P(("wide", "narrow"), None),
        P(("wide", "narrow"), None),
        P(("wide", "narrow"), None),
        P(),
        P(),
        P(),
        P(),
        P(),
        P(),
        P(),
        P(),
        P(),
        P(),
        P(),
        P(),
        P(),
        P(),
        P(),
        P(),
        P(("wide", "narrow")),
    )
    return jax.shard_map(
        local,
        mesh=mesh,
        in_specs=placed,
        out_specs=(
            P(("wide", "narrow")),
            P(("wide", "narrow"), None),
            P(("wide", "narrow"), None),
            P(),
            P(),
            P(),
            P(),
            P(),
            P(),
            P(),
            P(),
            P(),
            P(),
            P(),
            P(),
            P(),
            P(),
            P(),
            P(),
        ),
        check_vma=False,
    )
```

```python
import functools
import math

import jax
import jax.numpy as jnp
from jax import lax
from jax.experimental import pallas as pl
from jax.experimental.pallas import tpu as pltpu
from jax.sharding import PartitionSpec as P

SHARED = 2
DOMAINS = 2

EPSILON = 1e-05

f32 = jnp.float32
bf16 = jnp.bfloat16
i32 = jnp.int32
MESH = pl.DeviceIdType.MESH
AXES = ("wide", "narrow")
NT = (((1,), (1,)), ((), ()))
TN = (((0,), (0,)), ((), ()))
VMEM_LIMIT = 60 * 1024 * 1024
ROW_CHUNK = 1024
GROUP = 8
SPAN = 6


def vmem():
    return pl.BlockSpec(memory_space=pltpu.VMEM)


def smem():
    return pl.BlockSpec(memory_space=pltpu.SMEM)


def hbm():
    return pl.BlockSpec(memory_space=pl.ANY)


def params(**more):
    return pltpu.CompilerParams(vmem_limit_bytes=VMEM_LIMIT, **more)


def line_of(rows):
    return jnp.left_shift(jnp.right_shift(rows, 10), 7) + jnp.bitwise_and(rows, 127)


def lane_group_of(rows):
    return jnp.bitwise_and(jnp.right_shift(rows, 7), 7)


def identity(n):
    return (lax.broadcasted_iota(i32, (n, n), 0) == lax.broadcasted_iota(i32, (n, n), 1)).astype(bf16)


def gather_kernel(line, group, tab, out, lines, got):
    step = pl.program_id(0)
    width = tab.shape[0]
    per = tab.shape[1] // ROW_CHUNK
    eye = identity(128)

    def turn(c, carry):
        base = pl.multiple_of(c * ROW_CHUNK, ROW_CHUNK)
        stack = jnp.concatenate([tab[:, pl.ds(base + g * 128, 128)] for g in range(8)], axis=0)
        at = pl.multiple_of((step * per + c) * 128, 128)
        lines[pl.ds(at, 128), :] = lax.dot_general(eye, stack, NT, preferred_element_type=f32)
        return carry

    lax.fori_loop(0, per, turn, 0, unroll=8)

    @pl.when(step == pl.num_programs(0) - 1)
    def _():
        blocks, _, cap = group.shape
        batch = 4

        def serve(s, carry):
            def fetch(u, carry):
                for k in range(64):
                    j = u * 64 + k
                    got[pl.ds(j, 1), :] = lines[pl.ds(line[s * (batch * cap) + j], 1), :]
                return carry

            lax.fori_loop(0, batch * cap // 64, fetch, 0)
            turned = lax.dot_general(eye, got[...].astype(bf16), NT, preferred_element_type=f32)
            for b in range(batch):
                which = group[s * batch + b]
                rows = turned[:width, b * cap : (b + 1) * cap]
                for g in range(1, 8):
                    rows = jnp.where(which == g, turned[g * width : (g + 1) * width, b * cap : (b + 1) * cap], rows)
                out[s * batch + b] = rows.astype(bf16)
            return carry

        lax.fori_loop(0, blocks // batch, serve, 0)


def table_gather(tab_t, line, group):
    width, rows = tab_t.shape
    blocks, _, cap = group.shape
    columns = rows // 3
    return pl.pallas_call(
        gather_kernel,
        grid=(3,),
        in_specs=[smem(), vmem(), pl.BlockSpec((width, columns), lambda i: (0, i))],
        out_specs=vmem(),
        out_shape=jax.ShapeDtypeStruct((blocks, width, cap), bf16),
        scratch_shapes=[pltpu.VMEM((rows // 8, 128), f32), pltpu.VMEM((4 * cap, 128), f32)],
        compiler_params=params(),
        name="table_gather",
    )(line, group, tab_t)


def finish_kernel(n_more, line, line_v, group, returned, *refs):
    more, out, more_out = refs[:n_more], refs[n_more], refs[n_more + 1 : 2 * n_more + 1]
    lines, vals = refs[2 * n_more + 1 :]
    step = pl.program_id(0)
    per = out.shape[1] // ROW_CHUNK

    @pl.when(step == 0)
    def _():
        blocks, _, cap = group.shape

        def clear(i, carry):
            lines[pl.ds(pl.multiple_of(i * 1024, 1024), 1024), :] = jnp.zeros((1024, 128), f32)
            return carry

        lax.fori_loop(0, lines.shape[0] // 1024, clear, 0)
        batch = 32
        a = lax.div(lax.broadcasted_iota(i32, (cap, cap), 0), batch)
        near = a == lax.div(lax.broadcasted_iota(i32, (cap, cap), 1), batch)

        def serve(s, carry):
            which, own = group[s], returned[s].astype(f32)
            wide = jnp.concatenate([jnp.where(which == g, own, 0.0) for g in range(8)], axis=0)
            along = jnp.broadcast_to(line_v[s].astype(f32), (cap, cap))
            same = jnp.where(jnp.logical_and(along == along.T, near), 1.0, 0.0).astype(bf16)
            vals[...] = lax.dot_general(same, wide.astype(bf16), NT, preferred_element_type=f32)

            def add(u, carry):
                places, sums = [], []
                for k in range(batch):
                    j = u * batch + k
                    places.append(line[s * cap + j])
                    sums.append(lines[pl.ds(places[-1], 1), :] + vals[pl.ds(j, 1), :])
                for place, total in zip(places, sums):
                    lines[pl.ds(place, 1), :] = total
                return carry

            lax.fori_loop(0, cap // batch, add, 0)
            return carry

        lax.fori_loop(0, blocks, serve, 0)

    def turn(c, carry):
        width = out.shape[0]
        turned = lines[pl.ds(pl.multiple_of((step * per + c) * 128, 128), 128), :].T
        for g in range(8):
            at = pl.multiple_of(c * ROW_CHUNK + g * 128, 128)
            out[:, pl.ds(at, 128)] = turned[g * width : (g + 1) * width]
        return carry

    lax.fori_loop(0, per, turn, 0, unroll=4)
    for source, target in zip(more, more_out):
        tall, blocks, rows, lanes = source.shape
        for s in range(tall):
            for c in range(blocks):
                target[s * rows : (s + 1) * rows, c * lanes : (c + 1) * lanes] = source[s, c].astype(f32)


def finish(line, group, returned, rows, more):
    blocks, width, cap = returned.shape
    steps = 4
    in_more, out_more, shapes = [], [], []
    for x in more:
        tall, parts, r, lanes = x.shape
        if tall > 1:
            in_more.append(pl.BlockSpec((tall // steps, parts, r, lanes), lambda i: (i, 0, 0, 0)))
        else:
            in_more.append(pl.BlockSpec((1, parts, r // steps, lanes), lambda i: (0, 0, i, 0)))
        out_more.append(pl.BlockSpec((tall * r // steps, parts * lanes), lambda i: (i, 0)))
        shapes.append(jax.ShapeDtypeStruct((tall * r, parts * lanes), f32))
    return pl.pallas_call(
        functools.partial(finish_kernel, len(more)),
        grid=(steps,),
        in_specs=[smem(), vmem(), vmem(), vmem()] + in_more,
        out_specs=[pl.BlockSpec((width, rows // steps), lambda i: (0, i))] + out_more,
        out_shape=[jax.ShapeDtypeStruct((width, rows), f32)] + shapes,
        scratch_shapes=[pltpu.VMEM((rows // 8, 128), f32), pltpu.VMEM((cap, 128), f32)],
        compiler_params=params(),
        name="finish",
    )(line, line.reshape(blocks, 1, cap), group, returned, *more)


def hot(rows, index):
    column = lax.broadcasted_iota(i32, (rows, index.shape[1]), 0)
    return jnp.where(column == index, 1.0, 0.0).astype(bf16)


def count_kernel(starts, behave, counts, sums):
    owners, events, cap = counts.shape
    shift = cap.bit_length() - 1
    place = lax.broadcasted_iota(i32, (SPAN, 128), 0) * 128 + lax.broadcasted_iota(i32, (SPAN, 128), 1)
    last_block = behave.shape[0] - SPAN

    def group(e0, k):
        first, last = starts[e0], starts[e0 + GROUP]
        cuts = [starts[e0 + i] for i in range(1, GROUP)]
        b0 = lax.div(first, 128)

        def part(m):
            begin = b0 + m * SPAN
            b = jnp.minimum(begin, last_block)
            slot = behave[pl.ds(b, SPAN), :]
            p = place + b * 128
            event = jnp.zeros_like(p)
            for cut in cuts:
                event = event + jnp.where(p >= cut, 1, 0)
            key = jnp.right_shift(slot, shift) * GROUP + event
            mine = jnp.logical_and(jnp.logical_and(p >= first, p < last), p >= begin * 128)
            key = jnp.where(mine, key, -1)
            low = jnp.bitwise_and(slot, cap - 1)
            left = jnp.concatenate([hot(owners * GROUP, key[q : q + 1]) for q in range(SPAN)], axis=1)
            right = jnp.concatenate([hot(cap, low[q : q + 1]) for q in range(SPAN)], axis=1)
            return lax.dot_general(left, right, NT, preferred_element_type=f32)

        sums[k] = part(0)

        def more(m, carry):
            sums[k] += part(m)
            return carry

        lax.fori_loop(1, lax.div(last - b0 * 128 + (SPAN * 128 - 1), SPAN * 128), more, 0)

    def pair(g, carry):
        e0 = g * (2 * GROUP)
        group(e0, 0)
        group(e0 + GROUP, 1)
        for o in range(owners):
            both = [sums[k, o * GROUP : (o + 1) * GROUP, :] for k in range(2)]
            at = pl.ds(pl.multiple_of(e0, 2 * GROUP), 2 * GROUP)
            counts[o, at, :] = jnp.concatenate(both, axis=0).astype(bf16)
        return carry

    lax.fori_loop(0, events // (2 * GROUP), pair, 0)


def slot_counts(starts, behave, owners, cap):
    events = starts.shape[0] - 1
    return pl.pallas_call(
        count_kernel,
        in_specs=[smem(), vmem()],
        out_specs=vmem(),
        out_shape=jax.ShapeDtypeStruct((owners, events, cap), bf16),
        scratch_shapes=[pltpu.VMEM((2, owners * GROUP, cap), f32)],
        compiler_params=params(),
        name="slot_counts",
    )(starts, behave)


def pick_kernel(rows, live, field, counts, fields, pooled, table):
    owners, width, cap = rows.shape
    n_field, events = field.shape
    shift = cap.bit_length() - 1
    column = lax.broadcasted_iota(i32, (width, cap), 1)
    for o in range(owners):
        table[o * width : (o + 1) * width, :] = jnp.where(column < live[o], rows[o].astype(f32), 0.0).astype(bf16)

    def one(f, carry):
        slot = field[pl.ds(f, 1), :]
        owner = jnp.right_shift(slot, shift)
        got = jnp.dot(table[...], hot(cap, jnp.bitwise_and(slot, cap - 1)), preferred_element_type=f32)
        picked = got[:width]
        for o in range(1, owners):
            picked = jnp.where(owner == o, got[o * width : (o + 1) * width], picked)
        fields[pl.ds(pl.multiple_of(f * width, width), width), :] = picked.astype(bf16)
        return carry

    lax.fori_loop(0, n_field, one, 0, unroll=4)
    total = jnp.zeros((events, width), f32)
    for o in range(owners):
        total = total + lax.dot_general(counts[o], table[o * width : (o + 1) * width, :], NT, preferred_element_type=f32)
    pooled[...] = total.T


def pick_slots(rows, live, field_t, counts):
    owners, width, cap = rows.shape
    n_field, events = field_t.shape
    return pl.pallas_call(
        pick_kernel,
        in_specs=[vmem(), smem(), vmem(), vmem()],
        out_specs=[vmem(), vmem()],
        out_shape=[
            jax.ShapeDtypeStruct((n_field * width, events), bf16),
            jax.ShapeDtypeStruct((width, events), f32),
        ],
        scratch_shapes=[pltpu.VMEM((owners * width, cap), bf16)],
        compiler_params=params(),
        name="pick_slots",
    )(rows, live, field_t, counts)


def slots_back_kernel(field, d_fields, d_pooled, counts, out, total):
    owners, width, cap = out.shape
    n_field, events = field.shape
    shift = cap.bit_length() - 1
    total[...] = jnp.zeros(total.shape, f32)

    def one(f, carry):
        slot = field[pl.ds(f, 1), :]
        owner = jnp.right_shift(slot, shift)
        d = d_fields[pl.ds(pl.multiple_of(f * width, width), width), :].astype(f32)
        wide = jnp.concatenate([jnp.where(owner == o, d, 0.0).astype(bf16) for o in range(owners)], axis=0)
        total[...] += lax.dot_general(
            wide, hot(cap, jnp.bitwise_and(slot, cap - 1)), NT, preferred_element_type=f32
        )
        return carry

    lax.fori_loop(0, n_field, one, 0, unroll=2)
    for o in range(owners):
        behave = jnp.dot(d_pooled[...], counts[o], preferred_element_type=f32)
        out[o] = (total[o * width : (o + 1) * width] + behave).astype(bf16)


def slots_back(field_t, d_fields, d_pooled, counts):
    owners, _, cap = counts.shape
    width = d_pooled.shape[0]
    return pl.pallas_call(
        slots_back_kernel,
        in_specs=[vmem()] * 4,
        out_specs=vmem(),
        out_shape=jax.ShapeDtypeStruct((owners, width, cap), bf16),
        scratch_shapes=[pltpu.VMEM((owners * width, cap), f32)],
        compiler_params=params(),
        name="slots_back",
    )(field_t, d_fields, d_pooled, counts)


def place_bits():
    return [(axis, b) for axis in AXES for b in range(lax.axis_size(axis).bit_length() - 1)]


def bit_value(bit):
    return lax.rem(lax.div(lax.axis_index(bit[0]), 1 << bit[1]), 2)


def across(bit):
    axis, b = bit
    place = {a: lax.axis_index(a) for a in AXES}
    place[axis] = place[axis] + (1 - 2 * bit_value(bit)) * (1 << b)
    return tuple(place[a] for a in AXES)


class Piece:
    def __init__(self, part, inbox, total, order, sends, recvs):
        self.part, self.inbox, self.total = part, inbox, total
        self.order, self.sends, self.recvs = order, sends, recvs
        self.rows = part.shape[0]
        self.grain = self.rows >> len(order)
        self.offsets, self.copies = [0], []

    def at(self, ref, offset, n):
        return ref.at[pl.ds(pl.multiple_of(offset, self.grain), n)]

    def send(self):
        k, depth = len(self.copies), len(self.order)
        if k < depth:
            bit, half = self.order[k], self.rows >> (k + 1)
            value, offset = bit_value(bit), self.offsets[k]
            self.offsets.append(offset + value * half)
            source = self.at(self.part, offset + (1 - value) * half, half)
            target = self.inbox.at[pl.ds(self.rows - (self.rows >> k), half)]
        else:
            s = 2 * depth - 1 - k
            bit = self.order[s]
            source = target = self.at(self.total, self.offsets[s + 1], self.rows >> (s + 1))
        copy = pltpu.make_async_remote_copy(
            src_ref=source,
            dst_ref=target,
            send_sem=self.sends.at[k],
            recv_sem=self.recvs.at[k],
            device_id=across(bit),
            device_id_type=MESH,
        )
        copy.start()
        self.copies.append(copy)

    def take(self):
        k, depth = len(self.copies) - 1, len(self.order)
        self.copies[k].wait_recv()
        if k < depth:
            n, base, offset = self.rows >> (k + 1), self.rows - (self.rows >> k), self.offsets[k + 1]
            target = self.total if k == depth - 1 else self.part
            chunk = math.gcd(n, 64)

            def add(i, carry):
                at = pl.ds(pl.multiple_of(offset + i * chunk, math.gcd(self.grain, chunk)), chunk)
                came = self.inbox[pl.ds(pl.multiple_of(base + i * chunk, chunk), chunk), :]
                target[at, :] = (self.part[at, :].astype(f32) + came.astype(f32)).astype(target.dtype)
                return carry

            lax.fori_loop(0, n // chunk, add, 0)
        if k + 1 < 2 * depth:
            self.send()

    def drain(self):
        for copy in self.copies:
            copy.wait_send()


def everyone_else():
    n_wide, n_narrow = (lax.axis_size(a) for a in AXES)
    w, n = (lax.axis_index(a) for a in AXES)
    me = w * n_narrow + n
    total = n_wide * n_narrow
    for d in range(1, total):
        other = lax.rem(me + d, total)
        yield d, other, (lax.div(other, n_narrow), lax.rem(other, n_narrow))


def meet_all():
    barrier = pltpu.get_barrier_semaphore()
    for _, _, place in everyone_else():
        pl.semaphore_signal(barrier, inc=1, device_id=place, device_id_type=MESH)
    pl.semaphore_wait(barrier, lax.axis_size("wide") * lax.axis_size("narrow") - 1)


def lanes_of(rows, columns, devices):
    lanes = columns
    while lanes > 128 and (rows * (columns // lanes)) % (16 * devices):
        lanes //= 2
    return lanes


ORDERS = "BDADABGGBBBABGBAAA"


class Block:
    def __init__(self, rows, columns, devices):
        self.rows, self.columns = rows, columns
        self.lanes = lanes_of(rows, columns, devices)
        self.blocks = columns // self.lanes
        self.padded = -(-rows * self.blocks // (16 * devices)) * 16 * devices

    def put(self, piece, value):
        for c in range(self.blocks):
            piece[c * self.rows : (c + 1) * self.rows, :] = value[:, c * self.lanes : (c + 1) * self.lanes]
        extra = self.padded - self.rows * self.blocks
        if extra:
            piece[self.rows * self.blocks :, :] = jnp.zeros((extra, self.lanes), piece.dtype)

    def whole(self, total, n):
        return total[:, : self.rows * self.blocks].reshape(n, self.blocks, self.rows, self.lanes)


def orders():
    if tuple(lax.axis_size(a) for a in AXES) != (8, 4):
        return [place_bits()] * len(ORDERS)
    core, y, x, z0, z1 = ("narrow", 0), ("narrow", 1), ("wide", 0), ("wide", 1), ("wide", 2)
    ways = {
        "A": [core, x, y, z0, z1],
        "B": [core, y, x, z0, z1],
        "D": [core, z0, z1, y, x],
        "G": [core, z0, z1, x, y],
    }
    return [ways[way] for way in ORDERS]


def reduce_kernel(blocks, n_big, slot_grad, small, *refs):
    big = refs[:n_big]
    returned, small_total = refs[n_big : n_big + 2]
    totals = refs[n_big + 2 : 2 * n_big + 2]
    small_part, small_inbox = refs[2 * n_big + 2 : 2 * n_big + 4]
    parts = refs[2 * n_big + 4 : 3 * n_big + 4]
    inboxes = refs[3 * n_big + 4 : 4 * n_big + 4]
    sends, recvs, slot_sends, slot_recvs = refs[4 * n_big + 4 :]
    meet_all()
    me = lax.axis_index("wide") * lax.axis_size("narrow") + lax.axis_index("narrow")
    slot_copies = []
    for d, other, place in everyone_else():
        copy = pltpu.make_async_remote_copy(
            src_ref=slot_grad.at[other],
            dst_ref=returned.at[me],
            send_sem=slot_sends.at[d],
            recv_sem=slot_recvs.at[d],
            device_id=place,
            device_id_type=MESH,
        )
        copy.start()
        slot_copies.append(copy)
    returned[me] = slot_grad[me]
    pieces = [Piece(small_part, small_inbox, small_total, orders()[0], sends.at[0], recvs.at[0])]
    small_part[...] = small[...]
    pieces[0].send()
    for a in range(n_big):
        for i in range(parts[a].shape[0]):
            k = len(pieces)
            piece = Piece(parts[a].at[i], inboxes[a].at[i], totals[a].at[i], orders()[k - 1], sends.at[k], recvs.at[k])
            blocks[a].put(parts[a].at[i], big[a][i])
            piece.send()
            pieces.append(piece)
    for _ in range(2 * len(place_bits())):
        for piece in pieces:
            piece.take()
    for copy in slot_copies:
        copy.wait_recv()
    for copy in slot_copies:
        copy.wait_send()
    for piece in pieces:
        piece.drain()


def reduce_all(slot_grad, small, big, devices):
    blocks = [Block(x.shape[1], x.shape[2], devices) for x in big]
    shapes = [(x.shape[0], b.padded, b.lanes) for x, b in zip(big, blocks)]
    n_pieces = 1 + sum(x.shape[0] for x in big)
    steps = 2 * (devices.bit_length() - 1)
    out = pl.pallas_call(
        functools.partial(reduce_kernel, blocks, len(big)),
        in_specs=[vmem()] * (2 + len(big)),
        out_specs=[vmem()] * (2 + len(big)),
        out_shape=[jax.ShapeDtypeStruct(slot_grad.shape, bf16), jax.ShapeDtypeStruct(small.shape, f32)]
        + [jax.ShapeDtypeStruct(s, bf16) for s in shapes],
        scratch_shapes=[pltpu.VMEM(small.shape, f32)] * 2
        + [pltpu.VMEM(s, bf16) for s in shapes] * 2
        + [pltpu.SemaphoreType.DMA((n_pieces, steps))] * 2
        + [pltpu.SemaphoreType.DMA((devices,))] * 2,
        compiler_params=params(collective_id=0, has_side_effects=True),
        name="reduce_all",
    )(slot_grad, small, *big)
    return out[0], out[1], [b.whole(t, x.shape[0]) for b, t, x in zip(blocks, out[2:], big)]


def layer_norm(values, gain, shift):
    center = values - jnp.mean(values, axis=-1, keepdims=True)
    spread = jnp.mean(center * center, axis=-1, keepdims=True)
    return center * lax.rsqrt(spread + EPSILON) * gain + shift


def gelu_norm(pre, gain, shift):
    return layer_norm(jax.nn.gelu(pre), gain, shift)


def mixture(shared_logits, group_logits, outputs, onehot):
    shared_weights = jax.nn.softmax(shared_logits, axis=-1)
    shared_mix = jnp.sum(shared_weights.T[:, :, None] * outputs[:SHARED], axis=0)
    picked = jnp.sum(onehot[:, :, None] * group_logits, axis=1)
    group_weights = jax.nn.softmax(picked, axis=-1)
    domain_out = jnp.sum(onehot.T[:, :, None] * outputs[SHARED:], axis=0)
    return group_weights[:, 0:1] * shared_mix + group_weights[:, 1:2] * domain_out


def tower_head(pre_stack, tower_out, tower_out_bias, onehot):
    hidden = jax.nn.gelu(pre_stack)
    logits = jnp.sum(hidden * tower_out[:, None, :], axis=-1) + tower_out_bias[:, None]
    return jax.nn.sigmoid(jnp.sum(onehot.T * logits, axis=0))


def exact_dot(left, right):
    return jnp.dot(left, right, precision=lax.Precision.HIGHEST)


def local(
    table,
    dense,
    domains,
    lengths,
    requests,
    counts,
    field_slots,
    behave_slots,
    proj_w,
    proj_b,
    inter_gain,
    inter_bias,
    w_in,
    b_in,
    w_out,
    b_out,
    expert_gain,
    expert_bias,
    shared_gate,
    group_gate,
    tower_in,
    tower_in_bias,
    tower_out,
    tower_out_bias,
    pred_cotangent,
):
    n_wide = lax.axis_size("wide")
    n_narrow = lax.axis_size("narrow")
    devices = n_wide * n_narrow
    capacity = requests.shape[2]
    events = dense.shape[0]
    width = table.shape[1]
    sizes_seq = lengths.reshape(-1)
    starts = jnp.concatenate([jnp.zeros((1,), i32), jnp.cumsum(sizes_seq)])
    spread = slot_counts(starts, behave_slots.reshape(-1, 128), devices, capacity)
    asked = lax.all_to_all(requests, AXES, split_axis=1, concat_axis=1, tiled=True)
    asked = asked.reshape(devices, 1, capacity)
    line, group = line_of(asked), lane_group_of(asked)
    found = table_gather(table.T, line.reshape(-1), group)
    rows = lax.all_to_all(found, AXES, split_axis=0, concat_axis=0, tiled=True)
    field_t = field_slots.T
    field_width = field_t.shape[0] * width
    seq_len = sizes_seq.astype(f32)
    fields_t, pooled_sum = pick_slots(rows, counts.reshape(-1), field_t, spread)
    onehot = (domains[:, None] == jnp.arange(DOMAINS, dtype=jnp.int32)[None, :]).astype(f32)
    totals, squares, count = lax.psum(
        (exact_dot(onehot.T, dense), exact_dot(onehot.T, dense * dense), jnp.sum(onehot, axis=0)),
        ("wide", "narrow"),
    )
    count = count[:, None]
    mean = totals / count
    variance = squares / count - mean * mean
    inverse = lax.rsqrt(variance + EPSILON)
    event_inverse = exact_dot(onehot, inverse)
    centered = (dense - exact_dot(onehot, mean)) * event_inverse
    centered_low = centered.astype(bf16)
    pooled_t = (pooled_sum / seq_len[None, :]).astype(bf16)
    joined = jnp.concatenate([fields_t, pooled_t, centered_low.T], axis=0).T
    pre_proj = jnp.dot(joined, proj_w, preferred_element_type=f32) + proj_b
    state = gelu_norm(pre_proj, inter_gain, inter_bias)
    state_low = state.astype(bf16)
    kept = []
    outputs = []
    for expert in range(w_in.shape[0]):
        pre_in = jnp.dot(state_low, w_in[expert], preferred_element_type=f32) + b_in[expert]
        active = jax.nn.gelu(pre_in).astype(bf16)
        pre_out = jnp.dot(active, w_out[expert], preferred_element_type=f32) + b_out[expert]
        outputs.append(layer_norm(pre_out, expert_gain[expert], expert_bias[expert]))
        kept.append((pre_in, active, pre_out))
    outputs = jnp.stack(outputs)
    shared_logits = jnp.dot(state_low, shared_gate, preferred_element_type=f32)
    group_logits = jnp.einsum("ek,dkg->edg", state_low, group_gate, preferred_element_type=f32)

    def mixing(shared_part, group_part, expert_part):
        return mixture(shared_part, group_part, expert_part, onehot)

    mixed, mixing_back = jax.vjp(mixing, shared_logits, group_logits, outputs)
    after = state + mixed
    after_low = after.astype(bf16)
    tower_pre = (
        jnp.einsum("ek,dkj->dej", after_low, tower_in, preferred_element_type=f32)
        + tower_in_bias[:, None, :]
    )

    def heading(pre_part, out_part, bias_part):
        return tower_head(pre_part, out_part, bias_part, onehot)

    pred, heading_back = jax.vjp(heading, tower_pre, tower_out, tower_out_bias)
    d_tower_pre, d_tower_out, d_tower_out_bias = heading_back(pred_cotangent)
    d_tower_low = d_tower_pre.astype(bf16)
    d_tower_in = jnp.einsum("ek,dej->dkj", after_low, d_tower_low, preferred_element_type=f32)
    d_tower_in_bias = jnp.sum(d_tower_low.astype(f32), axis=1)
    d_after = jnp.einsum("dej,dkj->ek", d_tower_low, tower_in, preferred_element_type=f32)
    d_shared_logits, d_group_logits, d_outputs = mixing_back(d_after)
    state_wide = state_low.astype(f32)
    d_shared_gate = jnp.einsum(
        "ek,es->ks", state_wide, d_shared_logits, precision=lax.Precision.HIGHEST
    )
    d_group_gate = jnp.einsum(
        "ek,edg->dkg", state_wide, d_group_logits, precision=lax.Precision.HIGHEST
    )
    d_low = jnp.einsum(
        "es,ks->ek", d_shared_logits, shared_gate.astype(f32), precision=lax.Precision.HIGHEST
    )
    d_low = d_low + jnp.einsum(
        "edg,dkg->ek", d_group_logits, group_gate.astype(f32), precision=lax.Precision.HIGHEST
    )
    grads_w_in, grads_b_in, grads_w_out, grads_b_out, grads_gain, grads_bias = (
        [],
        [],
        [],
        [],
        [],
        [],
    )
    for expert in range(w_in.shape[0]):
        pre_in, active, pre_out = kept[expert]
        norm_back = jax.vjp(layer_norm, pre_out, expert_gain[expert], expert_bias[expert])[1]
        d_pre_out, d_gain_one, d_bias_one = norm_back(d_outputs[expert])
        d_out_low = d_pre_out.astype(bf16)
        grads_b_out.append(jnp.sum(d_out_low.astype(f32), axis=0))
        grads_w_out.append(jnp.einsum("ej,ek->jk", active, d_out_low, preferred_element_type=f32))
        d_active = jnp.einsum("ek,jk->ej", d_out_low, w_out[expert], preferred_element_type=f32)
        d_pre_in = jax.vjp(jax.nn.gelu, pre_in)[1](d_active)[0]
        d_in_low = d_pre_in.astype(bf16)
        grads_b_in.append(jnp.sum(d_in_low.astype(f32), axis=0))
        grads_w_in.append(jnp.einsum("ek,ej->kj", state_low, d_in_low, preferred_element_type=f32))
        d_low = d_low + jnp.einsum("ej,kj->ek", d_in_low, w_in[expert], preferred_element_type=f32)
        grads_gain.append(d_gain_one)
        grads_bias.append(d_bias_one)
    mixture_terms = (
        jnp.stack(grads_w_in),
        jnp.stack(grads_b_in),
        jnp.stack(grads_w_out),
        jnp.stack(grads_b_out),
        jnp.stack(grads_gain),
        jnp.stack(grads_bias),
        d_shared_gate,
        d_group_gate,
        d_tower_in,
        d_tower_in_bias,
        d_tower_out,
        d_tower_out_bias,
    )
    d_state = d_after + d_low
    d_pre_proj, d_inter_gain, d_inter_bias = jax.vjp(gelu_norm, pre_proj, inter_gain, inter_bias)[
        1
    ](d_state)
    d_proj_low = d_pre_proj.astype(bf16)
    d_proj_b = jnp.sum(d_proj_low.astype(f32), axis=0)
    d_proj_w = jnp.einsum("ef,ek->fk", joined, d_proj_low, preferred_element_type=f32)
    d_joined = jnp.einsum("ek,fk->ef", d_proj_low, proj_w, preferred_element_type=f32)
    d_centered = d_joined[:, field_width + width :]
    d_joined_t = d_joined.T
    scaled_t = d_joined_t[field_width : field_width + width] / seq_len[None, :]
    slot_grad = slots_back(field_t, d_joined_t[:field_width].astype(bf16), scaled_t.astype(bf16), spread)
    small_terms = mixture_terms[1:2] + mixture_terms[3:8] + mixture_terms[9:]
    small_terms += (d_proj_b, d_inter_gain, d_inter_bias)
    small_terms += (exact_dot(onehot.T, d_centered), exact_dot(onehot.T, d_centered * centered))
    flat = jnp.concatenate([term.reshape(-1) for term in small_terms])
    flat = jnp.pad(flat, (0, -flat.size % (devices * 1024))).reshape(-1, 128)
    n_experts, depth, units = w_in.shape
    half = units // 2
    big = (
        jnp.stack([mixture_terms[0][x, :, h * half : (h + 1) * half] for x in range(n_experts) for h in range(2)]),
        mixture_terms[2].reshape(2 * n_experts, half, depth),
        mixture_terms[8].reshape(1, -1, tower_in.shape[2]),
        d_proj_w[None],
    )
    returned, flat, totals = reduce_all(slot_grad, flat, [x.astype(bf16) for x in big], devices)
    totals[0] = totals[0].reshape(n_experts, -1, depth, totals[0].shape[3])
    d_table, d_w_in, d_w_out, d_tower_in, d_proj_w = finish(line.reshape(-1), group, returned, table.shape[0], totals)
    flat = flat.reshape(-1)
    sums, at = [], 0
    for term in small_terms:
        sums.append(flat[at : at + term.size].reshape(term.shape))
        at += term.size
    d_b_in, d_b_out, d_gain, d_bias, d_shared_gate, d_group_gate, d_tower_in_bias = sums[:7]
    d_tower_out, d_tower_out_bias, d_proj_b, d_inter_gain, d_inter_bias, sum_grad, sum_cross = sums[7:]
    d_dense = event_inverse * (
        d_centered
        - exact_dot(onehot, sum_grad / count)
        - centered * exact_dot(onehot, sum_cross / count)
    )
    return (
        pred,
        d_dense,
        d_table.T,
        d_proj_w,
        d_proj_b,
        d_inter_gain,
        d_inter_bias,
        d_w_in.reshape(w_in.shape),
        d_b_in,
        d_w_out.reshape(w_out.shape),
        d_b_out,
        d_gain,
        d_bias,
        d_shared_gate,
        d_group_gate,
        d_tower_in.reshape(tower_in.shape),
        d_tower_in_bias,
        d_tower_out,
        d_tower_out_bias,
    )


def solution(mesh):
    placed = (
        P(("wide", "narrow"), None),
        P(("wide", "narrow"), None),
        P(("wide", "narrow")),
        P(("wide", "narrow"), None),
        P(("wide", "narrow"), None, None),
        P(("wide", "narrow"), None),
        P(("wide", "narrow"), None),
        P(("wide", "narrow"), None),
        P(),
        P(),
        P(),
        P(),
        P(),
        P(),
        P(),
        P(),
        P(),
        P(),
        P(),
        P(),
        P(),
        P(),
        P(),
        P(),
        P(("wide", "narrow")),
    )
    return jax.shard_map(
        local,
        mesh=mesh,
        in_specs=placed,
        out_specs=(
            P(("wide", "narrow")),
            P(("wide", "narrow"), None),
            P(("wide", "narrow"), None),
            P(),
            P(),
            P(),
            P(),
            P(),
            P(),
            P(),
            P(),
            P(),
            P(),
            P(),
            P(),
            P(),
            P(),
            P(),
            P(),
        ),
        check_vma=False,
    )
```

```python
import functools
import math

import jax
import jax.numpy as jnp
from jax import lax
from jax.experimental import pallas as pl
from jax.experimental.pallas import tpu as pltpu
from jax.sharding import PartitionSpec as P

SHARED = 2
DOMAINS = 2

EPSILON = 1e-05

f32 = jnp.float32
bf16 = jnp.bfloat16
i32 = jnp.int32
MESH = pl.DeviceIdType.MESH
AXES = ("wide", "narrow")
NT = (((1,), (1,)), ((), ()))
TN = (((0,), (0,)), ((), ()))
VMEM_LIMIT = 60 * 1024 * 1024
ROW_CHUNK = 1024
GROUP = 8
SPAN = 6


def vmem():
    return pl.BlockSpec(memory_space=pltpu.VMEM)


def smem():
    return pl.BlockSpec(memory_space=pltpu.SMEM)


def hbm():
    return pl.BlockSpec(memory_space=pl.ANY)


def params(**more):
    return pltpu.CompilerParams(vmem_limit_bytes=VMEM_LIMIT, **more)


def line_of(rows):
    return jnp.left_shift(jnp.right_shift(rows, 10), 7) + jnp.bitwise_and(rows, 127)


def lane_group_of(rows):
    return jnp.bitwise_and(jnp.right_shift(rows, 7), 7)


def identity(n):
    return (lax.broadcasted_iota(i32, (n, n), 0) == lax.broadcasted_iota(i32, (n, n), 1)).astype(bf16)


def finish_kernel(n_more, line, line_v, group, returned, *refs):
    more, out, more_out = refs[:n_more], refs[n_more], refs[n_more + 1 : 2 * n_more + 1]
    lines, vals = refs[2 * n_more + 1 :]
    step = pl.program_id(0)
    per = out.shape[1] // ROW_CHUNK

    @pl.when(step == 0)
    def _():
        blocks, _, cap = group.shape

        def clear(i, carry):
            lines[pl.ds(pl.multiple_of(i * 1024, 1024), 1024), :] = jnp.zeros((1024, 128), f32)
            return carry

        lax.fori_loop(0, lines.shape[0] // 1024, clear, 0)
        batch = 32
        a = lax.div(lax.broadcasted_iota(i32, (cap, cap), 0), batch)
        near = a == lax.div(lax.broadcasted_iota(i32, (cap, cap), 1), batch)

        def serve(s, carry):
            which, own = group[s], returned[s].astype(f32)
            wide = jnp.concatenate([jnp.where(which == g, own, 0.0) for g in range(8)], axis=0)
            along = jnp.broadcast_to(line_v[s].astype(f32), (cap, cap))
            same = jnp.where(jnp.logical_and(along == along.T, near), 1.0, 0.0).astype(bf16)
            vals[...] = lax.dot_general(same, wide.astype(bf16), NT, preferred_element_type=f32)

            def add(u, carry):
                places, sums = [], []
                for k in range(batch):
                    j = u * batch + k
                    places.append(line[s * cap + j])
                    sums.append(lines[pl.ds(places[-1], 1), :] + vals[pl.ds(j, 1), :])
                for place, total in zip(places, sums):
                    lines[pl.ds(place, 1), :] = total
                return carry

            lax.fori_loop(0, cap // batch, add, 0)
            return carry

        lax.fori_loop(0, blocks, serve, 0)

    def turn(c, carry):
        width = out.shape[0]
        turned = lines[pl.ds(pl.multiple_of((step * per + c) * 128, 128), 128), :].T
        for g in range(8):
            at = pl.multiple_of(c * ROW_CHUNK + g * 128, 128)
            out[:, pl.ds(at, 128)] = turned[g * width : (g + 1) * width]
        return carry

    lax.fori_loop(0, per, turn, 0, unroll=4)
    for source, target in zip(more, more_out):
        tall, blocks, rows, lanes = source.shape
        for s in range(tall):
            for c in range(blocks):
                target[s * rows : (s + 1) * rows, c * lanes : (c + 1) * lanes] = source[s, c].astype(f32)


def finish(line, group, returned, rows, more):
    blocks, width, cap = returned.shape
    steps = 4
    in_more, out_more, shapes = [], [], []
    for x in more:
        tall, parts, r, lanes = x.shape
        if tall > 1:
            in_more.append(pl.BlockSpec((tall // steps, parts, r, lanes), lambda i: (i, 0, 0, 0)))
        else:
            in_more.append(pl.BlockSpec((1, parts, r // steps, lanes), lambda i: (0, 0, i, 0)))
        out_more.append(pl.BlockSpec((tall * r // steps, parts * lanes), lambda i: (i, 0)))
        shapes.append(jax.ShapeDtypeStruct((tall * r, parts * lanes), f32))
    return pl.pallas_call(
        functools.partial(finish_kernel, len(more)),
        grid=(steps,),
        in_specs=[smem(), vmem(), vmem(), vmem()] + in_more,
        out_specs=[pl.BlockSpec((width, rows // steps), lambda i: (0, i))] + out_more,
        out_shape=[jax.ShapeDtypeStruct((width, rows), f32)] + shapes,
        scratch_shapes=[pltpu.VMEM((rows // 8, 128), f32), pltpu.VMEM((cap, 128), f32)],
        compiler_params=params(),
        name="finish",
    )(line, line.reshape(blocks, 1, cap), group, returned, *more)


def hot(rows, index):
    column = lax.broadcasted_iota(i32, (rows, index.shape[1]), 0)
    return jnp.where(column == index, 1.0, 0.0).astype(bf16)


def count_kernel(starts, behave, counts, sums):
    owners, events, cap = counts.shape
    shift = cap.bit_length() - 1
    place = lax.broadcasted_iota(i32, (SPAN, 128), 0) * 128 + lax.broadcasted_iota(i32, (SPAN, 128), 1)
    last_block = behave.shape[0] - SPAN

    def group(e0, k):
        first, last = starts[e0], starts[e0 + GROUP]
        cuts = [starts[e0 + i] for i in range(1, GROUP)]
        b0 = lax.div(first, 128)

        def part(m):
            begin = b0 + m * SPAN
            b = jnp.minimum(begin, last_block)
            slot = behave[pl.ds(b, SPAN), :]
            p = place + b * 128
            event = jnp.zeros_like(p)
            for cut in cuts:
                event = event + jnp.where(p >= cut, 1, 0)
            key = jnp.right_shift(slot, shift) * GROUP + event
            mine = jnp.logical_and(jnp.logical_and(p >= first, p < last), p >= begin * 128)
            key = jnp.where(mine, key, -1)
            low = jnp.bitwise_and(slot, cap - 1)
            left = jnp.concatenate([hot(owners * GROUP, key[q : q + 1]) for q in range(SPAN)], axis=1)
            right = jnp.concatenate([hot(cap, low[q : q + 1]) for q in range(SPAN)], axis=1)
            return lax.dot_general(left, right, NT, preferred_element_type=f32)

        sums[k] = part(0)

        def more(m, carry):
            sums[k] += part(m)
            return carry

        lax.fori_loop(1, lax.div(last - b0 * 128 + (SPAN * 128 - 1), SPAN * 128), more, 0)

    def pair(g, carry):
        e0 = g * (2 * GROUP)
        group(e0, 0)
        group(e0 + GROUP, 1)
        for o in range(owners):
            both = [sums[k, o * GROUP : (o + 1) * GROUP, :] for k in range(2)]
            at = pl.ds(pl.multiple_of(e0, 2 * GROUP), 2 * GROUP)
            counts[o, at, :] = jnp.concatenate(both, axis=0).astype(bf16)
        return carry

    lax.fori_loop(0, events // (2 * GROUP), pair, 0)


def slot_counts(starts, behave, owners, cap):
    events = starts.shape[0] - 1
    return pl.pallas_call(
        count_kernel,
        in_specs=[smem(), vmem()],
        out_specs=vmem(),
        out_shape=jax.ShapeDtypeStruct((owners, events, cap), bf16),
        scratch_shapes=[pltpu.VMEM((2, owners * GROUP, cap), f32)],
        compiler_params=params(),
        name="slot_counts",
    )(starts, behave)


def slots_back_kernel(field, d_fields, d_pooled, counts, out, total):
    owners, width, cap = out.shape
    n_field, events = field.shape
    shift = cap.bit_length() - 1
    total[...] = jnp.zeros(total.shape, f32)

    def one(f, carry):
        slot = field[pl.ds(f, 1), :]
        owner = jnp.right_shift(slot, shift)
        d = d_fields[pl.ds(pl.multiple_of(f * width, width), width), :].astype(f32)
        wide = jnp.concatenate([jnp.where(owner == o, d, 0.0).astype(bf16) for o in range(owners)], axis=0)
        total[...] += lax.dot_general(
            wide, hot(cap, jnp.bitwise_and(slot, cap - 1)), NT, preferred_element_type=f32
        )
        return carry

    lax.fori_loop(0, n_field, one, 0, unroll=2)
    for o in range(owners):
        behave = jnp.dot(d_pooled[...], counts[o], preferred_element_type=f32)
        out[o] = (total[o * width : (o + 1) * width] + behave).astype(bf16)


def slots_back(field_t, d_fields, d_pooled, counts):
    owners, _, cap = counts.shape
    width = d_pooled.shape[0]
    return pl.pallas_call(
        slots_back_kernel,
        in_specs=[vmem()] * 4,
        out_specs=vmem(),
        out_shape=jax.ShapeDtypeStruct((owners, width, cap), bf16),
        scratch_shapes=[pltpu.VMEM((owners * width, cap), f32)],
        compiler_params=params(),
        name="slots_back",
    )(field_t, d_fields, d_pooled, counts)


def place_bits():
    return [(axis, b) for axis in AXES for b in range(lax.axis_size(axis).bit_length() - 1)]


def bit_value(bit):
    return lax.rem(lax.div(lax.axis_index(bit[0]), 1 << bit[1]), 2)


def across(bit):
    axis, b = bit
    place = {a: lax.axis_index(a) for a in AXES}
    place[axis] = place[axis] + (1 - 2 * bit_value(bit)) * (1 << b)
    return tuple(place[a] for a in AXES)


class Piece:
    def __init__(self, part, inbox, total, order, sends, recvs):
        self.part, self.inbox, self.total = part, inbox, total
        self.order, self.sends, self.recvs = order, sends, recvs
        self.rows = part.shape[0]
        self.grain = self.rows >> len(order)
        self.offsets, self.copies = [0], []

    def at(self, ref, offset, n):
        return ref.at[pl.ds(pl.multiple_of(offset, self.grain), n)]

    def send(self):
        k, depth = len(self.copies), len(self.order)
        if k < depth:
            bit, half = self.order[k], self.rows >> (k + 1)
            value, offset = bit_value(bit), self.offsets[k]
            self.offsets.append(offset + value * half)
            source = self.at(self.part, offset + (1 - value) * half, half)
            target = self.inbox.at[pl.ds(self.rows - (self.rows >> k), half)]
        else:
            s = 2 * depth - 1 - k
            bit = self.order[s]
            source = target = self.at(self.total, self.offsets[s + 1], self.rows >> (s + 1))
        copy = pltpu.make_async_remote_copy(
            src_ref=source,
            dst_ref=target,
            send_sem=self.sends.at[k],
            recv_sem=self.recvs.at[k],
            device_id=across(bit),
            device_id_type=MESH,
        )
        copy.start()
        self.copies.append(copy)

    def take(self):
        k, depth = len(self.copies) - 1, len(self.order)
        self.copies[k].wait_recv()
        if k < depth:
            n, base, offset = self.rows >> (k + 1), self.rows - (self.rows >> k), self.offsets[k + 1]
            target = self.total if k == depth - 1 else self.part
            chunk = math.gcd(n, 64)

            def add(i, carry):
                at = pl.ds(pl.multiple_of(offset + i * chunk, math.gcd(self.grain, chunk)), chunk)
                came = self.inbox[pl.ds(pl.multiple_of(base + i * chunk, chunk), chunk), :]
                target[at, :] = (self.part[at, :].astype(f32) + came.astype(f32)).astype(target.dtype)
                return carry

            lax.fori_loop(0, n // chunk, add, 0)
        if k + 1 < 2 * depth:
            self.send()

    def drain(self):
        for copy in self.copies:
            copy.wait_send()


def everyone_else():
    n_wide, n_narrow = (lax.axis_size(a) for a in AXES)
    w, n = (lax.axis_index(a) for a in AXES)
    me = w * n_narrow + n
    total = n_wide * n_narrow
    for d in range(1, total):
        other = lax.rem(me + d, total)
        yield d, other, (lax.div(other, n_narrow), lax.rem(other, n_narrow))


def meet_all():
    barrier = pltpu.get_barrier_semaphore()
    for _, _, place in everyone_else():
        pl.semaphore_signal(barrier, inc=1, device_id=place, device_id_type=MESH)
    pl.semaphore_wait(barrier, lax.axis_size("wide") * lax.axis_size("narrow") - 1)


def lanes_of(rows, columns, devices):
    lanes = columns
    while lanes > 128 and (rows * (columns // lanes)) % (16 * devices):
        lanes //= 2
    return lanes


ORDERS = "BDADABGGBBBABGBAAA"


class Block:
    def __init__(self, rows, columns, devices):
        self.rows, self.columns = rows, columns
        self.lanes = lanes_of(rows, columns, devices)
        self.blocks = columns // self.lanes
        self.padded = -(-rows * self.blocks // (16 * devices)) * 16 * devices

    def put(self, piece, value):
        for c in range(self.blocks):
            piece[c * self.rows : (c + 1) * self.rows, :] = value[:, c * self.lanes : (c + 1) * self.lanes]
        extra = self.padded - self.rows * self.blocks
        if extra:
            piece[self.rows * self.blocks :, :] = jnp.zeros((extra, self.lanes), piece.dtype)

    def whole(self, total, n):
        return total[:, : self.rows * self.blocks].reshape(n, self.blocks, self.rows, self.lanes)


def orders():
    if tuple(lax.axis_size(a) for a in AXES) != (8, 4):
        return [place_bits()] * len(ORDERS)
    core, y, x, z0, z1 = ("narrow", 0), ("narrow", 1), ("wide", 0), ("wide", 1), ("wide", 2)
    ways = {
        "A": [core, x, y, z0, z1],
        "B": [core, y, x, z0, z1],
        "D": [core, z0, z1, y, x],
        "G": [core, z0, z1, x, y],
    }
    return [ways[way] for way in ORDERS]


def reduce_kernel(blocks, n_big, slot_grad, small, *refs):
    big = refs[:n_big]
    returned, small_total = refs[n_big : n_big + 2]
    totals = refs[n_big + 2 : 2 * n_big + 2]
    small_part, small_inbox = refs[2 * n_big + 2 : 2 * n_big + 4]
    parts = refs[2 * n_big + 4 : 3 * n_big + 4]
    inboxes = refs[3 * n_big + 4 : 4 * n_big + 4]
    sends, recvs, slot_sends, slot_recvs = refs[4 * n_big + 4 :]
    meet_all()
    me = lax.axis_index("wide") * lax.axis_size("narrow") + lax.axis_index("narrow")
    slot_copies = []
    for d, other, place in everyone_else():
        copy = pltpu.make_async_remote_copy(
            src_ref=slot_grad.at[other],
            dst_ref=returned.at[me],
            send_sem=slot_sends.at[d],
            recv_sem=slot_recvs.at[d],
            device_id=place,
            device_id_type=MESH,
        )
        copy.start()
        slot_copies.append(copy)
    returned[me] = slot_grad[me]
    pieces = [Piece(small_part, small_inbox, small_total, orders()[0], sends.at[0], recvs.at[0])]
    small_part[...] = small[...]
    pieces[0].send()
    for a in range(n_big):
        for i in range(parts[a].shape[0]):
            k = len(pieces)
            piece = Piece(parts[a].at[i], inboxes[a].at[i], totals[a].at[i], orders()[k - 1], sends.at[k], recvs.at[k])
            blocks[a].put(parts[a].at[i], big[a][i])
            piece.send()
            pieces.append(piece)
    for _ in range(2 * len(place_bits())):
        for piece in pieces:
            piece.take()
    for copy in slot_copies:
        copy.wait_recv()
    for copy in slot_copies:
        copy.wait_send()
    for piece in pieces:
        piece.drain()


def reduce_all(slot_grad, small, big, devices):
    blocks = [Block(x.shape[1], x.shape[2], devices) for x in big]
    shapes = [(x.shape[0], b.padded, b.lanes) for x, b in zip(big, blocks)]
    n_pieces = 1 + sum(x.shape[0] for x in big)
    steps = 2 * (devices.bit_length() - 1)
    out = pl.pallas_call(
        functools.partial(reduce_kernel, blocks, len(big)),
        in_specs=[vmem()] * (2 + len(big)),
        out_specs=[vmem()] * (2 + len(big)),
        out_shape=[jax.ShapeDtypeStruct(slot_grad.shape, bf16), jax.ShapeDtypeStruct(small.shape, f32)]
        + [jax.ShapeDtypeStruct(s, bf16) for s in shapes],
        scratch_shapes=[pltpu.VMEM(small.shape, f32)] * 2
        + [pltpu.VMEM(s, bf16) for s in shapes] * 2
        + [pltpu.SemaphoreType.DMA((n_pieces, steps))] * 2
        + [pltpu.SemaphoreType.DMA((devices,))] * 2,
        compiler_params=params(collective_id=0, has_side_effects=True),
        name="reduce_all",
    )(slot_grad, small, *big)
    return out[0], out[1], [b.whole(t, x.shape[0]) for b, t, x in zip(blocks, out[2:], big)]


def lookup_kernel(
    requests, table, live, field, counts, dense, domains,
    fields, pooled, line_out, group, stats_out,
    tab, lines, got, line, line_smem, found, rows, slots, stats, stats_in,
    tab_sems, line_sem, ask_sends, ask_recvs, row_sends, row_recvs, stat_sends, stat_recvs,
):
    owners, _, cap = requests.shape
    width = tab.shape[0]
    n_field, events = field.shape
    chunks = tab_sems.shape[0]
    part = tab.shape[1] // chunks
    batch = 4
    n_narrow = lax.axis_size("narrow")
    me = lax.axis_index("wide") * n_narrow + lax.axis_index("narrow")

    loads = []
    for c in range(chunks):
        at = pl.ds(c * part, part)
        loads.append(pltpu.make_async_copy(table.at[:, at], tab.at[:, at], tab_sems.at[c]))
        loads[-1].start()
    lane = lax.broadcasted_iota(i32, (width, 128), 1)
    mine = jnp.zeros((width, 128), f32)
    for d in range(DOMAINS):
        here = domains[...] == d
        value = jnp.where(here, dense[...], 0.0)
        one = jnp.broadcast_to(jnp.where(here, 1.0, 0.0), value.shape)
        for k, term in enumerate((value, value * value, one)):
            mine = jnp.where(lane == k * DOMAINS + d, jnp.sum(term, axis=1, keepdims=True), mine)
    stats[...] = mine

    meet_all()

    def peer(d):
        other = lax.rem(me + d, owners)
        return other, (lax.div(other, n_narrow), lax.rem(other, n_narrow))

    def ask(d):
        other, place = peer(d)
        return pltpu.make_async_remote_copy(
            src_ref=requests.at[other], dst_ref=line.at[me], send_sem=ask_sends.at[d],
            recv_sem=ask_recvs.at[d], device_id=place, device_id_type=MESH)

    def tell(d):
        _, place = peer(d)
        return pltpu.make_async_remote_copy(
            src_ref=stats, dst_ref=stats_in.at[me], send_sem=stat_sends.at[d],
            recv_sem=stat_recvs.at[d], device_id=place, device_id_type=MESH)

    def answer(d):
        other, place = peer(d)
        return pltpu.make_async_remote_copy(
            src_ref=found.at[other], dst_ref=rows.at[me], send_sem=row_sends.at[d],
            recv_sem=row_recvs.at[d], device_id=place, device_id_type=MESH)

    def each(first, act):
        def step(d, carry):
            act(d)
            return carry

        lax.fori_loop(first, owners, step, 0)

    each(1, lambda d: ask(d).start())
    each(1, lambda d: tell(d).start())
    line[me] = requests[me]
    stats_in[me] = stats[...]

    eye = identity(128)
    for c in range(chunks):
        loads[c].wait()

        def turn(i, carry):
            base = pl.multiple_of(c * part + i * ROW_CHUNK, ROW_CHUNK)
            stack = jnp.concatenate([tab[:, pl.ds(base + g * 128, 128)] for g in range(8)], axis=0)
            at = pl.multiple_of((c * part // ROW_CHUNK + i) * 128, 128)
            lines[pl.ds(at, 128), :] = lax.dot_general(eye, stack, NT, preferred_element_type=f32)
            return carry

        lax.fori_loop(0, part // ROW_CHUNK, turn, 0, unroll=8)

    each(1, lambda d: ask(d).wait_recv())
    group[...] = lane_group_of(line[...])
    line_out[...] = line_of(line[...])
    to_smem = pltpu.make_async_copy(line_out, line_smem, line_sem)
    to_smem.start()
    to_smem.wait()

    def serve(b, carry):
        sources = [lax.rem(me + b * batch + k, owners) for k in range(batch)]
        for k in range(batch):

            def fetch(u, carry):
                for i in range(64):
                    j = u * 64 + i
                    got[pl.ds(k * cap + j, 1), :] = lines[pl.ds(line_smem[sources[k], 0, j], 1), :]
                return carry

            lax.fori_loop(0, cap // 64, fetch, 0)
        turned = lax.dot_general(eye, got[...].astype(bf16), NT, preferred_element_type=f32)
        for k in range(batch):
            which = group[sources[k]]
            picked = turned[:width, k * cap : (k + 1) * cap]
            for g in range(1, 8):
                picked = jnp.where(which == g, turned[g * width : (g + 1) * width, k * cap : (k + 1) * cap], picked)
            found[sources[k]] = picked.astype(bf16)
        for k in range(batch):
            d = b * batch + k
            if k:
                answer(d).start()
            else:
                pl.when(b > 0)(lambda: answer(d).start())
        return carry

    lax.fori_loop(0, owners // batch, serve, 0)
    rows[me] = found[me]
    each(1, lambda d: tell(d).wait_recv())
    total = stats_in[0]
    for o in range(1, owners):
        total = total + stats_in[o]
    stats_out[...] = total

    each(1, lambda d: answer(d).wait_recv())
    shift = cap.bit_length() - 1
    column = lax.broadcasted_iota(i32, (width, cap), 1)
    for o in range(owners):
        slots[o * width : (o + 1) * width, :] = jnp.where(column < live[o], rows[o].astype(f32), 0.0).astype(bf16)

    def one(f, carry):
        slot = field[pl.ds(f, 1), :]
        owner = jnp.right_shift(slot, shift)
        all_owners = jnp.dot(slots[...], hot(cap, jnp.bitwise_and(slot, cap - 1)), preferred_element_type=f32)
        picked = all_owners[:width]
        for o in range(1, owners):
            picked = jnp.where(owner == o, all_owners[o * width : (o + 1) * width], picked)
        fields[pl.ds(pl.multiple_of(f * width, width), width), :] = picked.astype(bf16)
        return carry

    lax.fori_loop(0, n_field, one, 0, unroll=2)
    total = jnp.zeros((events, width), f32)
    for o in range(owners):
        total = total + lax.dot_general(counts[o], slots[o * width : (o + 1) * width, :], NT, preferred_element_type=f32)
    pooled[...] = total.T
    each(1, lambda d: ask(d).wait_send())
    each(1, lambda d: tell(d).wait_send())
    each(1, lambda d: answer(d).wait_send())


def lookup(requests, table_t, live, field_t, counts, dense_t, domains):
    owners, _, cap = requests.shape
    width, rows = table_t.shape
    n_field, events = field_t.shape
    chunks = 6
    dma = pltpu.SemaphoreType.DMA
    return pl.pallas_call(
        lookup_kernel,
        in_specs=[vmem(), hbm(), smem(), vmem(), vmem(), vmem(), vmem()],
        out_specs=[vmem()] * 5,
        out_shape=[
            jax.ShapeDtypeStruct((n_field * width, events), bf16),
            jax.ShapeDtypeStruct((width, events), f32),
            jax.ShapeDtypeStruct((owners, 1, cap), i32),
            jax.ShapeDtypeStruct((owners, 1, cap), i32),
            jax.ShapeDtypeStruct((width, 128), f32),
        ],
        scratch_shapes=[
            pltpu.VMEM((width, rows), bf16),
            pltpu.VMEM((rows // 8, 128), f32),
            pltpu.VMEM((4 * cap, 128), f32),
            pltpu.VMEM((owners, 1, cap), i32),
            pltpu.SMEM((owners, 1, cap), i32),
            pltpu.VMEM((owners, width, cap), bf16),
            pltpu.VMEM((owners, width, cap), bf16),
            pltpu.VMEM((owners * width, cap), bf16),
            pltpu.VMEM((width, 128), f32),
            pltpu.VMEM((owners, width, 128), f32),
            dma((chunks,)),
            dma,
        ]
        + [dma((owners,))] * 6,
        compiler_params=params(collective_id=1, has_side_effects=True),
        name="lookup",
    )(requests, table_t, live, field_t, counts, dense_t, domains)


def layer_norm(values, gain, shift):
    center = values - jnp.mean(values, axis=-1, keepdims=True)
    spread = jnp.mean(center * center, axis=-1, keepdims=True)
    return center * lax.rsqrt(spread + EPSILON) * gain + shift


def gelu_norm(pre, gain, shift):
    return layer_norm(jax.nn.gelu(pre), gain, shift)


def mixture(shared_logits, group_logits, outputs, onehot):
    shared_weights = jax.nn.softmax(shared_logits, axis=-1)
    shared_mix = jnp.sum(shared_weights.T[:, :, None] * outputs[:SHARED], axis=0)
    picked = jnp.sum(onehot[:, :, None] * group_logits, axis=1)
    group_weights = jax.nn.softmax(picked, axis=-1)
    domain_out = jnp.sum(onehot.T[:, :, None] * outputs[SHARED:], axis=0)
    return group_weights[:, 0:1] * shared_mix + group_weights[:, 1:2] * domain_out


def tower_head(pre_stack, tower_out, tower_out_bias, onehot):
    hidden = jax.nn.gelu(pre_stack)
    logits = jnp.sum(hidden * tower_out[:, None, :], axis=-1) + tower_out_bias[:, None]
    return jax.nn.sigmoid(jnp.sum(onehot.T * logits, axis=0))


def exact_dot(left, right):
    return jnp.dot(left, right, precision=lax.Precision.HIGHEST)


def local(
    table,
    dense,
    domains,
    lengths,
    requests,
    counts,
    field_slots,
    behave_slots,
    proj_w,
    proj_b,
    inter_gain,
    inter_bias,
    w_in,
    b_in,
    w_out,
    b_out,
    expert_gain,
    expert_bias,
    shared_gate,
    group_gate,
    tower_in,
    tower_in_bias,
    tower_out,
    tower_out_bias,
    pred_cotangent,
):
    n_wide = lax.axis_size("wide")
    n_narrow = lax.axis_size("narrow")
    devices = n_wide * n_narrow
    capacity = requests.shape[2]
    events = dense.shape[0]
    width = table.shape[1]
    sizes_seq = lengths.reshape(-1)
    starts = jnp.concatenate([jnp.zeros((1,), i32), jnp.cumsum(sizes_seq)])
    spread = slot_counts(starts, behave_slots.reshape(-1, 128), devices, capacity)
    field_t = field_slots.T
    field_width = field_t.shape[0] * width
    seq_len = sizes_seq.astype(f32)
    fields_t, pooled_sum, line, group, stats = lookup(
        requests.reshape(devices, 1, capacity), table.T, counts.reshape(-1), field_t, spread, dense.T, domains[None]
    )
    onehot = (domains[:, None] == jnp.arange(DOMAINS, dtype=i32)[None, :]).astype(f32)
    totals = stats[:, :DOMAINS].T
    squares = stats[:, DOMAINS : 2 * DOMAINS].T
    count = stats[:1, 2 * DOMAINS : 3 * DOMAINS].T
    mean = totals / count
    variance = squares / count - mean * mean
    inverse = lax.rsqrt(variance + EPSILON)
    event_inverse = exact_dot(onehot, inverse)
    centered = (dense - exact_dot(onehot, mean)) * event_inverse
    centered_low = centered.astype(bf16)
    pooled_t = (pooled_sum / seq_len[None, :]).astype(bf16)
    joined = jnp.concatenate([fields_t, pooled_t, centered_low.T], axis=0).T
    pre_proj = jnp.dot(joined, proj_w, preferred_element_type=f32) + proj_b
    state = gelu_norm(pre_proj, inter_gain, inter_bias)
    state_low = state.astype(bf16)
    kept = []
    outputs = []
    for expert in range(w_in.shape[0]):
        pre_in = jnp.dot(state_low, w_in[expert], preferred_element_type=f32) + b_in[expert]
        active = jax.nn.gelu(pre_in).astype(bf16)
        pre_out = jnp.dot(active, w_out[expert], preferred_element_type=f32) + b_out[expert]
        outputs.append(layer_norm(pre_out, expert_gain[expert], expert_bias[expert]))
        kept.append((pre_in, active, pre_out))
    outputs = jnp.stack(outputs)
    shared_logits = jnp.dot(state_low, shared_gate, preferred_element_type=f32)
    group_logits = jnp.einsum("ek,dkg->edg", state_low, group_gate, preferred_element_type=f32)

    def mixing(shared_part, group_part, expert_part):
        return mixture(shared_part, group_part, expert_part, onehot)

    mixed, mixing_back = jax.vjp(mixing, shared_logits, group_logits, outputs)
    after = state + mixed
    after_low = after.astype(bf16)
    tower_pre = (
        jnp.einsum("ek,dkj->dej", after_low, tower_in, preferred_element_type=f32)
        + tower_in_bias[:, None, :]
    )

    def heading(pre_part, out_part, bias_part):
        return tower_head(pre_part, out_part, bias_part, onehot)

    pred, heading_back = jax.vjp(heading, tower_pre, tower_out, tower_out_bias)
    d_tower_pre, d_tower_out, d_tower_out_bias = heading_back(pred_cotangent)
    d_tower_low = d_tower_pre.astype(bf16)
    d_tower_in = jnp.einsum("ek,dej->dkj", after_low, d_tower_low, preferred_element_type=f32)
    d_tower_in_bias = jnp.sum(d_tower_low.astype(f32), axis=1)
    d_after = jnp.einsum("dej,dkj->ek", d_tower_low, tower_in, preferred_element_type=f32)
    d_shared_logits, d_group_logits, d_outputs = mixing_back(d_after)
    state_wide = state_low.astype(f32)
    d_shared_gate = jnp.einsum(
        "ek,es->ks", state_wide, d_shared_logits, precision=lax.Precision.HIGHEST
    )
    d_group_gate = jnp.einsum(
        "ek,edg->dkg", state_wide, d_group_logits, precision=lax.Precision.HIGHEST
    )
    d_low = jnp.einsum(
        "es,ks->ek", d_shared_logits, shared_gate.astype(f32), precision=lax.Precision.HIGHEST
    )
    d_low = d_low + jnp.einsum(
        "edg,dkg->ek", d_group_logits, group_gate.astype(f32), precision=lax.Precision.HIGHEST
    )
    grads_w_in, grads_b_in, grads_w_out, grads_b_out, grads_gain, grads_bias = (
        [],
        [],
        [],
        [],
        [],
        [],
    )
    for expert in range(w_in.shape[0]):
        pre_in, active, pre_out = kept[expert]
        norm_back = jax.vjp(layer_norm, pre_out, expert_gain[expert], expert_bias[expert])[1]
        d_pre_out, d_gain_one, d_bias_one = norm_back(d_outputs[expert])
        d_out_low = d_pre_out.astype(bf16)
        grads_b_out.append(jnp.sum(d_out_low.astype(f32), axis=0))
        grads_w_out.append(jnp.einsum("ej,ek->jk", active, d_out_low, preferred_element_type=f32))
        d_active = jnp.einsum("ek,jk->ej", d_out_low, w_out[expert], preferred_element_type=f32)
        d_pre_in = jax.vjp(jax.nn.gelu, pre_in)[1](d_active)[0]
        d_in_low = d_pre_in.astype(bf16)
        grads_b_in.append(jnp.sum(d_in_low.astype(f32), axis=0))
        grads_w_in.append(jnp.einsum("ek,ej->kj", state_low, d_in_low, preferred_element_type=f32))
        d_low = d_low + jnp.einsum("ej,kj->ek", d_in_low, w_in[expert], preferred_element_type=f32)
        grads_gain.append(d_gain_one)
        grads_bias.append(d_bias_one)
    mixture_terms = (
        jnp.stack(grads_w_in),
        jnp.stack(grads_b_in),
        jnp.stack(grads_w_out),
        jnp.stack(grads_b_out),
        jnp.stack(grads_gain),
        jnp.stack(grads_bias),
        d_shared_gate,
        d_group_gate,
        d_tower_in,
        d_tower_in_bias,
        d_tower_out,
        d_tower_out_bias,
    )
    d_state = d_after + d_low
    d_pre_proj, d_inter_gain, d_inter_bias = jax.vjp(gelu_norm, pre_proj, inter_gain, inter_bias)[
        1
    ](d_state)
    d_proj_low = d_pre_proj.astype(bf16)
    d_proj_b = jnp.sum(d_proj_low.astype(f32), axis=0)
    d_proj_w = jnp.einsum("ef,ek->fk", joined, d_proj_low, preferred_element_type=f32)
    d_joined = jnp.einsum("ek,fk->ef", d_proj_low, proj_w, preferred_element_type=f32)
    d_centered = d_joined[:, field_width + width :]
    d_joined_t = d_joined.T
    scaled_t = d_joined_t[field_width : field_width + width] / seq_len[None, :]
    slot_grad = slots_back(field_t, d_joined_t[:field_width].astype(bf16), scaled_t.astype(bf16), spread)
    small_terms = mixture_terms[1:2] + mixture_terms[3:8] + mixture_terms[9:]
    small_terms += (d_proj_b, d_inter_gain, d_inter_bias)
    small_terms += (exact_dot(onehot.T, d_centered), exact_dot(onehot.T, d_centered * centered))
    flat = jnp.concatenate([term.reshape(-1) for term in small_terms])
    flat = jnp.pad(flat, (0, -flat.size % (devices * 1024))).reshape(-1, 128)
    n_experts, depth, units = w_in.shape
    half = units // 2
    big = (
        jnp.stack([mixture_terms[0][x, :, h * half : (h + 1) * half] for x in range(n_experts) for h in range(2)]),
        mixture_terms[2].reshape(2 * n_experts, half, depth),
        mixture_terms[8].reshape(1, -1, tower_in.shape[2]),
        d_proj_w[None],
    )
    returned, flat, totals = reduce_all(slot_grad, flat, [x.astype(bf16) for x in big], devices)
    totals[0] = totals[0].reshape(n_experts, -1, depth, totals[0].shape[3])
    d_table, d_w_in, d_w_out, d_tower_in, d_proj_w = finish(line.reshape(-1), group, returned, table.shape[0], totals)
    flat = flat.reshape(-1)
    sums, at = [], 0
    for term in small_terms:
        sums.append(flat[at : at + term.size].reshape(term.shape))
        at += term.size
    d_b_in, d_b_out, d_gain, d_bias, d_shared_gate, d_group_gate, d_tower_in_bias = sums[:7]
    d_tower_out, d_tower_out_bias, d_proj_b, d_inter_gain, d_inter_bias, sum_grad, sum_cross = sums[7:]
    d_dense = event_inverse * (
        d_centered
        - exact_dot(onehot, sum_grad / count)
        - centered * exact_dot(onehot, sum_cross / count)
    )
    return (
        pred,
        d_dense,
        d_table.T,
        d_proj_w,
        d_proj_b,
        d_inter_gain,
        d_inter_bias,
        d_w_in.reshape(w_in.shape),
        d_b_in,
        d_w_out.reshape(w_out.shape),
        d_b_out,
        d_gain,
        d_bias,
        d_shared_gate,
        d_group_gate,
        d_tower_in.reshape(tower_in.shape),
        d_tower_in_bias,
        d_tower_out,
        d_tower_out_bias,
    )


def solution(mesh):
    placed = (
        P(("wide", "narrow"), None),
        P(("wide", "narrow"), None),
        P(("wide", "narrow")),
        P(("wide", "narrow"), None),
        P(("wide", "narrow"), None, None),
        P(("wide", "narrow"), None),
        P(("wide", "narrow"), None),
        P(("wide", "narrow"), None),
        P(),
        P(),
        P(),
        P(),
        P(),
        P(),
        P(),
        P(),
        P(),
        P(),
        P(),
        P(),
        P(),
        P(),
        P(),
        P(),
        P(("wide", "narrow")),
    )
    return jax.shard_map(
        local,
        mesh=mesh,
        in_specs=placed,
        out_specs=(
            P(("wide", "narrow")),
            P(("wide", "narrow"), None),
            P(("wide", "narrow"), None),
            P(),
            P(),
            P(),
            P(),
            P(),
            P(),
            P(),
            P(),
            P(),
            P(),
            P(),
            P(),
            P(),
            P(),
            P(),
            P(),
        ),
        check_vma=False,
    )
```

```python
import functools
import math

import jax
import jax.numpy as jnp
from jax import lax
from jax.experimental import pallas as pl
from jax.experimental.pallas import tpu as pltpu
from jax.sharding import PartitionSpec as P

SHARED = 2
DOMAINS = 2

EPSILON = 1e-05

f32 = jnp.float32
bf16 = jnp.bfloat16
i32 = jnp.int32
MESH = pl.DeviceIdType.MESH
AXES = ("wide", "narrow")
NT = (((1,), (1,)), ((), ()))
TN = (((0,), (0,)), ((), ()))
VMEM_LIMIT = 60 * 1024 * 1024
ROW_CHUNK = 1024
GROUP = 8
SPAN = 6


def vmem():
    return pl.BlockSpec(memory_space=pltpu.VMEM)


def smem():
    return pl.BlockSpec(memory_space=pltpu.SMEM)


def hbm():
    return pl.BlockSpec(memory_space=pl.ANY)


def params(**more):
    return pltpu.CompilerParams(vmem_limit_bytes=VMEM_LIMIT, **more)


def line_of(rows):
    return jnp.left_shift(jnp.right_shift(rows, 10), 7) + jnp.bitwise_and(rows, 127)


def lane_group_of(rows):
    return jnp.bitwise_and(jnp.right_shift(rows, 7), 7)


def identity(n):
    return (lax.broadcasted_iota(i32, (n, n), 0) == lax.broadcasted_iota(i32, (n, n), 1)).astype(bf16)


def hot(rows, index):
    column = lax.broadcasted_iota(i32, (rows, index.shape[1]), 0)
    return jnp.where(column == index, 1.0, 0.0).astype(bf16)


def count_kernel(starts, behave, counts, sums):
    owners, events, cap = counts.shape
    shift = cap.bit_length() - 1
    place = lax.broadcasted_iota(i32, (SPAN, 128), 0) * 128 + lax.broadcasted_iota(i32, (SPAN, 128), 1)
    last_block = behave.shape[0] - SPAN

    def group(e0, k):
        first, last = starts[e0], starts[e0 + GROUP]
        cuts = [starts[e0 + i] for i in range(1, GROUP)]
        b0 = lax.div(first, 128)

        def part(m):
            begin = b0 + m * SPAN
            b = jnp.minimum(begin, last_block)
            slot = behave[pl.ds(b, SPAN), :]
            p = place + b * 128
            event = jnp.zeros_like(p)
            for cut in cuts:
                event = event + jnp.where(p >= cut, 1, 0)
            key = jnp.right_shift(slot, shift) * GROUP + event
            mine = jnp.logical_and(jnp.logical_and(p >= first, p < last), p >= begin * 128)
            key = jnp.where(mine, key, -1)
            low = jnp.bitwise_and(slot, cap - 1)
            left = jnp.concatenate([hot(owners * GROUP, key[q : q + 1]) for q in range(SPAN)], axis=1)
            right = jnp.concatenate([hot(cap, low[q : q + 1]) for q in range(SPAN)], axis=1)
            return lax.dot_general(left, right, NT, preferred_element_type=f32)

        sums[k] = part(0)

        def more(m, carry):
            sums[k] += part(m)
            return carry

        lax.fori_loop(1, lax.div(last - b0 * 128 + (SPAN * 128 - 1), SPAN * 128), more, 0)

    def pair(g, carry):
        e0 = g * (2 * GROUP)
        group(e0, 0)
        group(e0 + GROUP, 1)
        for o in range(owners):
            both = [sums[k, o * GROUP : (o + 1) * GROUP, :] for k in range(2)]
            at = pl.ds(pl.multiple_of(e0, 2 * GROUP), 2 * GROUP)
            counts[o, at, :] = jnp.concatenate(both, axis=0).astype(bf16)
        return carry

    lax.fori_loop(0, events // (2 * GROUP), pair, 0)


def slot_counts(starts, behave, owners, cap):
    events = starts.shape[0] - 1
    return pl.pallas_call(
        count_kernel,
        in_specs=[smem(), vmem()],
        out_specs=vmem(),
        out_shape=jax.ShapeDtypeStruct((owners, events, cap), bf16),
        scratch_shapes=[pltpu.VMEM((2, owners * GROUP, cap), f32)],
        compiler_params=params(),
        name="slot_counts",
    )(starts, behave)


def place_bits():
    return [(axis, b) for axis in AXES for b in range(lax.axis_size(axis).bit_length() - 1)]


def bit_value(bit):
    return lax.rem(lax.div(lax.axis_index(bit[0]), 1 << bit[1]), 2)


def across(bit):
    axis, b = bit
    place = {a: lax.axis_index(a) for a in AXES}
    place[axis] = place[axis] + (1 - 2 * bit_value(bit)) * (1 << b)
    return tuple(place[a] for a in AXES)


class Piece:
    def __init__(self, part, inbox, own, total, order, own_sem, sends, recvs):
        self.part, self.inbox, self.own, self.total = part, inbox, own, total
        self.order, self.own_sem, self.sends, self.recvs = order, own_sem, sends, recvs
        self.rows = part.shape[0]
        self.grain = self.rows >> len(order)
        self.offsets, self.copies, self.taken = [0], [], 0

    def at(self, ref, offset, n):
        return ref.at[pl.ds(pl.multiple_of(offset, self.grain), n)]

    def keep(self):
        return pltpu.make_async_copy(self.own, self.at(self.total, self.offsets[-1], self.grain), self.own_sem)

    def send(self):
        k, depth = len(self.copies), len(self.order)
        if k < depth:
            bit, half = self.order[k], self.rows >> (k + 1)
            value, offset = bit_value(bit), self.offsets[k]
            self.offsets.append(offset + value * half)
            source = self.at(self.part, offset + (1 - value) * half, half)
            target = self.inbox.at[pl.ds(self.rows - (self.rows >> k), half)]
        else:
            s = 2 * depth - 1 - k
            bit = self.order[s]
            target = self.at(self.total, self.offsets[s + 1], self.rows >> (s + 1))
            source = self.own if k == depth else target
        copy = pltpu.make_async_remote_copy(
            src_ref=source,
            dst_ref=target,
            send_sem=self.sends.at[k],
            recv_sem=self.recvs.at[k],
            device_id=across(bit),
            device_id_type=MESH,
        )
        copy.start()
        self.copies.append(copy)

    def done(self):
        return self.taken == 2 * len(self.order)

    def take(self):
        k, depth = self.taken, len(self.order)
        self.copies[k].wait_recv()
        self.taken += 1
        if k < depth:
            n, base, offset = self.rows >> (k + 1), self.rows - (self.rows >> k), self.offsets[k + 1]
            chunk = math.gcd(n, 64)

            def add(i, carry):
                at = pl.ds(pl.multiple_of(offset + i * chunk, math.gcd(self.grain, chunk)), chunk)
                came = pl.ds(pl.multiple_of(base + i * chunk, chunk), chunk)
                total = (self.part[at, :].astype(f32) + self.inbox[came, :].astype(f32)).astype(self.part.dtype)
                if k == depth - 1:
                    self.own[pl.ds(pl.multiple_of(i * chunk, chunk), chunk), :] = total
                else:
                    self.part[at, :] = total
                return carry

            lax.fori_loop(0, n // chunk, add, 0)
        if k == depth - 1:
            self.keep().start()
        if k == depth:
            self.keep().wait()
        if not self.done():
            self.send()

    def drain(self):
        for copy in self.copies:
            copy.wait_send()


def everyone_else():
    n_wide, n_narrow = (lax.axis_size(a) for a in AXES)
    w, n = (lax.axis_index(a) for a in AXES)
    me = w * n_narrow + n
    total = n_wide * n_narrow
    for d in range(1, total):
        other = lax.rem(me + d, total)
        yield d, other, (lax.div(other, n_narrow), lax.rem(other, n_narrow))


def greet_all():
    barrier = pltpu.get_barrier_semaphore()
    for _, _, place in everyone_else():
        pl.semaphore_signal(barrier, inc=1, device_id=place, device_id_type=MESH)


def wait_for_all():
    pl.semaphore_wait(pltpu.get_barrier_semaphore(), lax.axis_size("wide") * lax.axis_size("narrow") - 1)


def meet_all():
    greet_all()
    wait_for_all()


def lanes_of(rows, columns, devices):
    lanes = columns
    while lanes > 128 and (rows * (columns // lanes)) % (16 * devices):
        lanes //= 2
    return lanes


ORDERS = "BDADABGGBBBABGBAAA"


class Block:
    def __init__(self, rows, columns, devices):
        self.rows, self.columns = rows, columns
        self.lanes = lanes_of(rows, columns, devices)
        self.blocks = columns // self.lanes
        self.padded = -(-rows * self.blocks // (16 * devices)) * 16 * devices

    def put(self, piece, value):
        for c in range(self.blocks):
            piece[c * self.rows : (c + 1) * self.rows, :] = value[:, c * self.lanes : (c + 1) * self.lanes]
        extra = self.padded - self.rows * self.blocks
        if extra:
            piece[self.rows * self.blocks :, :] = jnp.zeros((extra, self.lanes), piece.dtype)

    def whole(self, total, n):
        return total[:, : self.rows * self.blocks].reshape(n, self.blocks, self.rows, self.lanes)


def orders():
    if tuple(lax.axis_size(a) for a in AXES) != (8, 4):
        return [place_bits()] * len(ORDERS)
    core, y, x, z0, z1 = ("narrow", 0), ("narrow", 1), ("wide", 0), ("wide", 1), ("wide", 2)
    ways = {
        "A": [core, x, y, z0, z1],
        "B": [core, y, x, z0, z1],
        "D": [core, z0, z1, y, x],
        "G": [core, z0, z1, x, y],
    }
    return [ways[way] for way in ORDERS]


def lookup_kernel(
    requests, table, live, field, counts, dense, domains,
    fields, pooled, line_out, group, stats_out,
    tab, lines, got, line, line_smem, found, rows, slots, stats, stats_in,
    tab_sems, line_sem, ask_sends, ask_recvs, row_sends, row_recvs, stat_sends, stat_recvs,
):
    owners, _, cap = requests.shape
    width = tab.shape[0]
    n_field, events = field.shape
    chunks = tab_sems.shape[0]
    part = tab.shape[1] // chunks
    batch = 4
    n_narrow = lax.axis_size("narrow")
    me = lax.axis_index("wide") * n_narrow + lax.axis_index("narrow")

    loads = []
    for c in range(chunks):
        at = pl.ds(c * part, part)
        loads.append(pltpu.make_async_copy(table.at[:, at], tab.at[:, at], tab_sems.at[c]))
        loads[-1].start()
    lane = lax.broadcasted_iota(i32, (width, 128), 1)
    mine = jnp.zeros((width, 128), f32)
    for d in range(DOMAINS):
        here = domains[...] == d
        value = jnp.where(here, dense[...], 0.0)
        one = jnp.broadcast_to(jnp.where(here, 1.0, 0.0), value.shape)
        for k, term in enumerate((value, value * value, one)):
            mine = jnp.where(lane == k * DOMAINS + d, jnp.sum(term, axis=1, keepdims=True), mine)
    stats[...] = mine

    meet_all()

    def peer(d):
        other = lax.rem(me + d, owners)
        return other, (lax.div(other, n_narrow), lax.rem(other, n_narrow))

    def ask(d):
        other, place = peer(d)
        return pltpu.make_async_remote_copy(
            src_ref=requests.at[other], dst_ref=line.at[me], send_sem=ask_sends.at[d],
            recv_sem=ask_recvs.at[d], device_id=place, device_id_type=MESH)

    def tell(d):
        _, place = peer(d)
        return pltpu.make_async_remote_copy(
            src_ref=stats, dst_ref=stats_in.at[me], send_sem=stat_sends.at[d],
            recv_sem=stat_recvs.at[d], device_id=place, device_id_type=MESH)

    def answer(d):
        other, place = peer(d)
        return pltpu.make_async_remote_copy(
            src_ref=found.at[other], dst_ref=rows.at[me], send_sem=row_sends.at[d],
            recv_sem=row_recvs.at[d], device_id=place, device_id_type=MESH)

    def each(first, act):
        def step(d, carry):
            act(d)
            return carry

        lax.fori_loop(first, owners, step, 0)

    each(1, lambda d: ask(d).start())
    each(1, lambda d: tell(d).start())
    line[me] = requests[me]
    stats_in[me] = stats[...]

    eye = identity(128)
    for c in range(chunks):
        loads[c].wait()

        def turn(i, carry):
            base = pl.multiple_of(c * part + i * ROW_CHUNK, ROW_CHUNK)
            stack = jnp.concatenate([tab[:, pl.ds(base + g * 128, 128)] for g in range(8)], axis=0)
            at = pl.multiple_of((c * part // ROW_CHUNK + i) * 128, 128)
            lines[pl.ds(at, 128), :] = lax.dot_general(eye, stack, NT, preferred_element_type=f32)
            return carry

        lax.fori_loop(0, part // ROW_CHUNK, turn, 0, unroll=8)

    each(1, lambda d: ask(d).wait_recv())
    group[...] = lane_group_of(line[...])
    line_out[...] = line_of(line[...])
    to_smem = pltpu.make_async_copy(line_out, line_smem, line_sem)
    to_smem.start()
    to_smem.wait()

    def serve(b, carry):
        sources = [lax.rem(me + b * batch + k, owners) for k in range(batch)]
        for k in range(batch):

            def fetch(u, carry):
                for i in range(64):
                    j = u * 64 + i
                    got[pl.ds(k * cap + j, 1), :] = lines[pl.ds(line_smem[sources[k], 0, j], 1), :]
                return carry

            lax.fori_loop(0, cap // 64, fetch, 0)
        turned = lax.dot_general(eye, got[...].astype(bf16), NT, preferred_element_type=f32)
        for k in range(batch):
            which = group[sources[k]]
            picked = turned[:width, k * cap : (k + 1) * cap]
            for g in range(1, 8):
                picked = jnp.where(which == g, turned[g * width : (g + 1) * width, k * cap : (k + 1) * cap], picked)
            found[sources[k]] = picked.astype(bf16)
        for k in range(batch):
            d = b * batch + k
            if k:
                answer(d).start()
            else:
                pl.when(b > 0)(lambda: answer(d).start())
        return carry

    lax.fori_loop(0, owners // batch, serve, 0)
    rows[me] = found[me]
    each(1, lambda d: tell(d).wait_recv())
    total = stats_in[0]
    for o in range(1, owners):
        total = total + stats_in[o]
    stats_out[...] = total

    each(1, lambda d: answer(d).wait_recv())
    shift = cap.bit_length() - 1
    column = lax.broadcasted_iota(i32, (width, cap), 1)
    for o in range(owners):
        slots[o * width : (o + 1) * width, :] = jnp.where(column < live[o], rows[o].astype(f32), 0.0).astype(bf16)

    def one(f, carry):
        slot = field[pl.ds(f, 1), :]
        owner = jnp.right_shift(slot, shift)
        all_owners = jnp.dot(slots[...], hot(cap, jnp.bitwise_and(slot, cap - 1)), preferred_element_type=f32)
        picked = all_owners[:width]
        for o in range(1, owners):
            picked = jnp.where(owner == o, all_owners[o * width : (o + 1) * width], picked)
        fields[pl.ds(pl.multiple_of(f * width, width), width), :] = picked.astype(bf16)
        return carry

    lax.fori_loop(0, n_field, one, 0, unroll=2)
    total = jnp.zeros((events, width), f32)
    for o in range(owners):
        total = total + lax.dot_general(counts[o], slots[o * width : (o + 1) * width, :], NT, preferred_element_type=f32)
    pooled[...] = total.T
    each(1, lambda d: ask(d).wait_send())
    each(1, lambda d: tell(d).wait_send())
    each(1, lambda d: answer(d).wait_send())


def lookup(requests, table_t, live, field_t, counts, dense_t, domains):
    owners, _, cap = requests.shape
    width, rows = table_t.shape
    n_field, events = field_t.shape
    chunks = 6
    dma = pltpu.SemaphoreType.DMA
    return pl.pallas_call(
        lookup_kernel,
        in_specs=[vmem(), hbm(), smem(), vmem(), vmem(), vmem(), vmem()],
        out_specs=[vmem()] * 5,
        out_shape=[
            jax.ShapeDtypeStruct((n_field * width, events), bf16),
            jax.ShapeDtypeStruct((width, events), f32),
            jax.ShapeDtypeStruct((owners, 1, cap), i32),
            jax.ShapeDtypeStruct((owners, 1, cap), i32),
            jax.ShapeDtypeStruct((width, 128), f32),
        ],
        scratch_shapes=[
            pltpu.VMEM((width, rows), bf16),
            pltpu.VMEM((rows // 8, 128), f32),
            pltpu.VMEM((4 * cap, 128), f32),
            pltpu.VMEM((owners, 1, cap), i32),
            pltpu.SMEM((owners, 1, cap), i32),
            pltpu.VMEM((owners, width, cap), bf16),
            pltpu.VMEM((owners, width, cap), bf16),
            pltpu.VMEM((owners * width, cap), bf16),
            pltpu.VMEM((width, 128), f32),
            pltpu.VMEM((owners, width, 128), f32),
            dma((chunks,)),
            dma,
        ]
        + [dma((owners,))] * 6,
        compiler_params=params(collective_id=1, has_side_effects=True),
        name="lookup",
    )(requests, table_t, live, field_t, counts, dense_t, domains)


STRIPE = 64
GATE_ROWS = 16
GELU_SCALE = math.sqrt(2.0 / math.pi)
GELU_CUBE = 0.044715


def gelu_and_slope(x):
    square = x * x
    t = jnp.tanh(GELU_SCALE * (x + GELU_CUBE * (square * x)))
    half = 0.5 * (1.0 + t)
    return x * half, half + 0.5 * x * (1.0 - t * t) * (GELU_SCALE * (1.0 + 3.0 * GELU_CUBE * square))


def standardise(values):
    center = values - jnp.mean(values, axis=-1, keepdims=True)
    inverse = lax.rsqrt(jnp.mean(center * center, axis=-1, keepdims=True) + EPSILON)
    return center * inverse, inverse


def standardise_back(d, standard, inverse):
    along = jnp.mean(d * standard, axis=-1, keepdims=True)
    return inverse * (d - jnp.mean(d, axis=-1, keepdims=True) - standard * along)


def loop(n, body):
    def step(i, carry):
        body(i)
        return carry

    lax.fori_loop(0, n, step, 0)


def columns(rows):
    have = rows.shape[0]
    if have < 8:
        rows = jnp.concatenate([rows, jnp.zeros((8 - have, rows.shape[1]), f32)], axis=0)
    return rows.T


def thirds(x):
    high = x.astype(bf16)
    rest = x - high.astype(f32)
    middle = rest.astype(bf16)
    return jnp.concatenate([high, middle, (rest - middle.astype(f32)).astype(bf16)], axis=0)


def domain_moments(stats):
    result = []
    for d in range(DOMAINS):
        count = stats[:, 2 * DOMAINS + d : 2 * DOMAINS + d + 1]
        mean = stats[:, d : d + 1] / count
        variance = stats[:, DOMAINS + d : DOMAINS + d + 1] / count - mean * mean
        result.append((mean, lax.rsqrt(variance + EPSILON), count))
    return result


def by_domain(domains, values):
    picked = values[0]
    for d in range(1, DOMAINS):
        picked = jnp.where(domains == d, values[d], picked)
    return picked


class Rows:
    def __init__(self, experts, units, depth, tower, width):
        self.next = 0
        lines = lambda n: -(-n // 128)
        self.b_in = [self.take(lines(units)) for _ in range(experts)]
        self.b_out, self.gain, self.bias = ([self.take(lines(depth)) for _ in range(experts)] for _ in range(3))
        self.proj_b, self.inter_gain, self.inter_bias = (self.take(lines(depth)) for _ in range(3))
        self.gates = [self.take(lines(depth)) for _ in range(SHARED + 2 * DOMAINS)]
        self.tower_in_bias, self.tower_out = ([self.take(lines(tower)) for _ in range(DOMAINS)] for _ in range(2))
        self.tower_out_bias = self.take(1)
        self.dense = self.take(width)

    def take(self, n):
        at, self.next = self.next, self.next + n
        return at

    def padded(self, devices):
        return -(-self.next // (8 * devices)) * 8 * devices


def put_row(small, at, row):
    for c in range(row.shape[1] // 128):
        small[at + c : at + c + 1, :] = row[:, c * 128 : (c + 1) * 128]


def learn_kernel(
    shape, blocks,
    fields, pooled, lengths, dense, domains, cotangent, stats, proj_w, proj_b, inter_gain, inter_bias,
    w_in_hbm, b_in, w_out_hbm, b_out, expert_gain, expert_bias, gates, tower_in, tower_in_bias, tower_out,
    tower_out_bias, field, counts_hbm,
    pred, centered, d_centered, returned, small_total, total_in, total_out, total_tower, total_proj,
    w_in, w_out, joined, joined_rows, pre_slope, pre_standard, pre_inverse, state_low, state_turned, coef,
    active, slope, standard, inverse, work, after, after_low, after_turned, d_tower, d_after, d_state, products,
    d_out, d_in, d_fields, d_pooled, counts, slot_total, slot_grad,
    small_part, small_inbox, part_in, part_out, part_tower, part_proj, inbox_in, inbox_out, inbox_tower, inbox_proj,
    small_own, own_in, own_out, own_tower, own_proj, in_sems, out_sems, count_sems, own_sems, sends, recvs, slot_sends, slot_recvs,
):
    experts, depth, units = w_in.shape
    width, events = dense.shape
    n_field = field.shape[0]
    owners, _, cap = slot_grad.shape
    tower_units = tower_in.shape[2]
    greet_all()
    for x in range(experts):
        pltpu.make_async_copy(w_in_hbm.at[x], w_in.at[x], in_sems.at[x]).start()
        pltpu.make_async_copy(w_out_hbm.at[x], w_out.at[x], out_sems.at[x]).start()

    which = domains[...]
    moments = domain_moments(stats[...])
    mean, scale = (by_domain(which, [m[i] for m in moments]) for i in range(2))
    centered[...] = (dense[...] - mean) * scale
    joined[: n_field * width, :] = fields[...]
    joined[n_field * width : (n_field + 1) * width, :] = (pooled[...] / lengths[...]).astype(bf16)
    joined[(n_field + 1) * width :, :] = centered[...].astype(bf16)
    joined_rows[...] = joined[...].T
    quarter = 256

    def project(c):
        at = pl.ds(pl.multiple_of(c * quarter, quarter), quarter)
        work[:, at] = jnp.dot(joined_rows[...], proj_w[:, at], preferred_element_type=f32) + proj_b[:, at]

    loop(depth // quarter, project)

    def stripe(i):
        return pl.ds(pl.multiple_of(i * STRIPE, STRIPE), STRIPE)

    def start_state(i):
        at = stripe(i)
        value, pre_slope[at, :] = gelu_and_slope(work[at, :])
        pre_standard[at, :], pre_inverse[at, :] = standardise(value)
        state = pre_standard[at, :] * inter_gain[...] + inter_bias[...]
        after[at, :] = state
        state_low[at, :] = state.astype(bf16)

    loop(events // STRIPE, start_state)
    state_turned[...] = state_low[...].T
    logits = lax.dot_general(gates[...], state_low[...], NT, preferred_element_type=f32)

    def softmax_pair(a, b):
        top = jnp.maximum(a, b)
        a, b = jnp.exp(a - top), jnp.exp(b - top)
        return a / (a + b), b / (a + b)

    share = softmax_pair(logits[0:1], logits[1:2])
    group_logits = [
        by_domain(which, [logits[SHARED + 2 * d + i : SHARED + 2 * d + i + 1] for d in range(DOMAINS)]) for i in range(2)
    ]
    level = softmax_pair(*group_logits)
    here = [jnp.where(which == d, 1.0, 0.0) for d in range(DOMAINS)]
    weights = [level[0] * share[0], level[0] * share[1]] + [level[1] * here[d] for d in range(DOMAINS)]
    weight_columns = columns(jnp.concatenate(weights, axis=0))
    coef[...] = weight_columns

    def expert_forward(x):
        pltpu.make_async_copy(w_in_hbm.at[x], w_in.at[x], in_sems.at[x]).wait()

        def enter(c):
            at = pl.ds(pl.multiple_of(c * quarter, quarter), quarter)
            pre = jnp.dot(state_low[...], w_in[x, :, at], preferred_element_type=f32) + b_in[x, :, at]
            value, rise = gelu_and_slope(pre)
            active[x, :, at] = value.astype(bf16)
            slope[x, :, at] = rise.astype(bf16)

        loop(units // quarter, enter)
        pltpu.make_async_copy(w_out_hbm.at[x], w_out.at[x], out_sems.at[x]).wait()

        def leave(c):
            at = pl.ds(pl.multiple_of(c * quarter, quarter), quarter)
            work[:, at] = jnp.dot(active[x], w_out[x, :, at], preferred_element_type=f32) + b_out[x, :, at]

        loop(depth // quarter, leave)

        def mix(i):
            at = stripe(i)
            value, inverse[at, x : x + 1] = standardise(work[at, :])
            standard[x, at, :] = value.astype(bf16)
            after[at, :] += coef[at, x : x + 1] * (value * expert_gain[x] + expert_bias[x])

        loop(events // STRIPE, mix)

    for x in range(experts):
        expert_forward(x)
    after_low[...] = after[...].astype(bf16)
    after_turned[...] = after_low[...].T

    here_columns = columns(jnp.concatenate(here + [cotangent[...]], axis=0))
    logit = jnp.zeros((events, 1), f32)
    for d in range(DOMAINS):
        pre = jnp.dot(after_low[...], tower_in[d], preferred_element_type=f32) + tower_in_bias[d : d + 1, :]
        value, rise = gelu_and_slope(pre)
        work[:, d * tower_units : (d + 1) * tower_units] = value
        d_after[:, d * tower_units : (d + 1) * tower_units] = rise
        head = jnp.sum(value * tower_out[d : d + 1, :], axis=1, keepdims=True) + tower_out_bias[:, d : d + 1]
        logit = logit + here_columns[:, d : d + 1] * head
    chance = 1.0 / (1.0 + jnp.exp(-logit))
    d_logit = here_columns[:, DOMAINS : DOMAINS + 1] * chance * (1.0 - chance)
    pred[...] = jnp.broadcast_to(chance, (events, 8)).T[0:1, :]
    lane = lax.broadcasted_iota(i32, (1, 128), 1)
    bias_row = jnp.zeros((1, 128), f32)
    for d in range(DOMAINS):
        at = slice(d * tower_units, (d + 1) * tower_units)
        mine = d_logit * here_columns[:, d : d + 1]
        put_row(small_part, shape.tower_out[d], jnp.sum(mine * work[:, at], axis=0, keepdims=True))
        bias_row = jnp.where(lane == d, jnp.sum(mine, axis=0, keepdims=True), bias_row)
        low = (mine * tower_out[d : d + 1, :] * d_after[:, at]).astype(bf16)
        d_tower[d] = low
        put_row(small_part, shape.tower_in_bias[d], jnp.sum(low.astype(f32), axis=0, keepdims=True))
    small_part[shape.tower_out_bias : shape.tower_out_bias + 1, :] = bias_row

    wait_for_all()
    ways = orders()
    pieces = []

    def send(block, parts, inboxes, owns, totals, i, value):
        k = len(pieces)
        block.put(parts.at[i], value)
        piece = Piece(
            parts.at[i], inboxes.at[i], owns.at[i], totals.at[i], ways[k], own_sems.at[k], sends.at[k], recvs.at[k]
        )
        piece.send()
        pieces.append(piece)

    towers = [jnp.dot(after_turned[...], d_tower[d], preferred_element_type=f32).astype(bf16) for d in range(DOMAINS)]
    send(blocks[2], part_tower, inbox_tower, own_tower, total_tower, 0, jnp.concatenate(towers, axis=0))
    d_after[...] = sum(
        lax.dot_general(d_tower[d], tower_in[d], NT, preferred_element_type=f32) for d in range(DOMAINS)
    )
    d_state[...] = d_after[...]

    products[...] = jnp.zeros(products.shape, f32)
    zero = jnp.zeros((1, depth), f32)
    half = units // 2
    for x in range(experts):

        def unmix(i, sums):
            at = stripe(i)
            d, value = d_after[at, :], standard[x, at, :].astype(f32)
            products[at, x : x + 1] = jnp.sum(d * (value * expert_gain[x] + expert_bias[x]), axis=1, keepdims=True)
            d = coef[at, x : x + 1] * d
            low = standardise_back(d * expert_gain[x], value, inverse[at, x : x + 1]).astype(bf16)
            d_out[at, :] = low
            terms = (d * value, d, low.astype(f32))
            return tuple(s + jnp.sum(t, axis=0, keepdims=True) for s, t in zip(sums, terms))

        for place, row in zip((shape.gain[x], shape.bias[x], shape.b_out[x]),
                              lax.fori_loop(0, events // STRIPE, unmix, (zero,) * 3)):
            put_row(small_part, place, row)
        older = list(pieces)
        for h in range(2):
            value = lax.dot_general(active[x, :, h * half : (h + 1) * half], d_out[...], TN, preferred_element_type=f32)
            send(blocks[1], part_out, inbox_out, own_out, total_out, 2 * x + h, value.astype(bf16))

        def unenter(c):
            at = pl.ds(pl.multiple_of(c * quarter, quarter), quarter)
            d = lax.dot_general(d_out[...], w_out[x, at, :], NT, preferred_element_type=f32)
            low = (d * slope[x, :, at].astype(f32)).astype(bf16)
            d_in[:, at] = low
            row = jnp.sum(low.astype(f32), axis=0, keepdims=True)
            for q in range(quarter // 128):
                small_part[pl.ds(shape.b_in[x] + c * (quarter // 128) + q, 1), :] = row[:, q * 128 : (q + 1) * 128]

        loop(units // quarter, unenter)
        for h in range(2):
            value = jnp.dot(state_turned[...], d_in[:, h * half : (h + 1) * half], preferred_element_type=f32)
            send(blocks[0], part_in, inbox_in, own_in, total_in, 2 * x + h, value.astype(bf16))

        def unstate(c):
            at = pl.ds(pl.multiple_of(c * quarter, quarter), quarter)
            d_state[:, at] += lax.dot_general(d_in[...], w_in[x, at, :], NT, preferred_element_type=f32)

        loop(depth // quarter, unstate)
        for piece in older:
            piece.take()

    q = products[...].T
    q = [q[x : x + 1] for x in range(experts)]
    d_level = (share[0] * q[0] + share[1] * q[1], by_domain(which, q[SHARED:]))
    mean_share = share[0] * q[0] + share[1] * q[1]
    d_share = [level[0] * share[s] * (q[s] - mean_share) for s in range(SHARED)]
    mean_level = level[0] * d_level[0] + level[1] * d_level[1]
    d_group = [level[i] * (d_level[i] - mean_level) for i in range(2)]
    rows = d_share + [d_group[i] * here[d] for d in range(DOMAINS) for i in range(2)]
    d_logits = jnp.concatenate(rows + [jnp.zeros((GATE_ROWS - len(rows), events), f32)], axis=0)
    split = thirds(d_logits)
    gate_sums = jnp.dot(split, state_low[...], preferred_element_type=f32)
    gate_sums = sum(gate_sums[i * GATE_ROWS : (i + 1) * GATE_ROWS] for i in range(3))
    for i, place in enumerate(shape.gates):
        put_row(small_part, place, gate_sums[i : i + 1])
    gates_thrice = jnp.concatenate([gates[...]] * 3, axis=0)
    d_state[...] += lax.dot_general(split, gates_thrice, TN, preferred_element_type=f32)

    def unstart(i, sums):
        at = stripe(i)
        d, value = d_state[at, :], pre_standard[at, :]
        low = (standardise_back(d * inter_gain[...], value, pre_inverse[at, :]) * pre_slope[at, :]).astype(bf16)
        d_out[at, :] = low
        terms = (d * value, d, low.astype(f32))
        return tuple(s + jnp.sum(t, axis=0, keepdims=True) for s, t in zip(sums, terms))

    for place, row in zip((shape.inter_gain, shape.inter_bias, shape.proj_b),
                          lax.fori_loop(0, events // STRIPE, unstart, (zero,) * 3)):
        put_row(small_part, place, row)
    value = jnp.dot(joined[...], d_out[...], preferred_element_type=f32)
    send(blocks[3], part_proj, inbox_proj, own_proj, total_proj, 0, value.astype(bf16))
    ahead = counts.shape[0]

    def fetch(o):
        slot = o % ahead if isinstance(o, int) else lax.rem(o, ahead)
        return pltpu.make_async_copy(counts_hbm.at[o], counts.at[slot], count_sems.at[slot])

    for o in range(ahead):
        fetch(o).start()
    n_all = n_field * width
    d_fields[...] = lax.dot_general(proj_w[:n_all, :], d_out[...], NT, preferred_element_type=f32).astype(bf16)
    tail = lax.dot_general(proj_w[n_all:, :], d_out[...], NT, preferred_element_type=f32)
    d_pooled[...] = (tail[:width] / lengths[...]).astype(bf16)
    d_centered[...] = tail[width:]
    lanes = lax.broadcasted_iota(i32, (width, 128), 1)
    sums = jnp.zeros((width, 128), f32)
    for d in range(DOMAINS):
        mine = jnp.where(which == d, tail[width:], 0.0)
        for k, term in enumerate((mine, mine * centered[...])):
            sums = jnp.where(lanes == k * DOMAINS + d, jnp.sum(term, axis=1, keepdims=True), sums)
    small_part[shape.dense : shape.dense + width, :] = sums
    if small_part.shape[0] > shape.next:
        small_part[shape.next :, :] = jnp.zeros((small_part.shape[0] - shape.next, 128), f32)
    k = len(pieces)
    small_piece = Piece(
        small_part, small_inbox, small_own, small_total, ways[0], own_sems.at[k], sends.at[k], recvs.at[k]
    )
    small_piece.send()
    for piece in pieces:
        piece.take()
    pieces.append(small_piece)

    shift = cap.bit_length() - 1
    slot_total[...] = jnp.zeros(slot_total.shape, f32)

    def scatter(f, carry):
        slot = field[pl.ds(f, 1), :]
        owner = jnp.right_shift(slot, shift)
        d = d_fields[pl.ds(pl.multiple_of(f * width, width), width), :].astype(f32)
        wide = jnp.concatenate([jnp.where(owner == o, d, 0.0).astype(bf16) for o in range(owners)], axis=0)
        slot_total[...] += lax.dot_general(
            wide, hot(cap, jnp.bitwise_and(slot, cap - 1)), NT, preferred_element_type=f32
        )
        return carry

    def scatter_some(first, last):
        lax.fori_loop(first, last, scatter, 0)

    middle = n_field // 2
    scatter_some(0, middle)
    for piece in pieces:
        piece.take()
    scatter_some(middle, n_field)

    def spread(o):
        fetch(o).wait()
        behave = jnp.dot(d_pooled[...], counts[lax.rem(o, ahead)], preferred_element_type=f32)
        at = pl.ds(pl.multiple_of(o * width, width), width)
        slot_grad[o] = (slot_total[at, :] + behave).astype(bf16)
        pl.when(o + ahead < owners)(lambda: fetch(o + ahead).start())

    loop(owners, spread)
    me = lax.axis_index("wide") * lax.axis_size("narrow") + lax.axis_index("narrow")
    slot_copies = []
    for d, other, place in everyone_else():
        copy = pltpu.make_async_remote_copy(
            src_ref=slot_grad.at[other], dst_ref=returned.at[me], send_sem=slot_sends.at[d],
            recv_sem=slot_recvs.at[d], device_id=place, device_id_type=MESH)
        copy.start()
        slot_copies.append(copy)
    returned[me] = slot_grad[me]

    while any(not piece.done() for piece in pieces):
        for piece in pieces:
            if not piece.done():
                piece.take()
    for copy in slot_copies:
        copy.wait_recv()
    for copy in slot_copies:
        copy.wait_send()
    for piece in pieces:
        piece.drain()


def learn(fields, pooled, lengths, dense, domains, cotangent, stats, model, field, counts, devices):
    w_in, tower_in, proj_w = model[4], model[11], model[0]
    experts, depth, units = w_in.shape
    width, events = dense.shape
    owners, _, cap = counts.shape
    tower_units = tower_in.shape[2]
    half = units // 2
    shape = Rows(experts, units, depth, tower_units, width)
    n_small = shape.padded(devices)
    blocks = [
        Block(depth, half, devices), Block(half, depth, devices),
        Block(DOMAINS * depth, tower_units, devices), Block(proj_w.shape[0], depth, devices),
    ]
    numbers = (2 * experts, 2 * experts, 1, 1)
    pieces = [(n, b.padded, b.lanes) for n, b in zip(numbers, blocks)]
    steps = 2 * (devices.bit_length() - 1)
    n_pieces = sum(numbers) + 1
    joined = proj_w.shape[0]
    space = lambda *s: pltpu.VMEM(s, f32)
    low = lambda *s: pltpu.VMEM(s, bf16)
    dma = lambda *s: pltpu.SemaphoreType.DMA(s)
    in_specs = [vmem()] * 24
    in_specs[11] = in_specs[13] = in_specs[23] = hbm()
    out = pl.pallas_call(
        functools.partial(learn_kernel, shape, blocks),
        in_specs=in_specs,
        out_specs=[vmem()] * 4 + [hbm()] * 5,
        out_shape=[
            jax.ShapeDtypeStruct((1, events), f32),
            jax.ShapeDtypeStruct((width, events), f32),
            jax.ShapeDtypeStruct((width, events), f32),
            jax.ShapeDtypeStruct((owners, width, cap), bf16),
            jax.ShapeDtypeStruct((n_small, 128), f32),
        ]
        + [jax.ShapeDtypeStruct(s, bf16) for s in pieces],
        scratch_shapes=[
            low(experts, depth, units), low(experts, units, depth), low(joined, events), low(events, joined),
            space(events, depth), space(events, depth), space(events, 1), low(events, depth),
            low(depth, events), space(events, 8), low(experts, events, units), low(experts, events, units),
            low(experts, events, depth), space(events, 8), space(events, depth), space(events, depth),
            low(events, depth), low(depth, events), low(DOMAINS, events, tower_units), space(events, depth),
            space(events, depth), space(events, 8), low(events, depth), low(events, units),
            low(joined - 2 * width, events), low(width, events), low(4, events, cap), space(owners * width, cap),
            low(owners, width, cap), space(n_small, 128), space(n_small, 128),
        ]
        + [pltpu.VMEM(s, bf16) for s in pieces] * 2
        + [space(n_small // devices, 128)]
        + [low(n, rows // devices, lanes) for n, rows, lanes in pieces]
        + [dma(experts), dma(experts), dma(4), dma(n_pieces), dma(n_pieces, steps), dma(n_pieces, steps), dma(devices), dma(devices)],
        compiler_params=params(collective_id=0, has_side_effects=True),
        name="learn",
    )(fields, pooled, lengths, dense, domains, cotangent, stats, *model, field, counts)
    return out[:5], [b.whole(t, n) for b, t, n in zip(blocks, out[5:], numbers)], shape


def get_row(small, at, n):
    return jnp.concatenate([small[at + c : at + c + 1, :] for c in range(n // 128)], axis=1)


def finish_kernel(shape, line, line_v, group, returned, domains, stats, centered, d_centered, small, *refs):
    more, out, more_out = refs[:4], refs[4], refs[5:9]
    d_dense, b_in, b_out, gain, bias, proj_b, inter_gain, inter_bias, gates, tower_in_bias, tower_out, tower_bias = refs[9:21]
    lines, vals = refs[21:]
    step = pl.program_id(0)
    per = out.shape[1] // ROW_CHUNK

    @pl.when(step == 0)
    def _():
        for target, places in (
            (b_in, shape.b_in), (b_out, shape.b_out), (gain, shape.gain), (bias, shape.bias),
            (proj_b, [shape.proj_b]), (inter_gain, [shape.inter_gain]), (inter_bias, [shape.inter_bias]),
            (gates, shape.gates), (tower_in_bias, shape.tower_in_bias), (tower_out, shape.tower_out),
            (tower_bias, [shape.tower_out_bias]),
        ):
            for i, at in enumerate(places):
                target[i : i + 1, :] = get_row(small, at, target.shape[1])
        which = domains[...]
        sums = small[shape.dense : shape.dense + centered.shape[0], :]
        moments = domain_moments(stats[...])
        scale = by_domain(which, [m[1] for m in moments])
        straight = by_domain(which, [sums[:, d : d + 1] / m[2] for d, m in enumerate(moments)])
        cross = by_domain(which, [sums[:, DOMAINS + d : DOMAINS + d + 1] / m[2] for d, m in enumerate(moments)])
        d_dense[...] = scale * (d_centered[...] - straight - centered[...] * cross)

        blocks, _, cap = group.shape

        def clear(i, carry):
            lines[pl.ds(pl.multiple_of(i * 1024, 1024), 1024), :] = jnp.zeros((1024, 128), f32)
            return carry

        lax.fori_loop(0, lines.shape[0] // 1024, clear, 0)
        batch = 32
        a = lax.div(lax.broadcasted_iota(i32, (cap, cap), 0), batch)
        near = a == lax.div(lax.broadcasted_iota(i32, (cap, cap), 1), batch)

        def serve(s, carry):
            which, own = group[s], returned[s].astype(f32)
            wide = jnp.concatenate([jnp.where(which == g, own, 0.0) for g in range(8)], axis=0)
            along = jnp.broadcast_to(line_v[s].astype(f32), (cap, cap))
            same = jnp.where(jnp.logical_and(along == along.T, near), 1.0, 0.0).astype(bf16)
            vals[...] = lax.dot_general(same, wide.astype(bf16), NT, preferred_element_type=f32)

            def add(u, carry):
                places, sums = [], []
                for k in range(batch):
                    j = u * batch + k
                    places.append(line[s * cap + j])
                    sums.append(lines[pl.ds(places[-1], 1), :] + vals[pl.ds(j, 1), :])
                for place, total in zip(places, sums):
                    lines[pl.ds(place, 1), :] = total
                return carry

            lax.fori_loop(0, cap // batch, add, 0)
            return carry

        lax.fori_loop(0, blocks, serve, 0)

    def turn(c, carry):
        width = out.shape[0]
        turned = lines[pl.ds(pl.multiple_of((step * per + c) * 128, 128), 128), :].T
        for g in range(8):
            at = pl.multiple_of(c * ROW_CHUNK + g * 128, 128)
            out[:, pl.ds(at, 128)] = turned[g * width : (g + 1) * width]
        return carry

    lax.fori_loop(0, per, turn, 0, unroll=4)
    for source, target in zip(more, more_out):
        tall, blocks, rows, lanes = source.shape
        for s in range(tall):
            for c in range(blocks):
                target[s * rows : (s + 1) * rows, c * lanes : (c + 1) * lanes] = source[s, c].astype(f32)


def finish(shape, line, group, returned, domains, stats, centered, d_centered, small, more, rows):
    blocks, width, cap = returned.shape
    events = centered.shape[1]
    experts, units, depth = len(shape.b_in), more[0].shape[1] * more[0].shape[3], more[0].shape[2]
    tower = more[2].shape[1] * more[2].shape[3]
    steps = 4
    in_more, out_more, shapes = [], [], []
    for x in more:
        tall, parts, r, lanes = x.shape
        if tall > 1:
            in_more.append(pl.BlockSpec((tall // steps, parts, r, lanes), lambda i: (i, 0, 0, 0)))
        else:
            in_more.append(pl.BlockSpec((1, parts, r // steps, lanes), lambda i: (0, 0, i, 0)))
        out_more.append(pl.BlockSpec((tall * r // steps, parts * lanes), lambda i: (i, 0)))
        shapes.append((tall * r, parts * lanes))
    shapes += [(width, events), (experts, units)] + [(experts, depth)] * 3 + [(1, depth)] * 3
    shapes += [(len(shape.gates), depth), (DOMAINS, tower), (DOMAINS, tower), (1, 128)]
    return pl.pallas_call(
        functools.partial(finish_kernel, shape),
        grid=(steps,),
        in_specs=[smem()] + [vmem()] * 8 + in_more,
        out_specs=[pl.BlockSpec((width, rows // steps), lambda i: (0, i))] + out_more + [vmem()] * 12,
        out_shape=[jax.ShapeDtypeStruct(s, f32) for s in [(width, rows)] + shapes],
        scratch_shapes=[pltpu.VMEM((rows // 8, 128), f32), pltpu.VMEM((cap, 128), f32)],
        compiler_params=params(),
        name="finish",
    )(line.reshape(-1), line, group, returned, domains, stats, centered, d_centered, small, *more)


def local(
    table,
    dense,
    domains,
    lengths,
    requests,
    counts,
    field_slots,
    behave_slots,
    proj_w,
    proj_b,
    inter_gain,
    inter_bias,
    w_in,
    b_in,
    w_out,
    b_out,
    expert_gain,
    expert_bias,
    shared_gate,
    group_gate,
    tower_in,
    tower_in_bias,
    tower_out,
    tower_out_bias,
    pred_cotangent,
):
    devices = lax.axis_size("wide") * lax.axis_size("narrow")
    capacity = requests.shape[2]
    experts, depth, units = w_in.shape
    starts = jnp.concatenate([jnp.zeros((1,), i32), jnp.cumsum(lengths.reshape(-1))])
    counts_of = slot_counts(starts, behave_slots.reshape(-1, 128), devices, capacity)
    field = field_slots.T
    dense_t, which = dense.T, domains[None]
    fields, pooled, line, group, stats = lookup(
        requests.reshape(devices, 1, capacity), table.T, counts.reshape(-1), field, counts_of, dense_t, which
    )
    gates = jnp.concatenate([shared_gate.T, group_gate.transpose(0, 2, 1).reshape(-1, depth)], axis=0)
    gates = jnp.pad(gates, ((0, GATE_ROWS - gates.shape[0]), (0, 0)))
    tall = lambda x: x.reshape(experts, 1, -1)
    model = (
        proj_w, proj_b[None], inter_gain[None], inter_bias[None], w_in, tall(b_in), w_out, tall(b_out),
        tall(expert_gain), tall(expert_bias), gates, tower_in, tower_in_bias, tower_out, tower_out_bias[None],
    )
    (pred, centered, d_centered, returned, small), totals, shape = learn(
        fields, pooled, lengths.astype(f32), dense_t, which, pred_cotangent[None], stats, model, field, counts_of, devices
    )
    totals[0] = totals[0].reshape(experts, -1, depth, totals[0].shape[3])
    out = finish(shape, line, group, returned, which, stats, centered, d_centered, small, totals, table.shape[0])
    d_table, d_w_in, d_w_out, d_tower_in, d_proj_w, d_dense, d_b_in, d_b_out, d_gain, d_bias = out[:10]
    d_proj_b, d_inter_gain, d_inter_bias, d_gates, d_tower_in_bias, d_tower_out, d_tower_bias = out[10:]
    return (
        pred[0],
        d_dense.T,
        d_table.T,
        d_proj_w,
        d_proj_b[0],
        d_inter_gain[0],
        d_inter_bias[0],
        d_w_in.reshape(w_in.shape),
        d_b_in,
        d_w_out.reshape(w_out.shape),
        d_b_out,
        d_gain,
        d_bias,
        d_gates[:SHARED].T,
        d_gates[SHARED:].reshape(DOMAINS, 2, depth).transpose(0, 2, 1),
        d_tower_in.reshape(tower_in.shape),
        d_tower_in_bias,
        d_tower_out,
        d_tower_bias[0, :DOMAINS],
    )


def solution(mesh):
    placed = (
        P(("wide", "narrow"), None),
        P(("wide", "narrow"), None),
        P(("wide", "narrow")),
        P(("wide", "narrow"), None),
        P(("wide", "narrow"), None, None),
        P(("wide", "narrow"), None),
        P(("wide", "narrow"), None),
        P(("wide", "narrow"), None),
        P(),
        P(),
        P(),
        P(),
        P(),
        P(),
        P(),
        P(),
        P(),
        P(),
        P(),
        P(),
        P(),
        P(),
        P(),
        P(),
        P(("wide", "narrow")),
    )
    return jax.shard_map(
        local,
        mesh=mesh,
        in_specs=placed,
        out_specs=(
            P(("wide", "narrow")),
            P(("wide", "narrow"), None),
            P(("wide", "narrow"), None),
            P(),
            P(),
            P(),
            P(),
            P(),
            P(),
            P(),
            P(),
            P(),
            P(),
            P(),
            P(),
            P(),
            P(),
            P(),
            P(),
        ),
        check_vma=False,
    )
```

```python
import functools
import math

import jax
import jax.numpy as jnp
from jax import lax
from jax.experimental import pallas as pl
from jax.experimental.pallas import tpu as pltpu
from jax.sharding import PartitionSpec as P

SHARED = 2
DOMAINS = 2

EPSILON = 1e-05

f32 = jnp.float32
bf16 = jnp.bfloat16
i32 = jnp.int32
MESH = pl.DeviceIdType.MESH
AXES = ("wide", "narrow")
NT = (((1,), (1,)), ((), ()))
TN = (((0,), (0,)), ((), ()))
VMEM_LIMIT = 60 * 1024 * 1024
ROW_CHUNK = 1024
GROUP = 8
SPAN = 6
BUNCH = 4
ADD_STEPS = 4


def vmem():
    return pl.BlockSpec(memory_space=pltpu.VMEM)


def smem():
    return pl.BlockSpec(memory_space=pltpu.SMEM)


def hbm():
    return pl.BlockSpec(memory_space=pl.ANY)


def params(**more):
    return pltpu.CompilerParams(vmem_limit_bytes=VMEM_LIMIT, **more)


def line_of(rows):
    return jnp.left_shift(jnp.right_shift(rows, 10), 7) + jnp.bitwise_and(rows, 127)


def lane_group_of(rows):
    return jnp.bitwise_and(jnp.right_shift(rows, 7), 7)


def identity(n):
    return (lax.broadcasted_iota(i32, (n, n), 0) == lax.broadcasted_iota(i32, (n, n), 1)).astype(bf16)


def hot(rows, index):
    column = lax.broadcasted_iota(i32, (rows, index.shape[1]), 0)
    return jnp.where(column == index, 1.0, 0.0).astype(bf16)


def count_kernel(lengths, behave, counts, sums, done):
    owners, _, cap = counts.shape
    shift = cap.bit_length() - 1
    step = pl.program_id(0)
    place = lax.broadcasted_iota(i32, (SPAN, 128), 0) * 128 + lax.broadcasted_iota(i32, (SPAN, 128), 1)
    last_block = behave.shape[0] - SPAN
    ends = [jnp.where(step == 0, 0, done[0])]
    for i in range(BUNCH * GROUP):
        ends.append(ends[-1] + lengths[0, step * (BUNCH * GROUP) + i])
    done[0] = ends[-1]

    def part(k, m):
        cuts = ends[k * GROUP : (k + 1) * GROUP + 1]
        begin = lax.div(cuts[0], 128) + m * SPAN
        b = jnp.minimum(begin, last_block)
        slot = behave[pl.ds(b, SPAN), :]
        p = place + b * 128
        event = jnp.zeros_like(p)
        for cut in cuts[1:-1]:
            event = event + jnp.where(p >= cut, 1, 0)
        mine = jnp.logical_and(jnp.logical_and(p >= cuts[0], p < cuts[-1]), p >= begin * 128)
        key = jnp.where(mine, jnp.right_shift(slot, shift) * GROUP + event, -1)
        low = jnp.bitwise_and(slot, cap - 1)
        left = jnp.concatenate([hot(owners * GROUP, key[q : q + 1]) for q in range(SPAN)], axis=1)
        right = jnp.concatenate([hot(cap, low[q : q + 1]) for q in range(SPAN)], axis=1)
        return lax.dot_general(left, right, NT, preferred_element_type=f32)

    parts = []
    for k in range(BUNCH):
        sums[k] = part(k, 0)
        first, last = ends[k * GROUP], ends[(k + 1) * GROUP]
        parts.append(lax.div(last - lax.div(first, 128) * 128 + (SPAN * 128 - 1), SPAN * 128))
    most = functools.reduce(jnp.maximum, parts)

    @pl.when(most > 1)
    def _():
        for k in range(BUNCH):

            def more(m, carry):
                sums[k] += part(k, m)
                return carry

            lax.fori_loop(1, parts[k], more, 0)

    for t in range(BUNCH // 2):
        for o in range(owners):
            both = [sums[2 * t + k, o * GROUP : (o + 1) * GROUP, :] for k in range(2)]
            counts[o, t * 2 * GROUP : (t + 1) * 2 * GROUP, :] = jnp.concatenate(both, axis=0).astype(bf16)


def slot_counts(lengths, behave, owners, cap):
    events = lengths.shape[1]
    size = BUNCH * GROUP
    return pl.pallas_call(
        count_kernel,
        grid=(events // size,),
        in_specs=[smem(), vmem()],
        out_specs=pl.BlockSpec((owners, size, cap), lambda i: (0, i, 0)),
        out_shape=jax.ShapeDtypeStruct((owners, events, cap), bf16),
        scratch_shapes=[pltpu.VMEM((BUNCH, owners * GROUP, cap), f32), pltpu.SMEM((1,), i32)],
        compiler_params=params(),
        name="slot_counts",
    )(lengths, behave)


def place_bits():
    return [(axis, b) for axis in AXES for b in range(lax.axis_size(axis).bit_length() - 1)]


def bit_value(bit):
    return lax.rem(lax.div(lax.axis_index(bit[0]), 1 << bit[1]), 2)


def across(bit):
    axis, b = bit
    place = {a: lax.axis_index(a) for a in AXES}
    place[axis] = place[axis] + (1 - 2 * bit_value(bit)) * (1 << b)
    return tuple(place[a] for a in AXES)


class Piece:
    def __init__(self, part, inbox, own, total, order, own_sem, sends, recvs):
        self.part, self.inbox, self.own, self.total = part, inbox, own, total
        self.order, self.own_sem, self.sends, self.recvs = order, own_sem, sends, recvs
        self.rows = part.shape[0]
        self.grain = self.rows >> len(order)
        self.offsets, self.copies, self.taken = [0], [], 0

    def at(self, ref, offset, n):
        return ref.at[pl.ds(pl.multiple_of(offset, self.grain), n)]

    def keep(self):
        return pltpu.make_async_copy(self.own, self.at(self.total, self.offsets[-1], self.grain), self.own_sem)

    def send(self):
        k, depth = len(self.copies), len(self.order)
        if k < depth:
            bit, half = self.order[k], self.rows >> (k + 1)
            value, offset = bit_value(bit), self.offsets[k]
            self.offsets.append(offset + value * half)
            source = self.at(self.part, offset + (1 - value) * half, half)
            target = self.inbox.at[pl.ds(self.rows - (self.rows >> k), half)]
        else:
            s = 2 * depth - 1 - k
            bit = self.order[s]
            target = self.at(self.total, self.offsets[s + 1], self.rows >> (s + 1))
            source = self.own if k == depth else target
        copy = pltpu.make_async_remote_copy(
            src_ref=source,
            dst_ref=target,
            send_sem=self.sends.at[k],
            recv_sem=self.recvs.at[k],
            device_id=across(bit),
            device_id_type=MESH,
        )
        copy.start()
        self.copies.append(copy)

    def done(self):
        return self.taken == 2 * len(self.order)

    def take(self):
        k, depth = self.taken, len(self.order)
        self.copies[k].wait_recv()
        self.taken += 1
        if k < depth:
            n, base, offset = self.rows >> (k + 1), self.rows - (self.rows >> k), self.offsets[k + 1]
            chunk = math.gcd(n, 64)

            def add(i, carry):
                at = pl.ds(pl.multiple_of(offset + i * chunk, math.gcd(self.grain, chunk)), chunk)
                came = pl.ds(pl.multiple_of(base + i * chunk, chunk), chunk)
                total = (self.part[at, :].astype(f32) + self.inbox[came, :].astype(f32)).astype(self.part.dtype)
                if k == depth - 1:
                    self.own[pl.ds(pl.multiple_of(i * chunk, chunk), chunk), :] = total
                else:
                    self.part[at, :] = total
                return carry

            lax.fori_loop(0, n // chunk, add, 0)
        if k == depth - 1:
            self.keep().start()
        if k == depth:
            self.keep().wait()
        if not self.done():
            self.send()

    def drain(self):
        for copy in self.copies:
            copy.wait_send()


def everyone_else():
    n_wide, n_narrow = (lax.axis_size(a) for a in AXES)
    w, n = (lax.axis_index(a) for a in AXES)
    me = w * n_narrow + n
    total = n_wide * n_narrow
    for d in range(1, total):
        other = lax.rem(me + d, total)
        yield d, other, (lax.div(other, n_narrow), lax.rem(other, n_narrow))


def greet_all():
    barrier = pltpu.get_barrier_semaphore()
    for _, _, place in everyone_else():
        pl.semaphore_signal(barrier, inc=1, device_id=place, device_id_type=MESH)


def wait_for_all():
    pl.semaphore_wait(pltpu.get_barrier_semaphore(), lax.axis_size("wide") * lax.axis_size("narrow") - 1)


def meet_all():
    greet_all()
    wait_for_all()


def lanes_of(rows, columns, devices):
    lanes = columns
    while lanes > 128 and (rows * (columns // lanes)) % (16 * devices):
        lanes //= 2
    return lanes


ORDERS = "BDADABGGBBBABGBAAA"


class Block:
    def __init__(self, rows, columns, devices):
        self.rows, self.columns = rows, columns
        self.lanes = lanes_of(rows, columns, devices)
        self.blocks = columns // self.lanes
        self.padded = -(-rows * self.blocks // (16 * devices)) * 16 * devices

    def put(self, piece, value):
        for c in range(self.blocks):
            piece[c * self.rows : (c + 1) * self.rows, :] = value[:, c * self.lanes : (c + 1) * self.lanes]
        extra = self.padded - self.rows * self.blocks
        if extra:
            piece[self.rows * self.blocks :, :] = jnp.zeros((extra, self.lanes), piece.dtype)

    def whole(self, total, n):
        return total[:, : self.rows * self.blocks].reshape(n, self.blocks, self.rows, self.lanes)


def orders():
    if tuple(lax.axis_size(a) for a in AXES) != (8, 4):
        return [place_bits()] * len(ORDERS)
    core, y, x, z0, z1 = ("narrow", 0), ("narrow", 1), ("wide", 0), ("wide", 1), ("wide", 2)
    ways = {
        "A": [core, x, y, z0, z1],
        "B": [core, y, x, z0, z1],
        "D": [core, z0, z1, y, x],
        "G": [core, z0, z1, x, y],
    }
    return [ways[way] for way in ORDERS]


def lookup_kernel(
    requests_in, table, live, field, counts_hbm, dense, domains,
    fields, pooled, line_out, group, stats_out,
    requests, counts, tab, lines, got, line, line_smem, found, rows, slots, stats, stats_in,
    tab_sems, counts_sem, line_sem, ask_sends, ask_recvs, row_sends, row_recvs, stat_sends, stat_recvs,
):
    owners, _, cap = requests.shape
    width = tab.shape[0]
    n_field, events = field.shape
    chunks = tab_sems.shape[0]
    part = tab.shape[1] // chunks
    n_narrow = lax.axis_size("narrow")
    me = lax.axis_index("wide") * n_narrow + lax.axis_index("narrow")

    loads = []
    for c in range(chunks):
        at = pl.ds(c * part, part)
        loads.append(pltpu.make_async_copy(table.at[:, at], tab.at[:, at], tab_sems.at[c]))
        loads[-1].start()
    load_counts = pltpu.make_async_copy(counts_hbm, counts, counts_sem)
    load_counts.start()
    for o in range(owners):
        requests[o] = requests_in[o : o + 1, :]
    lane = lax.broadcasted_iota(i32, (width, 128), 1)
    mine = jnp.zeros((width, 128), f32)
    for d in range(DOMAINS):
        here = domains[...] == d
        value = jnp.where(here, dense[...], 0.0)
        one = jnp.broadcast_to(jnp.where(here, 1.0, 0.0), value.shape)
        for k, term in enumerate((value, value * value, one)):
            mine = jnp.where(lane == k * DOMAINS + d, jnp.sum(term, axis=1, keepdims=True), mine)
    stats[...] = mine

    meet_all()

    def peer(d):
        other = lax.rem(me + d, owners)
        return other, (lax.div(other, n_narrow), lax.rem(other, n_narrow))

    def ask(d):
        other, place = peer(d)
        return pltpu.make_async_remote_copy(
            src_ref=requests.at[other], dst_ref=line.at[me], send_sem=ask_sends.at[d],
            recv_sem=ask_recvs.at[d], device_id=place, device_id_type=MESH)

    def tell(d):
        _, place = peer(d)
        return pltpu.make_async_remote_copy(
            src_ref=stats, dst_ref=stats_in.at[me], send_sem=stat_sends.at[d],
            recv_sem=stat_recvs.at[d], device_id=place, device_id_type=MESH)

    def answer(d):
        other, place = peer(d)
        return pltpu.make_async_remote_copy(
            src_ref=found.at[other], dst_ref=rows.at[me], send_sem=row_sends.at[d],
            recv_sem=row_recvs.at[d], device_id=place, device_id_type=MESH)

    def each(first, act):
        def step(d, carry):
            act(d)
            return carry

        lax.fori_loop(first, owners, step, 0)

    each(1, lambda d: ask(d).start())
    each(1, lambda d: tell(d).start())
    line[me] = requests[me]
    stats_in[me] = stats[...]

    eye = identity(128)
    for c in range(chunks):
        loads[c].wait()

        def turn(i, carry):
            base = pl.multiple_of(c * part + i * ROW_CHUNK, ROW_CHUNK)
            stack = jnp.concatenate([tab[:, pl.ds(base + g * 128, 128)] for g in range(8)], axis=0)
            at = pl.multiple_of((c * part // ROW_CHUNK + i) * 128, 128)
            lines[pl.ds(at, 128), :] = lax.dot_general(eye, stack, NT, preferred_element_type=f32)
            return carry

        lax.fori_loop(0, part // ROW_CHUNK, turn, 0, unroll=8)

    each(1, lambda d: ask(d).wait_recv())
    group[...] = lane_group_of(line[...])
    line_out[...] = line_of(line[...])
    to_smem = pltpu.make_async_copy(line_out, line_smem, line_sem)
    to_smem.start()
    to_smem.wait()

    def source(d):
        return lax.rem(me + d, owners)

    def fetch(d):
        s, half = source(d), lax.rem(d, 2) * cap
        for j in range(cap):
            got[pl.ds(half + j, 1), :] = lines[pl.ds(line_smem[s, 0, j], 1), :]

    def turn_out(d):
        s, half = source(d), pl.multiple_of(lax.rem(d, 2) * cap, cap)
        turned = lax.dot_general(eye, got[pl.ds(half, cap), :].astype(bf16), NT, preferred_element_type=f32)
        which = jnp.broadcast_to(group[s], (width, cap))
        picked = turned[:width]
        for g in range(1, 8):
            picked = jnp.where(which == g, turned[g * width : (g + 1) * width], picked)
        found[s] = picked.astype(bf16)

    fetch(0)

    def serve(d, carry):
        turn_out(d - 1)
        fetch(d)
        pl.when(d > 1)(lambda: answer(d - 1).start())
        return carry

    lax.fori_loop(1, owners, serve, 0)
    turn_out(owners - 1)
    answer(owners - 1).start()
    rows[me] = found[me]
    each(1, lambda d: tell(d).wait_recv())
    total = stats_in[0]
    for o in range(1, owners):
        total = total + stats_in[o]
    stats_out[...] = total

    each(1, lambda d: answer(d).wait_recv())
    shift = cap.bit_length() - 1
    column = lax.broadcasted_iota(i32, (width, cap), 1)
    for o in range(owners):
        slots[o * width : (o + 1) * width, :] = jnp.where(column < live[o], rows[o].astype(f32), 0.0).astype(bf16)

    def one(f, carry):
        slot = field[pl.ds(f, 1), :]
        owner = jnp.broadcast_to(jnp.right_shift(slot, shift), (width, events))
        all_owners = jnp.dot(slots[...], hot(cap, jnp.bitwise_and(slot, cap - 1)), preferred_element_type=f32)
        picked = all_owners[:width]
        for o in range(1, owners):
            picked = jnp.where(owner == o, all_owners[o * width : (o + 1) * width], picked)
        fields[pl.ds(pl.multiple_of(f * width, width), width), :] = picked.astype(bf16)
        return carry

    lax.fori_loop(0, n_field, one, 0, unroll=2)
    load_counts.wait()
    total = jnp.zeros((events, width), f32)
    for o in range(owners):
        total = total + lax.dot_general(counts[o], slots[o * width : (o + 1) * width, :], NT, preferred_element_type=f32)
    pooled[...] = total.T
    each(1, lambda d: ask(d).wait_send())
    each(1, lambda d: tell(d).wait_send())
    each(1, lambda d: answer(d).wait_send())


def lookup(requests, table_t, live, field_t, counts, dense_t, domains):
    owners, cap = requests.shape
    width, rows = table_t.shape
    n_field, events = field_t.shape
    chunks = 6
    dma = pltpu.SemaphoreType.DMA
    return pl.pallas_call(
        lookup_kernel,
        in_specs=[vmem(), hbm(), smem(), vmem(), hbm(), vmem(), vmem()],
        out_specs=[vmem()] * 5,
        out_shape=[
            jax.ShapeDtypeStruct((n_field * width, events), bf16),
            jax.ShapeDtypeStruct((width, events), f32),
            jax.ShapeDtypeStruct((owners, 1, cap), i32),
            jax.ShapeDtypeStruct((owners, 1, cap), i32),
            jax.ShapeDtypeStruct((width, 128), f32),
        ],
        scratch_shapes=[
            pltpu.VMEM((owners, 1, cap), i32),
            pltpu.VMEM((owners, events, cap), bf16),
            pltpu.VMEM((width, rows), bf16),
            pltpu.VMEM((rows // 8, 128), f32),
            pltpu.VMEM((2 * cap, 128), f32),
            pltpu.VMEM((owners, 1, cap), i32),
            pltpu.SMEM((owners, 1, cap), i32),
            pltpu.VMEM((owners, width, cap), bf16),
            pltpu.VMEM((owners, width, cap), bf16),
            pltpu.VMEM((owners * width, cap), bf16),
            pltpu.VMEM((width, 128), f32),
            pltpu.VMEM((owners, width, 128), f32),
            dma((chunks,)),
            dma,
            dma,
        ]
        + [dma((owners,))] * 6,
        compiler_params=params(collective_id=1, has_side_effects=True),
        name="lookup",
    )(requests, table_t, live, field_t, counts, dense_t, domains)


STRIPE = 64
GATE_ROWS = 16
GELU_SCALE = math.sqrt(2.0 / math.pi)
GELU_CUBE = 0.044715


def gelu_and_slope(x):
    square = x * x
    t = jnp.tanh(GELU_SCALE * (x + GELU_CUBE * (square * x)))
    half = 0.5 * (1.0 + t)
    return x * half, half + 0.5 * x * (1.0 - t * t) * (GELU_SCALE * (1.0 + 3.0 * GELU_CUBE * square))


def standardise(values):
    center = values - jnp.mean(values, axis=-1, keepdims=True)
    inverse = lax.rsqrt(jnp.mean(center * center, axis=-1, keepdims=True) + EPSILON)
    return center * inverse, inverse


def standardise_back(d, standard, inverse):
    along = jnp.mean(d * standard, axis=-1, keepdims=True)
    return inverse * (d - jnp.mean(d, axis=-1, keepdims=True) - standard * along)


def loop(n, body):
    def step(i, carry):
        body(i)
        return carry

    lax.fori_loop(0, n, step, 0)


def columns(rows):
    have = rows.shape[0]
    if have < 8:
        rows = jnp.concatenate([rows, jnp.zeros((8 - have, rows.shape[1]), f32)], axis=0)
    return rows.T


def thirds(x):
    high = x.astype(bf16)
    rest = x - high.astype(f32)
    middle = rest.astype(bf16)
    return jnp.concatenate([high, middle, (rest - middle.astype(f32)).astype(bf16)], axis=0)


def domain_moments(stats):
    result = []
    for d in range(DOMAINS):
        count = stats[:, 2 * DOMAINS + d : 2 * DOMAINS + d + 1]
        mean = stats[:, d : d + 1] / count
        variance = stats[:, DOMAINS + d : DOMAINS + d + 1] / count - mean * mean
        result.append((mean, lax.rsqrt(variance + EPSILON), count))
    return result


def by_domain(domains, values):
    picked = values[0]
    for d in range(1, DOMAINS):
        picked = jnp.where(domains == d, values[d], picked)
    return picked


class Rows:
    def __init__(self, experts, units, depth, tower, width):
        self.next = 0
        lines = lambda n: -(-n // 128)
        self.b_in = [self.take(lines(units)) for _ in range(experts)]
        self.b_out, self.gain, self.bias = ([self.take(lines(depth)) for _ in range(experts)] for _ in range(3))
        self.proj_b, self.inter_gain, self.inter_bias = (self.take(lines(depth)) for _ in range(3))
        self.gates = [self.take(lines(depth)) for _ in range(SHARED + 2 * DOMAINS)]
        self.tower_in_bias, self.tower_out = ([self.take(lines(tower)) for _ in range(DOMAINS)] for _ in range(2))
        self.tower_out_bias = self.take(1)
        self.dense = self.take(width)

    def take(self, n):
        at, self.next = self.next, self.next + n
        return at

    def padded(self, devices):
        return -(-self.next // (8 * devices)) * 8 * devices


def put_row(small, at, row):
    for c in range(row.shape[1] // 128):
        small[at + c : at + c + 1, :] = row[:, c * 128 : (c + 1) * 128]


def learn_kernel(
    shape, blocks,
    fields, pooled, lengths, dense, domains, cotangent, stats, proj_w, proj_b, inter_gain, inter_bias,
    w_in_hbm, b_in, w_out_hbm, b_out, expert_gain, expert_bias, shared_gate, group_gate, tower_in, tower_in_bias, tower_out,
    tower_out_bias, field, counts_hbm,
    pred, centered, d_centered, returned, small_total, total_in, total_out, total_tower, total_proj,
    w_in, w_out, joined, pre_slope, pre_standard, pre_inverse, state_low, state_turned, coef,
    active, slope, standard, inverse, work, after, after_low, after_turned, d_tower, d_after, products,
    d_out, d_in, d_pooled, gates, counts, slot_total, slot_grad,
    small_part, small_inbox, part_in, part_out, part_tower, part_proj, inbox_in, inbox_out, inbox_tower, inbox_proj,
    small_own, own_in, own_out, own_tower, own_proj, in_sems, out_sems, count_sems, own_sems, sends, recvs, slot_sends, slot_recvs,
):
    experts, depth, units = w_in.shape
    width, events = dense.shape
    n_field = field.shape[0]
    owners, _, cap = slot_grad.shape
    tower_units = tower_in.shape[2]
    greet_all()
    for x in range(experts):
        pltpu.make_async_copy(w_in_hbm.at[x], w_in.at[x], in_sems.at[x]).start()
        pltpu.make_async_copy(w_out_hbm.at[x], w_out.at[x], out_sems.at[x]).start()

    which = domains[...]
    length = lengths[...].astype(f32)
    rows = [shared_gate[...].astype(f32)] + [group_gate[d].astype(f32) for d in range(DOMAINS)]
    have = SHARED + 2 * DOMAINS
    gates[...] = jnp.concatenate(rows + [jnp.zeros((GATE_ROWS - have, depth), f32)], axis=0).astype(bf16)
    moments = domain_moments(stats[...])
    mean, scale = (by_domain(which, [m[i] for m in moments]) for i in range(2))
    centered[...] = (dense[...] - mean) * scale
    joined[: n_field * width, :] = fields[...]
    joined[n_field * width : (n_field + 1) * width, :] = (pooled[...] / length).astype(bf16)
    joined[(n_field + 1) * width :, :] = centered[...].astype(bf16)
    joined_rows, d_state, d_fields = d_in.at[:, : joined.shape[0]], after, joined
    joined_rows[...] = joined[...].T
    quarter = 256

    def project(c):
        at = pl.ds(pl.multiple_of(c * quarter, quarter), quarter)
        work[:, at] = jnp.dot(joined_rows[...], proj_w[:, at], preferred_element_type=f32) + proj_b[:, at]

    loop(depth // quarter, project)

    def stripe(i):
        return pl.ds(pl.multiple_of(i * STRIPE, STRIPE), STRIPE)

    def start_state(i):
        at = stripe(i)
        value, pre_slope[at, :] = gelu_and_slope(work[at, :])
        pre_standard[at, :], pre_inverse[at, :] = standardise(value)
        state = pre_standard[at, :] * inter_gain[...] + inter_bias[...]
        after[at, :] = state
        state_low[at, :] = state.astype(bf16)

    loop(events // STRIPE, start_state)
    state_turned[...] = state_low[...].T
    logits = lax.dot_general(gates[...], state_low[...], NT, preferred_element_type=f32)

    def softmax_pair(a, b):
        top = jnp.maximum(a, b)
        a, b = jnp.exp(a - top), jnp.exp(b - top)
        return a / (a + b), b / (a + b)

    share = softmax_pair(logits[0:1], logits[1:2])
    group_logits = [
        by_domain(which, [logits[SHARED + 2 * d + i : SHARED + 2 * d + i + 1] for d in range(DOMAINS)]) for i in range(2)
    ]
    level = softmax_pair(*group_logits)
    here = [jnp.where(which == d, 1.0, 0.0) for d in range(DOMAINS)]
    weights = [level[0] * share[0], level[0] * share[1]] + [level[1] * here[d] for d in range(DOMAINS)]
    weight_columns = columns(jnp.concatenate(weights, axis=0))
    coef[...] = weight_columns

    def expert_forward(x):
        pltpu.make_async_copy(w_in_hbm.at[x], w_in.at[x], in_sems.at[x]).wait()

        def enter(c):
            at = pl.ds(pl.multiple_of(c * quarter, quarter), quarter)
            pre = jnp.dot(state_low[...], w_in[x, :, at], preferred_element_type=f32) + b_in[x : x + 1, at]
            value, rise = gelu_and_slope(pre)
            active[x, :, at] = value.astype(bf16)
            slope[x, :, at] = rise.astype(bf16)

        loop(units // quarter, enter)
        pltpu.make_async_copy(w_out_hbm.at[x], w_out.at[x], out_sems.at[x]).wait()

        def leave(c):
            at = pl.ds(pl.multiple_of(c * quarter, quarter), quarter)
            work[:, at] = jnp.dot(active[x], w_out[x, :, at], preferred_element_type=f32) + b_out[x : x + 1, at]

        loop(depth // quarter, leave)

        def mix(i):
            at = stripe(i)
            value, inverse[at, x : x + 1] = standardise(work[at, :])
            standard[x, at, :] = value.astype(bf16)
            after[at, :] += coef[at, x : x + 1] * (value * expert_gain[x : x + 1, :] + expert_bias[x : x + 1, :])

        loop(events // STRIPE, mix)

    for x in range(experts):
        expert_forward(x)
    after_low[...] = after[...].astype(bf16)
    after_turned[...] = after_low[...].T

    here_columns = columns(jnp.concatenate(here + [cotangent[...]], axis=0))
    logit = jnp.zeros((events, 1), f32)
    for d in range(DOMAINS):
        pre = jnp.dot(after_low[...], tower_in[d], preferred_element_type=f32) + tower_in_bias[d : d + 1, :]
        value, rise = gelu_and_slope(pre)
        work[:, d * tower_units : (d + 1) * tower_units] = value
        d_after[:, d * tower_units : (d + 1) * tower_units] = rise
        head = jnp.sum(value * tower_out[d : d + 1, :], axis=1, keepdims=True) + tower_out_bias[:, d : d + 1]
        logit = logit + here_columns[:, d : d + 1] * head
    chance = 1.0 / (1.0 + jnp.exp(-logit))
    d_logit = here_columns[:, DOMAINS : DOMAINS + 1] * chance * (1.0 - chance)
    pred[...] = jnp.broadcast_to(chance, (events, 8)).T[0:1, :]
    lane = lax.broadcasted_iota(i32, (1, 128), 1)
    bias_row = jnp.zeros((1, 128), f32)
    for d in range(DOMAINS):
        at = slice(d * tower_units, (d + 1) * tower_units)
        mine = d_logit * here_columns[:, d : d + 1]
        put_row(small_part, shape.tower_out[d], jnp.sum(mine * work[:, at], axis=0, keepdims=True))
        bias_row = jnp.where(lane == d, jnp.sum(mine, axis=0, keepdims=True), bias_row)
        low = (mine * tower_out[d : d + 1, :] * d_after[:, at]).astype(bf16)
        d_tower[d] = low
        put_row(small_part, shape.tower_in_bias[d], jnp.sum(low.astype(f32), axis=0, keepdims=True))
    small_part[shape.tower_out_bias : shape.tower_out_bias + 1, :] = bias_row

    wait_for_all()
    ways = orders()
    pieces, clock = [], [0]

    def pump():
        for piece in pieces:
            if not piece.done() and piece.sent_at < clock[0]:
                piece.take()
                piece.sent_at = clock[0]
        clock[0] += 1

    def send(block, parts, inboxes, owns, totals, i, value):
        k = len(pieces)
        block.put(parts.at[i], value)
        piece = Piece(
            parts.at[i], inboxes.at[i], owns.at[i], totals.at[i], ways[k], own_sems.at[k], sends.at[k], recvs.at[k]
        )
        piece.send()
        piece.sent_at = clock[0]
        pieces.append(piece)

    towers = [jnp.dot(after_turned[...], d_tower[d], preferred_element_type=f32).astype(bf16) for d in range(DOMAINS)]
    send(blocks[2], part_tower, inbox_tower, own_tower, total_tower, 0, jnp.concatenate(towers, axis=0))
    d_after[...] = sum(
        lax.dot_general(d_tower[d], tower_in[d], NT, preferred_element_type=f32) for d in range(DOMAINS)
    )
    d_state[...] = d_after[...]

    products[...] = jnp.zeros(products.shape, f32)
    zero = jnp.zeros((1, depth), f32)
    half = units // 2
    for x in range(experts):

        def unmix(i, sums):
            at = stripe(i)
            d, value = d_after[at, :], standard[x, at, :].astype(f32)
            products[at, x : x + 1] = jnp.sum(d * (value * expert_gain[x : x + 1, :] + expert_bias[x : x + 1, :]), axis=1, keepdims=True)
            d = coef[at, x : x + 1] * d
            low = standardise_back(d * expert_gain[x : x + 1, :], value, inverse[at, x : x + 1]).astype(bf16)
            d_out[at, :] = low
            terms = (d * value, d, low.astype(f32))
            return tuple(s + jnp.sum(t, axis=0, keepdims=True) for s, t in zip(sums, terms))

        for place, row in zip((shape.gain[x], shape.bias[x], shape.b_out[x]),
                              lax.fori_loop(0, events // STRIPE, unmix, (zero,) * 3)):
            put_row(small_part, place, row)
        pump()
        for h in range(2):
            value = lax.dot_general(active[x, :, h * half : (h + 1) * half], d_out[...], TN, preferred_element_type=f32)
            send(blocks[1], part_out, inbox_out, own_out, total_out, 2 * x + h, value.astype(bf16))

        def unenter(c):
            at = pl.ds(pl.multiple_of(c * quarter, quarter), quarter)
            d = lax.dot_general(d_out[...], w_out[x, at, :], NT, preferred_element_type=f32)
            low = (d * slope[x, :, at].astype(f32)).astype(bf16)
            d_in[:, at] = low
            row = jnp.sum(low.astype(f32), axis=0, keepdims=True)
            for q in range(quarter // 128):
                small_part[pl.ds(shape.b_in[x] + c * (quarter // 128) + q, 1), :] = row[:, q * 128 : (q + 1) * 128]

        loop(units // quarter, unenter)
        for h in range(2):
            value = jnp.dot(state_turned[...], d_in[:, h * half : (h + 1) * half], preferred_element_type=f32)
            send(blocks[0], part_in, inbox_in, own_in, total_in, 2 * x + h, value.astype(bf16))

        def unstate(c):
            at = pl.ds(pl.multiple_of(c * quarter, quarter), quarter)
            d_state[:, at] += lax.dot_general(d_in[...], w_in[x, at, :], NT, preferred_element_type=f32)

        loop(depth // quarter, unstate)
        pump()

    q = products[...].T
    q = [q[x : x + 1] for x in range(experts)]
    d_level = (share[0] * q[0] + share[1] * q[1], by_domain(which, q[SHARED:]))
    mean_share = share[0] * q[0] + share[1] * q[1]
    d_share = [level[0] * share[s] * (q[s] - mean_share) for s in range(SHARED)]
    mean_level = level[0] * d_level[0] + level[1] * d_level[1]
    d_group = [level[i] * (d_level[i] - mean_level) for i in range(2)]
    rows = d_share + [d_group[i] * here[d] for d in range(DOMAINS) for i in range(2)]
    d_logits = jnp.concatenate(rows + [jnp.zeros((GATE_ROWS - len(rows), events), f32)], axis=0)
    split = thirds(d_logits)
    gate_sums = jnp.dot(split, state_low[...], preferred_element_type=f32)
    gate_sums = sum(gate_sums[i * GATE_ROWS : (i + 1) * GATE_ROWS] for i in range(3))
    for i, place in enumerate(shape.gates):
        put_row(small_part, place, gate_sums[i : i + 1])
    gates_thrice = jnp.concatenate([gates[...]] * 3, axis=0)
    d_state[...] += lax.dot_general(split, gates_thrice, TN, preferred_element_type=f32)

    def unstart(i, sums):
        at = stripe(i)
        d, value = d_state[at, :], pre_standard[at, :]
        low = (standardise_back(d * inter_gain[...], value, pre_inverse[at, :]) * pre_slope[at, :]).astype(bf16)
        d_out[at, :] = low
        terms = (d * value, d, low.astype(f32))
        return tuple(s + jnp.sum(t, axis=0, keepdims=True) for s, t in zip(sums, terms))

    for place, row in zip((shape.inter_gain, shape.inter_bias, shape.proj_b),
                          lax.fori_loop(0, events // STRIPE, unstart, (zero,) * 3)):
        put_row(small_part, place, row)
    value = jnp.dot(joined[...], d_out[...], preferred_element_type=f32)
    send(blocks[3], part_proj, inbox_proj, own_proj, total_proj, 0, value.astype(bf16))
    ahead = counts.shape[0]

    def fetch(o):
        slot = o % ahead if isinstance(o, int) else lax.rem(o, ahead)
        return pltpu.make_async_copy(counts_hbm.at[o], counts.at[slot], count_sems.at[slot])

    for o in range(ahead):
        fetch(o).start()
    n_all = n_field * width
    d_fields[:n_all, :] = lax.dot_general(proj_w[:n_all, :], d_out[...], NT, preferred_element_type=f32).astype(bf16)
    tail = lax.dot_general(proj_w[n_all:, :], d_out[...], NT, preferred_element_type=f32)
    d_pooled[...] = (tail[:width] / length).astype(bf16)
    d_centered[...] = tail[width:]
    lanes = lax.broadcasted_iota(i32, (width, 128), 1)
    sums = jnp.zeros((width, 128), f32)
    for d in range(DOMAINS):
        mine = jnp.where(which == d, tail[width:], 0.0)
        for k, term in enumerate((mine, mine * centered[...])):
            sums = jnp.where(lanes == k * DOMAINS + d, jnp.sum(term, axis=1, keepdims=True), sums)
    small_part[shape.dense : shape.dense + width, :] = sums
    if small_part.shape[0] > shape.next:
        small_part[shape.next :, :] = jnp.zeros((small_part.shape[0] - shape.next, 128), f32)
    k = len(pieces)
    small_piece = Piece(
        small_part, small_inbox, small_own, small_total, ways[0], own_sems.at[k], sends.at[k], recvs.at[k]
    )
    small_piece.send()
    small_piece.sent_at = clock[0]
    pieces.append(small_piece)
    pump()

    shift = cap.bit_length() - 1
    slot_total[...] = jnp.zeros(slot_total.shape, f32)

    def scatter(f, carry):
        slot = field[pl.ds(f, 1), :]
        owner = jnp.right_shift(slot, shift)
        d = d_fields[pl.ds(pl.multiple_of(f * width, width), width), :].astype(f32)
        wide = jnp.concatenate([jnp.where(owner == o, d, 0.0).astype(bf16) for o in range(owners)], axis=0)
        slot_total[...] += lax.dot_general(
            wide, hot(cap, jnp.bitwise_and(slot, cap - 1)), NT, preferred_element_type=f32
        )
        return carry

    for first in range(0, n_field, 4):
        lax.fori_loop(first, min(first + 4, n_field), scatter, 0, unroll=2)
        pump()

    def spread(o):
        fetch(o).wait()
        behave = jnp.dot(d_pooled[...], counts[lax.rem(o, ahead)], preferred_element_type=f32)
        at = pl.ds(pl.multiple_of(o * width, width), width)
        slot_grad[o] = (slot_total[at, :] + behave).astype(bf16)
        pl.when(o + ahead < owners)(lambda: fetch(o + ahead).start())

    for first in range(0, owners, owners // 8):

        def spread_some(o, carry):
            spread(o)
            return carry

        lax.fori_loop(first, first + owners // 8, spread_some, 0)
        pump()
    me = lax.axis_index("wide") * lax.axis_size("narrow") + lax.axis_index("narrow")
    slot_copies = []
    for d, other, place in everyone_else():
        copy = pltpu.make_async_remote_copy(
            src_ref=slot_grad.at[other], dst_ref=returned.at[me], send_sem=slot_sends.at[d],
            recv_sem=slot_recvs.at[d], device_id=place, device_id_type=MESH)
        copy.start()
        slot_copies.append(copy)
    returned[me] = slot_grad[me]

    while any(not piece.done() for piece in pieces):
        for piece in pieces:
            if not piece.done():
                piece.take()
    for copy in slot_copies:
        copy.wait_recv()
    for copy in slot_copies:
        copy.wait_send()
    for piece in pieces:
        piece.drain()


def learn(fields, pooled, lengths, dense, domains, cotangent, stats, model, field, counts, devices):
    w_in, tower_in, proj_w = model[4], model[12], model[0]
    experts, depth, units = w_in.shape
    width, events = dense.shape
    owners, _, cap = counts.shape
    tower_units = tower_in.shape[2]
    half = units // 2
    shape = Rows(experts, units, depth, tower_units, width)
    n_small = shape.padded(devices)
    blocks = [
        Block(depth, half, devices), Block(half, depth, devices),
        Block(DOMAINS * depth, tower_units, devices), Block(proj_w.shape[0], depth, devices),
    ]
    numbers = (2 * experts, 2 * experts, 1, 1)
    pieces = [(n, b.padded, b.lanes) for n, b in zip(numbers, blocks)]
    steps = 2 * (devices.bit_length() - 1)
    n_pieces = sum(numbers) + 1
    joined = proj_w.shape[0]
    space = lambda *s: pltpu.VMEM(s, f32)
    low = lambda *s: pltpu.VMEM(s, bf16)
    dma = lambda *s: pltpu.SemaphoreType.DMA(s)
    in_specs = [vmem()] * 25
    in_specs[11] = in_specs[13] = in_specs[24] = hbm()
    out = pl.pallas_call(
        functools.partial(learn_kernel, shape, blocks),
        in_specs=in_specs,
        out_specs=[vmem()] * 4 + [hbm()] * 5,
        out_shape=[
            jax.ShapeDtypeStruct((1, events), f32),
            jax.ShapeDtypeStruct((width, events), f32),
            jax.ShapeDtypeStruct((width, events), f32),
            jax.ShapeDtypeStruct((owners, width, cap), bf16),
            jax.ShapeDtypeStruct((n_small, 128), f32),
        ]
        + [jax.ShapeDtypeStruct(s, bf16) for s in pieces],
        scratch_shapes=[
            low(experts, depth, units), low(experts, units, depth), low(joined, events),
            space(events, depth), space(events, depth), space(events, 1), low(events, depth),
            low(depth, events), space(events, 8), low(experts, events, units), low(experts, events, units),
            low(experts, events, depth), space(events, 8), space(events, depth), space(events, depth),
            low(events, depth), low(depth, events), low(DOMAINS, events, tower_units), space(events, depth),
            space(events, 8), low(events, depth), low(events, units), low(width, events), low(GATE_ROWS, depth), low(4, events, cap), space(owners * width, cap),
            low(owners, width, cap), space(n_small, 128), space(n_small, 128),
        ]
        + [pltpu.VMEM(s, bf16) for s in pieces] * 2
        + [space(n_small // devices, 128)]
        + [low(n, rows // devices, lanes) for n, rows, lanes in pieces]
        + [dma(experts), dma(experts), dma(4), dma(n_pieces), dma(n_pieces, steps), dma(n_pieces, steps), dma(devices), dma(devices)],
        compiler_params=params(collective_id=0, has_side_effects=True),
        name="learn",
    )(fields, pooled, lengths, dense, domains, cotangent, stats, *model, field, counts)
    return out[:5], [b.whole(t, n) for b, t, n in zip(blocks, out[5:], numbers)], shape


def get_row(small, at, n):
    return jnp.concatenate([small[at + c : at + c + 1, :] for c in range(n // 128)], axis=1)


def finish_kernel(shape, line, line_v, group, returned, domains, stats, centered, d_centered, small, *refs):
    more, out, more_out = refs[:4], refs[4], refs[5:9]
    d_dense, b_in, b_out, gain, bias, proj_b, inter_gain, inter_bias, gates, tower_in_bias, tower_out, tower_bias = refs[9:21]
    lines, vals = refs[21:]
    step = pl.program_id(0)
    per = out.shape[1] // ROW_CHUNK

    @pl.when(step == 0)
    def _():
        for target, places in (
            (b_in, shape.b_in), (b_out, shape.b_out), (gain, shape.gain), (bias, shape.bias),
            (proj_b, [shape.proj_b]), (inter_gain, [shape.inter_gain]), (inter_bias, [shape.inter_bias]),
            (gates, shape.gates), (tower_in_bias, shape.tower_in_bias), (tower_out, shape.tower_out),
            (tower_bias, [shape.tower_out_bias]),
        ):
            for i, at in enumerate(places):
                target[i : i + 1, :] = get_row(small, at, target.shape[1])
        which = domains[...]
        sums = small[shape.dense : shape.dense + centered.shape[0], :]
        moments = domain_moments(stats[...])
        scale = by_domain(which, [m[1] for m in moments])
        straight = by_domain(which, [sums[:, d : d + 1] / m[2] for d, m in enumerate(moments)])
        cross = by_domain(which, [sums[:, DOMAINS + d : DOMAINS + d + 1] / m[2] for d, m in enumerate(moments)])
        d_dense[...] = scale * (d_centered[...] - straight - centered[...] * cross)

        def clear(i, carry):
            lines[pl.ds(pl.multiple_of(i * 1024, 1024), 1024), :] = jnp.zeros((1024, 128), f32)
            return carry

        lax.fori_loop(0, lines.shape[0] // 1024, clear, 0)

    width, cap = returned.shape[1:]

    @pl.when(step < ADD_STEPS)
    def _():
        batch = 32
        a = lax.div(lax.broadcasted_iota(i32, (cap, cap), 0), batch)
        near = a == lax.div(lax.broadcasted_iota(i32, (cap, cap), 1), batch)
        each = group.shape[0] // ADD_STEPS

        def prepare(s, slot):
            which, own = jnp.broadcast_to(group[s], (width, cap)), returned[s].astype(f32)
            wide = jnp.concatenate([jnp.where(which == g, own, 0.0) for g in range(8)], axis=0)
            along = jnp.broadcast_to(line_v[s].astype(f32), (cap, cap))
            same = jnp.where(jnp.logical_and(along == along.T, near), 1.0, 0.0).astype(bf16)
            vals[slot] = lax.dot_general(same, wide.astype(bf16), NT, preferred_element_type=f32)

        def add(s, slot):
            for u in range(0, cap, batch):
                places, sums = [], []
                for j in range(u, u + batch):
                    places.append(line[s * cap + j])
                    sums.append(lines[pl.ds(places[-1], 1), :] + vals[slot, j : j + 1, :])
                for place, total in zip(places, sums):
                    lines[pl.ds(place, 1), :] = total

        prepare(step * each, 0)

        def serve(i, carry):
            s = step * each + i * 2
            prepare(s + 1, 1)
            add(s, 0)
            prepare(jnp.minimum(s + 2, group.shape[0] - 1), 0)
            add(s + 1, 1)
            return carry

        lax.fori_loop(0, each // 2, serve, 0)
        for source, target in zip(more, more_out):
            tall, blocks, rows, lanes = source.shape
            for s in range(tall):
                for c in range(blocks):
                    target[s * rows : (s + 1) * rows, c * lanes : (c + 1) * lanes] = source[s, c].astype(f32)

    @pl.when(step >= ADD_STEPS)
    def _():
        def turn(c, carry):
            at = pl.multiple_of(((step - ADD_STEPS) * per + c) * 128, 128)
            turned = lines[pl.ds(at, 128), :].T
            for g in range(8):
                at = pl.multiple_of(c * ROW_CHUNK + g * 128, 128)
                out[:, pl.ds(at, 128)] = turned[g * width : (g + 1) * width]
            return carry

        lax.fori_loop(0, per, turn, 0, unroll=4)


def finish(shape, line, group, returned, domains, stats, centered, d_centered, small, more, rows):
    blocks, width, cap = returned.shape
    events = centered.shape[1]
    experts, units, depth = len(shape.b_in), more[0].shape[1] * more[0].shape[3], more[0].shape[2]
    tower = more[2].shape[1] * more[2].shape[3]
    steps, turns = ADD_STEPS, 4
    early = lambda i: jnp.minimum(i, steps - 1)
    in_more, out_more, shapes = [], [], []
    for x in more:
        tall, parts, r, lanes = x.shape
        if tall > 1:
            in_more.append(pl.BlockSpec((tall // steps, parts, r, lanes), lambda i: (early(i), 0, 0, 0)))
        else:
            in_more.append(pl.BlockSpec((1, parts, r // steps, lanes), lambda i: (0, 0, early(i), 0)))
        out_more.append(pl.BlockSpec((tall * r // steps, parts * lanes), lambda i: (early(i), 0)))
        shapes.append((tall * r, parts * lanes))
    shapes += [(width, events), (experts, units)] + [(experts, depth)] * 3 + [(1, depth)] * 3
    shapes += [(len(shape.gates), depth), (DOMAINS, tower), (DOMAINS, tower), (1, 128)]
    return pl.pallas_call(
        functools.partial(finish_kernel, shape),
        grid=(steps + turns,),
        in_specs=[smem()] + [vmem()] * 8 + in_more,
        out_specs=[pl.BlockSpec((width, rows // turns), lambda i: (0, jnp.maximum(i - steps, 0)))] + out_more + [vmem()] * 12,
        out_shape=[jax.ShapeDtypeStruct(s, f32) for s in [(width, rows)] + shapes],
        scratch_shapes=[pltpu.VMEM((rows // 8, 128), f32), pltpu.VMEM((2, cap, 128), f32)],
        compiler_params=params(),
        name="finish",
    )(line.reshape(-1), line, group, returned, domains, stats, centered, d_centered, small, *more)


def local(
    table,
    dense,
    domains,
    lengths,
    requests,
    counts,
    field_slots,
    behave_slots,
    proj_w,
    proj_b,
    inter_gain,
    inter_bias,
    w_in,
    b_in,
    w_out,
    b_out,
    expert_gain,
    expert_bias,
    shared_gate,
    group_gate,
    tower_in,
    tower_in_bias,
    tower_out,
    tower_out_bias,
    pred_cotangent,
):
    devices = lax.axis_size("wide") * lax.axis_size("narrow")
    capacity = requests.shape[2]
    experts, depth, units = w_in.shape
    counts_of = slot_counts(lengths, behave_slots.reshape(-1, 128), devices, capacity)
    field = field_slots.T
    dense_t, which = dense.T, domains[None]
    fields, pooled, line, group, stats = lookup(
        requests[0], table.T, counts.reshape(-1), field, counts_of, dense_t, which
    )
    model = (
        proj_w, proj_b[None], inter_gain[None], inter_bias[None], w_in, b_in, w_out, b_out, expert_gain, expert_bias,
        shared_gate.T, group_gate.transpose(0, 2, 1), tower_in, tower_in_bias, tower_out, tower_out_bias[None],
    )
    (pred, centered, d_centered, returned, small), totals, shape = learn(
        fields, pooled, lengths, dense_t, which, pred_cotangent[None], stats, model, field, counts_of, devices
    )
    totals[0] = totals[0].reshape(experts, -1, depth, totals[0].shape[3])
    out = finish(shape, line, group, returned, which, stats, centered, d_centered, small, totals, table.shape[0])
    d_table, d_w_in, d_w_out, d_tower_in, d_proj_w, d_dense, d_b_in, d_b_out, d_gain, d_bias = out[:10]
    d_proj_b, d_inter_gain, d_inter_bias, d_gates, d_tower_in_bias, d_tower_out, d_tower_bias = out[10:]
    return (
        pred[0],
        d_dense.T,
        d_table.T,
        d_proj_w,
        d_proj_b[0],
        d_inter_gain[0],
        d_inter_bias[0],
        d_w_in.reshape(w_in.shape),
        d_b_in,
        d_w_out.reshape(w_out.shape),
        d_b_out,
        d_gain,
        d_bias,
        d_gates[:SHARED].T,
        d_gates[SHARED:].reshape(DOMAINS, 2, depth).transpose(0, 2, 1),
        d_tower_in.reshape(tower_in.shape),
        d_tower_in_bias,
        d_tower_out,
        d_tower_bias[0, :DOMAINS],
    )


def solution(mesh):
    placed = (
        P(("wide", "narrow"), None),
        P(("wide", "narrow"), None),
        P(("wide", "narrow")),
        P(("wide", "narrow"), None),
        P(("wide", "narrow"), None, None),
        P(("wide", "narrow"), None),
        P(("wide", "narrow"), None),
        P(("wide", "narrow"), None),
        P(),
        P(),
        P(),
        P(),
        P(),
        P(),
        P(),
        P(),
        P(),
        P(),
        P(),
        P(),
        P(),
        P(),
        P(),
        P(),
        P(("wide", "narrow")),
    )
    return jax.shard_map(
        local,
        mesh=mesh,
        in_specs=placed,
        out_specs=(
            P(("wide", "narrow")),
            P(("wide", "narrow"), None),
            P(("wide", "narrow"), None),
            P(),
            P(),
            P(),
            P(),
            P(),
            P(),
            P(),
            P(),
            P(),
            P(),
            P(),
            P(),
            P(),
            P(),
            P(),
            P(),
        ),
        check_vma=False,
    )
```

```python
import functools
import math

import jax
import jax.numpy as jnp
from jax import lax
from jax.experimental import pallas as pl
from jax.experimental.pallas import tpu as pltpu
from jax.sharding import PartitionSpec as P

SHARED = 2
DOMAINS = 2

EPSILON = 1e-05

f32 = jnp.float32
bf16 = jnp.bfloat16
i32 = jnp.int32
MESH = pl.DeviceIdType.MESH
AXES = ("wide", "narrow")
NT = (((1,), (1,)), ((), ()))
TN = (((0,), (0,)), ((), ()))
VMEM_LIMIT = 60 * 1024 * 1024
ROW_CHUNK = 1024
GROUP = 8
SPAN = 6
BUNCH = 4
ADD_STEPS = 4


def vmem():
    return pl.BlockSpec(memory_space=pltpu.VMEM)


def smem():
    return pl.BlockSpec(memory_space=pltpu.SMEM)


def hbm():
    return pl.BlockSpec(memory_space=pl.ANY)


def params(**more):
    return pltpu.CompilerParams(vmem_limit_bytes=VMEM_LIMIT, **more)


def line_of(rows):
    return jnp.left_shift(jnp.right_shift(rows, 10), 7) + jnp.bitwise_and(rows, 127)


def lane_group_of(rows):
    return jnp.bitwise_and(jnp.right_shift(rows, 7), 7)


def identity(n):
    return (lax.broadcasted_iota(i32, (n, n), 0) == lax.broadcasted_iota(i32, (n, n), 1)).astype(bf16)


def hot(rows, index):
    column = lax.broadcasted_iota(i32, (rows, index.shape[1]), 0)
    return jnp.where(column == index, 1.0, 0.0).astype(bf16)


def count_kernel(lengths, behave, counts, sums, done):
    owners, _, cap = counts.shape
    shift = cap.bit_length() - 1
    step = pl.program_id(0)
    place = lax.broadcasted_iota(i32, (SPAN, 128), 0) * 128 + lax.broadcasted_iota(i32, (SPAN, 128), 1)
    last_block = behave.shape[0] - SPAN
    ends = [jnp.where(step == 0, 0, done[0])]
    for i in range(BUNCH * GROUP):
        ends.append(ends[-1] + lengths[0, step * (BUNCH * GROUP) + i])
    done[0] = ends[-1]

    def part(k, m):
        cuts = ends[k * GROUP : (k + 1) * GROUP + 1]
        begin = lax.div(cuts[0], 128) + m * SPAN
        b = jnp.minimum(begin, last_block)
        slot = behave[pl.ds(b, SPAN), :]
        p = place + b * 128
        event = jnp.zeros_like(p)
        for cut in cuts[1:-1]:
            event = event + jnp.where(p >= cut, 1, 0)
        mine = jnp.logical_and(jnp.logical_and(p >= cuts[0], p < cuts[-1]), p >= begin * 128)
        key = jnp.where(mine, jnp.right_shift(slot, shift) * GROUP + event, -1)
        low = jnp.bitwise_and(slot, cap - 1)
        left = jnp.concatenate([hot(owners * GROUP, key[q : q + 1]) for q in range(SPAN)], axis=1)
        right = jnp.concatenate([hot(cap, low[q : q + 1]) for q in range(SPAN)], axis=1)
        return lax.dot_general(left, right, NT, preferred_element_type=f32)

    parts = []
    for k in range(BUNCH):
        sums[k] = part(k, 0)
        first, last = ends[k * GROUP], ends[(k + 1) * GROUP]
        parts.append(lax.div(last - lax.div(first, 128) * 128 + (SPAN * 128 - 1), SPAN * 128))
    most = functools.reduce(jnp.maximum, parts)

    @pl.when(most > 1)
    def _():
        for k in range(BUNCH):

            def more(m, carry):
                sums[k] += part(k, m)
                return carry

            lax.fori_loop(1, parts[k], more, 0)

    for t in range(BUNCH // 2):
        for o in range(owners):
            both = [sums[2 * t + k, o * GROUP : (o + 1) * GROUP, :] for k in range(2)]
            counts[o, t * 2 * GROUP : (t + 1) * 2 * GROUP, :] = jnp.concatenate(both, axis=0).astype(bf16)


def slot_counts(lengths, behave, owners, cap):
    events = lengths.shape[1]
    size = BUNCH * GROUP
    return pl.pallas_call(
        count_kernel,
        grid=(events // size,),
        in_specs=[smem(), vmem()],
        out_specs=pl.BlockSpec((owners, size, cap), lambda i: (0, i, 0)),
        out_shape=jax.ShapeDtypeStruct((owners, events, cap), bf16),
        scratch_shapes=[pltpu.VMEM((BUNCH, owners * GROUP, cap), f32), pltpu.SMEM((1,), i32)],
        compiler_params=params(),
        name="slot_counts",
    )(lengths, behave)


def place_bits():
    return [(axis, b) for axis in AXES for b in range(lax.axis_size(axis).bit_length() - 1)]


def bit_value(bit):
    return lax.rem(lax.div(lax.axis_index(bit[0]), 1 << bit[1]), 2)


def across(bit):
    axis, b = bit
    place = {a: lax.axis_index(a) for a in AXES}
    place[axis] = place[axis] + (1 - 2 * bit_value(bit)) * (1 << b)
    return tuple(place[a] for a in AXES)


class Piece:
    def __init__(self, part, inbox, own, total, order, own_sem, sends, recvs):
        self.part, self.inbox, self.own, self.total = part, inbox, own, total
        self.order, self.own_sem, self.sends, self.recvs = order, own_sem, sends, recvs
        self.rows = part.shape[0]
        self.grain = self.rows >> len(order)
        self.offsets, self.copies, self.taken = [0], [], 0

    def at(self, ref, offset, n):
        return ref.at[pl.ds(pl.multiple_of(offset, self.grain), n)]

    def keep(self):
        return pltpu.make_async_copy(self.own, self.at(self.total, self.offsets[-1], self.grain), self.own_sem)

    def send(self):
        k, depth = len(self.copies), len(self.order)
        if k < depth:
            bit, half = self.order[k], self.rows >> (k + 1)
            value, offset = bit_value(bit), self.offsets[k]
            self.offsets.append(offset + value * half)
            source = self.at(self.part, offset + (1 - value) * half, half)
            target = self.inbox.at[pl.ds(self.rows - (self.rows >> k), half)]
        else:
            s = 2 * depth - 1 - k
            bit = self.order[s]
            target = self.at(self.total, self.offsets[s + 1], self.rows >> (s + 1))
            source = self.own if k == depth else target
        copy = pltpu.make_async_remote_copy(
            src_ref=source,
            dst_ref=target,
            send_sem=self.sends.at[k],
            recv_sem=self.recvs.at[k],
            device_id=across(bit),
            device_id_type=MESH,
        )
        copy.start()
        self.copies.append(copy)

    def done(self):
        return self.taken == 2 * len(self.order)

    def take(self):
        k, depth = self.taken, len(self.order)
        self.copies[k].wait_recv()
        self.taken += 1
        if k < depth:
            n, base, offset = self.rows >> (k + 1), self.rows - (self.rows >> k), self.offsets[k + 1]
            chunk = math.gcd(n, 64)

            def add(i, carry):
                at = pl.ds(pl.multiple_of(offset + i * chunk, math.gcd(self.grain, chunk)), chunk)
                came = pl.ds(pl.multiple_of(base + i * chunk, chunk), chunk)
                total = (self.part[at, :].astype(f32) + self.inbox[came, :].astype(f32)).astype(self.part.dtype)
                if k == depth - 1:
                    self.own[pl.ds(pl.multiple_of(i * chunk, chunk), chunk), :] = total
                else:
                    self.part[at, :] = total
                return carry

            lax.fori_loop(0, n // chunk, add, 0)
        if k == depth - 1:
            self.keep().start()
        if k == depth:
            self.keep().wait()
        if not self.done():
            self.send()

    def drain(self):
        for copy in self.copies:
            copy.wait_send()


def everyone_else():
    n_wide, n_narrow = (lax.axis_size(a) for a in AXES)
    w, n = (lax.axis_index(a) for a in AXES)
    me = w * n_narrow + n
    total = n_wide * n_narrow
    for d in range(1, total):
        other = lax.rem(me + d, total)
        yield d, other, (lax.div(other, n_narrow), lax.rem(other, n_narrow))


def greet_all():
    barrier = pltpu.get_barrier_semaphore()
    for _, _, place in everyone_else():
        pl.semaphore_signal(barrier, inc=1, device_id=place, device_id_type=MESH)


def wait_for_all():
    pl.semaphore_wait(pltpu.get_barrier_semaphore(), lax.axis_size("wide") * lax.axis_size("narrow") - 1)


def meet_all():
    greet_all()
    wait_for_all()


def lanes_of(rows, columns, devices):
    lanes = columns
    while lanes > 128 and (rows * (columns // lanes)) % (16 * devices):
        lanes //= 2
    return lanes


ORDERS = "ABABGABDABABGABABA"


class Block:
    def __init__(self, rows, columns, devices):
        self.rows, self.columns = rows, columns
        self.lanes = lanes_of(rows, columns, devices)
        self.blocks = columns // self.lanes
        self.padded = -(-rows * self.blocks // (16 * devices)) * 16 * devices

    def put(self, piece, value):
        for c in range(self.blocks):
            piece[c * self.rows : (c + 1) * self.rows, :] = value[:, c * self.lanes : (c + 1) * self.lanes]
        extra = self.padded - self.rows * self.blocks
        if extra:
            piece[self.rows * self.blocks :, :] = jnp.zeros((extra, self.lanes), piece.dtype)

    def whole(self, total, n):
        return total[:, : self.rows * self.blocks].reshape(n, self.blocks, self.rows, self.lanes)


def orders():
    if tuple(lax.axis_size(a) for a in AXES) != (8, 4):
        return [place_bits()] * len(ORDERS)
    core, y, x, z0, z1 = ("narrow", 0), ("narrow", 1), ("wide", 0), ("wide", 1), ("wide", 2)
    ways = {
        "A": [core, x, y, z0, z1],
        "B": [core, y, x, z0, z1],
        "D": [core, z0, z1, y, x],
        "G": [core, z0, z1, x, y],
    }
    return [ways[way] for way in ORDERS]


def lookup_kernel(
    requests_in, table, live, field, counts_hbm, dense, domains,
    fields, pooled, line_out, group, stats_out,
    requests, counts, tab, lines, got, line, line_smem, found, rows, slots, stats, stats_in,
    tab_sems, counts_sem, line_sem, ask_sends, ask_recvs, row_sends, row_recvs, stat_sends, stat_recvs,
):
    owners, _, cap = requests.shape
    width = tab.shape[0]
    n_field, events = field.shape
    chunks = tab_sems.shape[0]
    part = tab.shape[1] // chunks
    n_narrow = lax.axis_size("narrow")
    me = lax.axis_index("wide") * n_narrow + lax.axis_index("narrow")

    loads = []
    for c in range(chunks):
        at = pl.ds(c * part, part)
        loads.append(pltpu.make_async_copy(table.at[:, at], tab.at[:, at], tab_sems.at[c]))
        loads[-1].start()
    load_counts = pltpu.make_async_copy(counts_hbm, counts, counts_sem)
    load_counts.start()
    for o in range(owners):
        requests[o] = requests_in[o : o + 1, :]
    lane = lax.broadcasted_iota(i32, (width, 128), 1)
    mine = jnp.zeros((width, 128), f32)
    for d in range(DOMAINS):
        here = domains[...] == d
        value = jnp.where(here, dense[...], 0.0)
        one = jnp.broadcast_to(jnp.where(here, 1.0, 0.0), value.shape)
        for k, term in enumerate((value, value * value, one)):
            mine = jnp.where(lane == k * DOMAINS + d, jnp.sum(term, axis=1, keepdims=True), mine)
    stats[...] = mine

    meet_all()

    def peer(d):
        other = lax.rem(me + d, owners)
        return other, (lax.div(other, n_narrow), lax.rem(other, n_narrow))

    def ask(d):
        other, place = peer(d)
        return pltpu.make_async_remote_copy(
            src_ref=requests.at[other], dst_ref=line.at[me], send_sem=ask_sends.at[d],
            recv_sem=ask_recvs.at[d], device_id=place, device_id_type=MESH)

    def tell(d):
        _, place = peer(d)
        return pltpu.make_async_remote_copy(
            src_ref=stats, dst_ref=stats_in.at[me], send_sem=stat_sends.at[d],
            recv_sem=stat_recvs.at[d], device_id=place, device_id_type=MESH)

    def answer(d):
        other, place = peer(d)
        return pltpu.make_async_remote_copy(
            src_ref=found.at[other], dst_ref=rows.at[me], send_sem=row_sends.at[d],
            recv_sem=row_recvs.at[d], device_id=place, device_id_type=MESH)

    def each(first, act):
        def step(d, carry):
            act(d)
            return carry

        lax.fori_loop(first, owners, step, 0)

    each(1, lambda d: ask(d).start())
    each(1, lambda d: tell(d).start())
    line[me] = requests[me]
    stats_in[me] = stats[...]

    eye = identity(128)
    for c in range(chunks):
        loads[c].wait()

        def turn(i, carry):
            base = pl.multiple_of(c * part + i * ROW_CHUNK, ROW_CHUNK)
            stack = jnp.concatenate([tab[:, pl.ds(base + g * 128, 128)] for g in range(8)], axis=0)
            at = pl.multiple_of((c * part // ROW_CHUNK + i) * 128, 128)
            lines[pl.ds(at, 128), :] = lax.dot_general(eye, stack, NT, preferred_element_type=f32)
            return carry

        lax.fori_loop(0, part // ROW_CHUNK, turn, 0, unroll=8)

    each(1, lambda d: ask(d).wait_recv())
    group[...] = lane_group_of(line[...])
    line_out[...] = line_of(line[...])
    to_smem = pltpu.make_async_copy(line_out, line_smem, line_sem)
    to_smem.start()
    to_smem.wait()

    def source(d):
        return lax.rem(me + d, owners)

    def fetch(d):
        s, half = source(d), lax.rem(d, 2) * cap
        for j in range(cap):
            got[pl.ds(half + j, 1), :] = lines[pl.ds(line_smem[s, 0, j], 1), :]

    def turn_out(d):
        s, half = source(d), pl.multiple_of(lax.rem(d, 2) * cap, cap)
        turned = lax.dot_general(eye, got[pl.ds(half, cap), :].astype(bf16), NT, preferred_element_type=f32)
        which = jnp.broadcast_to(group[s], (width, cap))
        picked = turned[:width]
        for g in range(1, 8):
            picked = jnp.where(which == g, turned[g * width : (g + 1) * width], picked)
        found[s] = picked.astype(bf16)

    fetch(0)

    def serve(d, carry):
        turn_out(d - 1)
        fetch(d)
        pl.when(d > 1)(lambda: answer(d - 1).start())
        return carry

    lax.fori_loop(1, owners, serve, 0)
    turn_out(owners - 1)
    answer(owners - 1).start()
    rows[me] = found[me]
    each(1, lambda d: tell(d).wait_recv())
    total = stats_in[0]
    for o in range(1, owners):
        total = total + stats_in[o]
    stats_out[...] = total

    each(1, lambda d: answer(d).wait_recv())
    shift = cap.bit_length() - 1
    column = lax.broadcasted_iota(i32, (width, cap), 1)
    for o in range(owners):
        slots[o * width : (o + 1) * width, :] = jnp.where(column < live[o], rows[o].astype(f32), 0.0).astype(bf16)

    def one(f, carry):
        slot = field[pl.ds(f, 1), :]
        owner = jnp.broadcast_to(jnp.right_shift(slot, shift), (width, events))
        all_owners = jnp.dot(slots[...], hot(cap, jnp.bitwise_and(slot, cap - 1)), preferred_element_type=f32)
        picked = all_owners[:width]
        for o in range(1, owners):
            picked = jnp.where(owner == o, all_owners[o * width : (o + 1) * width], picked)
        fields[pl.ds(pl.multiple_of(f * width, width), width), :] = picked.astype(bf16)
        return carry

    lax.fori_loop(0, n_field, one, 0, unroll=2)
    load_counts.wait()
    total = jnp.zeros((events, width), f32)
    for o in range(owners):
        total = total + lax.dot_general(counts[o], slots[o * width : (o + 1) * width, :], NT, preferred_element_type=f32)
    pooled[...] = total.T
    each(1, lambda d: ask(d).wait_send())
    each(1, lambda d: tell(d).wait_send())
    each(1, lambda d: answer(d).wait_send())


def lookup(requests, table_t, live, field_t, counts, dense_t, domains):
    owners, cap = requests.shape
    width, rows = table_t.shape
    n_field, events = field_t.shape
    chunks = 6
    dma = pltpu.SemaphoreType.DMA
    return pl.pallas_call(
        lookup_kernel,
        in_specs=[vmem(), hbm(), smem(), vmem(), hbm(), vmem(), vmem()],
        out_specs=[vmem()] * 5,
        out_shape=[
            jax.ShapeDtypeStruct((n_field * width, events), bf16),
            jax.ShapeDtypeStruct((width, events), f32),
            jax.ShapeDtypeStruct((owners, 1, cap), i32),
            jax.ShapeDtypeStruct((owners, 1, cap), i32),
            jax.ShapeDtypeStruct((width, 128), f32),
        ],
        scratch_shapes=[
            pltpu.VMEM((owners, 1, cap), i32),
            pltpu.VMEM((owners, events, cap), bf16),
            pltpu.VMEM((width, rows), bf16),
            pltpu.VMEM((rows // 8, 128), f32),
            pltpu.VMEM((2 * cap, 128), f32),
            pltpu.VMEM((owners, 1, cap), i32),
            pltpu.SMEM((owners, 1, cap), i32),
            pltpu.VMEM((owners, width, cap), bf16),
            pltpu.VMEM((owners, width, cap), bf16),
            pltpu.VMEM((owners * width, cap), bf16),
            pltpu.VMEM((width, 128), f32),
            pltpu.VMEM((owners, width, 128), f32),
            dma((chunks,)),
            dma,
            dma,
        ]
        + [dma((owners,))] * 6,
        compiler_params=params(collective_id=1, has_side_effects=True),
        name="lookup",
    )(requests, table_t, live, field_t, counts, dense_t, domains)


STRIPE = 128
GATE_ROWS = 16
GELU_SCALE = math.sqrt(2.0 / math.pi)
GELU_CUBE = 0.044715


def gelu_and_slope(x):
    square = x * x
    t = jnp.tanh(GELU_SCALE * (x + GELU_CUBE * (square * x)))
    half = 0.5 * (1.0 + t)
    return x * half, half + 0.5 * x * (1.0 - t * t) * (GELU_SCALE * (1.0 + 3.0 * GELU_CUBE * square))


def standardise(values):
    center = values - jnp.mean(values, axis=-1, keepdims=True)
    inverse = lax.rsqrt(jnp.mean(center * center, axis=-1, keepdims=True) + EPSILON)
    return center * inverse, inverse


def standardise_back(d, standard, inverse):
    along = jnp.mean(d * standard, axis=-1, keepdims=True)
    return inverse * (d - jnp.mean(d, axis=-1, keepdims=True) - standard * along)


def loop(n, body):
    def step(i, carry):
        body(i)
        return carry

    lax.fori_loop(0, n, step, 0, unroll=2)


def columns(rows):
    have = rows.shape[0]
    if have < 8:
        rows = jnp.concatenate([rows, jnp.zeros((8 - have, rows.shape[1]), f32)], axis=0)
    return rows.T


def thirds(x):
    high = x.astype(bf16)
    rest = x - high.astype(f32)
    middle = rest.astype(bf16)
    return jnp.concatenate([high, middle, (rest - middle.astype(f32)).astype(bf16)], axis=0)


def domain_moments(stats):
    result = []
    for d in range(DOMAINS):
        count = stats[:, 2 * DOMAINS + d : 2 * DOMAINS + d + 1]
        mean = stats[:, d : d + 1] / count
        variance = stats[:, DOMAINS + d : DOMAINS + d + 1] / count - mean * mean
        result.append((mean, lax.rsqrt(variance + EPSILON), count))
    return result


def by_domain(domains, values):
    picked = values[0]
    for d in range(1, DOMAINS):
        picked = jnp.where(domains == d, values[d], picked)
    return picked


class Rows:
    def __init__(self, experts, units, depth, tower, width):
        self.next = 0
        lines = lambda n: -(-n // 128)
        self.b_in = [self.take(lines(units)) for _ in range(experts)]
        self.b_out, self.gain, self.bias = ([self.take(lines(depth)) for _ in range(experts)] for _ in range(3))
        self.proj_b, self.inter_gain, self.inter_bias = (self.take(lines(depth)) for _ in range(3))
        self.gates = [self.take(lines(depth)) for _ in range(SHARED + 2 * DOMAINS)]
        self.tower_in_bias, self.tower_out = ([self.take(lines(tower)) for _ in range(DOMAINS)] for _ in range(2))
        self.tower_out_bias = self.take(1)
        self.dense = self.take(width)

    def take(self, n):
        at, self.next = self.next, self.next + n
        return at

    def padded(self, devices):
        return -(-self.next // (8 * devices)) * 8 * devices


def put_row(small, at, row):
    for c in range(row.shape[1] // 128):
        small[at + c : at + c + 1, :] = row[:, c * 128 : (c + 1) * 128]


def learn_kernel(
    shape, blocks,
    fields, pooled, lengths, dense, domains, cotangent, stats, proj_w, proj_b, inter_gain, inter_bias,
    w_in_hbm, b_in, w_out_hbm, b_out, expert_gain, expert_bias, shared_gate, group_gate, tower_in, tower_in_bias, tower_out,
    tower_out_bias, field, counts_hbm,
    pred, centered, d_centered, returned, small_total, total_in, total_out, total_tower, total_proj,
    w_in, w_out, joined, pre_slope, pre_standard, pre_inverse, state_low, state_turned, coef,
    active, slope, standard, inverse, work, after, after_low, after_turned, d_tower, d_after, products,
    d_out, d_in, d_pooled, gates, counts, slot_total, slot_grad,
    small_part, small_inbox, part_in, part_out, part_tower, part_proj, inbox_in, inbox_out, inbox_tower, inbox_proj,
    small_own, own_in, own_out, own_tower, own_proj, in_sems, out_sems, count_sems, own_sems, sends, recvs, slot_sends, slot_recvs,
):
    experts, depth, units = w_in.shape
    width, events = dense.shape
    n_field = field.shape[0]
    owners, _, cap = slot_grad.shape
    tower_units = tower_in.shape[2]
    greet_all()
    for x in range(experts):
        pltpu.make_async_copy(w_in_hbm.at[x], w_in.at[x], in_sems.at[x]).start()
        pltpu.make_async_copy(w_out_hbm.at[x], w_out.at[x], out_sems.at[x]).start()

    which = domains[...]
    length = lengths[...].astype(f32)
    rows = [shared_gate[...].astype(f32)] + [group_gate[d].astype(f32) for d in range(DOMAINS)]
    have = SHARED + 2 * DOMAINS
    gates[...] = jnp.concatenate(rows + [jnp.zeros((GATE_ROWS - have, depth), f32)], axis=0).astype(bf16)
    moments = domain_moments(stats[...])
    mean, scale = (by_domain(which, [m[i] for m in moments]) for i in range(2))
    centered[...] = (dense[...] - mean) * scale
    joined[: n_field * width, :] = fields[...]
    joined[n_field * width : (n_field + 1) * width, :] = (pooled[...] / length).astype(bf16)
    joined[(n_field + 1) * width :, :] = centered[...].astype(bf16)
    joined_rows, d_state, d_fields = d_in.at[:, : joined.shape[0]], after, joined
    joined_rows[...] = joined[...].T
    quarter = 256

    def project(c):
        at = pl.ds(pl.multiple_of(c * quarter, quarter), quarter)
        work[:, at] = jnp.dot(joined_rows[...], proj_w[:, at], preferred_element_type=f32) + proj_b[:, at]

    loop(depth // quarter, project)

    def stripe(i):
        return pl.ds(pl.multiple_of(i * STRIPE, STRIPE), STRIPE)

    def start_state(i):
        at = stripe(i)
        value, pre_slope[at, :] = gelu_and_slope(work[at, :])
        pre_standard[at, :], pre_inverse[at, :] = standardise(value)
        state = pre_standard[at, :] * inter_gain[...] + inter_bias[...]
        after[at, :] = state
        state_low[at, :] = state.astype(bf16)

    loop(events // STRIPE, start_state)
    state_turned[...] = state_low[...].T
    logits = lax.dot_general(gates[...], state_low[...], NT, preferred_element_type=f32)

    def softmax_pair(a, b):
        top = jnp.maximum(a, b)
        a, b = jnp.exp(a - top), jnp.exp(b - top)
        return a / (a + b), b / (a + b)

    share = softmax_pair(logits[0:1], logits[1:2])
    group_logits = [
        by_domain(which, [logits[SHARED + 2 * d + i : SHARED + 2 * d + i + 1] for d in range(DOMAINS)]) for i in range(2)
    ]
    level = softmax_pair(*group_logits)
    here = [jnp.where(which == d, 1.0, 0.0) for d in range(DOMAINS)]
    weights = [level[0] * share[0], level[0] * share[1]] + [level[1] * here[d] for d in range(DOMAINS)]
    weight_columns = columns(jnp.concatenate(weights, axis=0))
    coef[...] = weight_columns

    def expert_forward(x):
        pltpu.make_async_copy(w_in_hbm.at[x], w_in.at[x], in_sems.at[x]).wait()

        def enter(c):
            at = pl.ds(pl.multiple_of(c * quarter, quarter), quarter)
            pre = jnp.dot(state_low[...], w_in[x, :, at], preferred_element_type=f32) + b_in[x : x + 1, at]
            value, rise = gelu_and_slope(pre)
            active[x, :, at] = value.astype(bf16)
            slope[x, :, at] = rise.astype(bf16)

        loop(units // quarter, enter)
        pltpu.make_async_copy(w_out_hbm.at[x], w_out.at[x], out_sems.at[x]).wait()

        def leave(c):
            at = pl.ds(pl.multiple_of(c * quarter, quarter), quarter)
            work[:, at] = jnp.dot(active[x], w_out[x, :, at], preferred_element_type=f32) + b_out[x : x + 1, at]

        loop(depth // quarter, leave)

        def mix(i):
            at = stripe(i)
            value, inverse[at, x : x + 1] = standardise(work[at, :])
            standard[x, at, :] = value.astype(bf16)
            after[at, :] += coef[at, x : x + 1] * (value * expert_gain[x : x + 1, :] + expert_bias[x : x + 1, :])

        loop(events // STRIPE, mix)

    for x in range(experts):
        expert_forward(x)
    after_low[...] = after[...].astype(bf16)
    after_turned[...] = after_low[...].T

    here_columns = columns(jnp.concatenate(here + [cotangent[...]], axis=0))
    logit = jnp.zeros((events, 1), f32)
    for d in range(DOMAINS):
        pre = jnp.dot(after_low[...], tower_in[d], preferred_element_type=f32) + tower_in_bias[d : d + 1, :]
        value, rise = gelu_and_slope(pre)
        work[:, d * tower_units : (d + 1) * tower_units] = value
        d_after[:, d * tower_units : (d + 1) * tower_units] = rise
        head = jnp.sum(value * tower_out[d : d + 1, :], axis=1, keepdims=True) + tower_out_bias[:, d : d + 1]
        logit = logit + here_columns[:, d : d + 1] * head
    chance = 1.0 / (1.0 + jnp.exp(-logit))
    d_logit = here_columns[:, DOMAINS : DOMAINS + 1] * chance * (1.0 - chance)
    pred[...] = jnp.broadcast_to(chance, (events, 8)).T[0:1, :]
    lane = lax.broadcasted_iota(i32, (1, 128), 1)
    bias_row = jnp.zeros((1, 128), f32)
    for d in range(DOMAINS):
        at = slice(d * tower_units, (d + 1) * tower_units)
        mine = d_logit * here_columns[:, d : d + 1]
        put_row(small_part, shape.tower_out[d], jnp.sum(mine * work[:, at], axis=0, keepdims=True))
        bias_row = jnp.where(lane == d, jnp.sum(mine, axis=0, keepdims=True), bias_row)
        low = (mine * tower_out[d : d + 1, :] * d_after[:, at]).astype(bf16)
        d_tower[d] = low
        put_row(small_part, shape.tower_in_bias[d], jnp.sum(low.astype(f32), axis=0, keepdims=True))
    small_part[shape.tower_out_bias : shape.tower_out_bias + 1, :] = bias_row

    wait_for_all()
    ways = orders()
    pieces, clock = [], [0]

    def pump():
        for piece in pieces:
            if not piece.done() and piece.sent_at < clock[0] - 2:
                piece.take()
                piece.sent_at = clock[0]
        clock[0] += 1

    def send(block, parts, inboxes, owns, totals, i, value):
        k = len(pieces)
        block.put(parts.at[i], value)
        piece = Piece(
            parts.at[i], inboxes.at[i], owns.at[i], totals.at[i], ways[k], own_sems.at[k], sends.at[k], recvs.at[k]
        )
        piece.send()
        piece.sent_at = clock[0]
        pieces.append(piece)

    towers = [jnp.dot(after_turned[...], d_tower[d], preferred_element_type=f32).astype(bf16) for d in range(DOMAINS)]
    send(blocks[2], part_tower, inbox_tower, own_tower, total_tower, 0, jnp.concatenate(towers, axis=0))
    d_after[...] = sum(
        lax.dot_general(d_tower[d], tower_in[d], NT, preferred_element_type=f32) for d in range(DOMAINS)
    )
    d_state[...] = d_after[...]

    products[...] = jnp.zeros(products.shape, f32)
    zero = jnp.zeros((1, depth), f32)
    half = units // 2
    for x in range(experts):

        def unmix(i, sums):
            at = stripe(i)
            d, value = d_after[at, :], standard[x, at, :].astype(f32)
            products[at, x : x + 1] = jnp.sum(d * (value * expert_gain[x : x + 1, :] + expert_bias[x : x + 1, :]), axis=1, keepdims=True)
            d = coef[at, x : x + 1] * d
            low = standardise_back(d * expert_gain[x : x + 1, :], value, inverse[at, x : x + 1]).astype(bf16)
            d_out[at, :] = low
            terms = (d * value, d, low.astype(f32))
            return tuple(s + jnp.sum(t, axis=0, keepdims=True) for s, t in zip(sums, terms))

        for place, row in zip((shape.gain[x], shape.bias[x], shape.b_out[x]),
                              lax.fori_loop(0, events // STRIPE, unmix, (zero,) * 3, unroll=2)):
            put_row(small_part, place, row)
        pump()
        for h in range(2):
            value = lax.dot_general(active[x, :, h * half : (h + 1) * half], d_out[...], TN, preferred_element_type=f32)
            send(blocks[1], part_out, inbox_out, own_out, total_out, 2 * x + h, value.astype(bf16))

        def unenter(c):
            at = pl.ds(pl.multiple_of(c * quarter, quarter), quarter)
            d = lax.dot_general(d_out[...], w_out[x, at, :], NT, preferred_element_type=f32)
            low = (d * slope[x, :, at].astype(f32)).astype(bf16)
            d_in[:, at] = low
            row = jnp.sum(low.astype(f32), axis=0, keepdims=True)
            for q in range(quarter // 128):
                small_part[pl.ds(shape.b_in[x] + c * (quarter // 128) + q, 1), :] = row[:, q * 128 : (q + 1) * 128]

        loop(units // quarter, unenter)
        for h in range(2):
            value = jnp.dot(state_turned[...], d_in[:, h * half : (h + 1) * half], preferred_element_type=f32)
            send(blocks[0], part_in, inbox_in, own_in, total_in, 2 * x + h, value.astype(bf16))

        def unstate(c):
            at = pl.ds(pl.multiple_of(c * quarter, quarter), quarter)
            d_state[:, at] += lax.dot_general(d_in[...], w_in[x, at, :], NT, preferred_element_type=f32)

        loop(depth // quarter, unstate)
        pump()

    ahead = counts.shape[0]

    def fetch(o):
        slot = o % ahead if isinstance(o, int) else lax.rem(o, ahead)
        return pltpu.make_async_copy(counts_hbm.at[o], counts.at[slot], count_sems.at[slot])

    for o in range(ahead):
        fetch(o).start()
    q = products[...].T
    q = [q[x : x + 1] for x in range(experts)]
    d_level = (share[0] * q[0] + share[1] * q[1], by_domain(which, q[SHARED:]))
    mean_share = share[0] * q[0] + share[1] * q[1]
    d_share = [level[0] * share[s] * (q[s] - mean_share) for s in range(SHARED)]
    mean_level = level[0] * d_level[0] + level[1] * d_level[1]
    d_group = [level[i] * (d_level[i] - mean_level) for i in range(2)]
    rows = d_share + [d_group[i] * here[d] for d in range(DOMAINS) for i in range(2)]
    d_logits = jnp.concatenate(rows + [jnp.zeros((GATE_ROWS - len(rows), events), f32)], axis=0)
    split = thirds(d_logits)
    gate_sums = jnp.dot(split, state_low[...], preferred_element_type=f32)
    gate_sums = sum(gate_sums[i * GATE_ROWS : (i + 1) * GATE_ROWS] for i in range(3))
    for i, place in enumerate(shape.gates):
        put_row(small_part, place, gate_sums[i : i + 1])
    gates_thrice = jnp.concatenate([gates[...]] * 3, axis=0)
    d_state[...] += lax.dot_general(split, gates_thrice, TN, preferred_element_type=f32)

    def unstart(i, sums):
        at = stripe(i)
        d, value = d_state[at, :], pre_standard[at, :]
        low = (standardise_back(d * inter_gain[...], value, pre_inverse[at, :]) * pre_slope[at, :]).astype(bf16)
        d_out[at, :] = low
        terms = (d * value, d, low.astype(f32))
        return tuple(s + jnp.sum(t, axis=0, keepdims=True) for s, t in zip(sums, terms))

    for place, row in zip((shape.inter_gain, shape.inter_bias, shape.proj_b),
                          lax.fori_loop(0, events // STRIPE, unstart, (zero,) * 3, unroll=2)):
        put_row(small_part, place, row)
    value = jnp.dot(joined[...], d_out[...], preferred_element_type=f32)
    send(blocks[3], part_proj, inbox_proj, own_proj, total_proj, 0, value.astype(bf16))
    n_all = n_field * width
    d_fields[:n_all, :] = lax.dot_general(proj_w[:n_all, :], d_out[...], NT, preferred_element_type=f32).astype(bf16)
    tail = lax.dot_general(proj_w[n_all:, :], d_out[...], NT, preferred_element_type=f32)
    d_pooled[...] = (tail[:width] / length).astype(bf16)
    d_centered[...] = tail[width:]
    lanes = lax.broadcasted_iota(i32, (width, 128), 1)
    sums = jnp.zeros((width, 128), f32)
    for d in range(DOMAINS):
        mine = jnp.where(which == d, tail[width:], 0.0)
        for k, term in enumerate((mine, mine * centered[...])):
            sums = jnp.where(lanes == k * DOMAINS + d, jnp.sum(term, axis=1, keepdims=True), sums)
    small_part[shape.dense : shape.dense + width, :] = sums
    if small_part.shape[0] > shape.next:
        small_part[shape.next :, :] = jnp.zeros((small_part.shape[0] - shape.next, 128), f32)
    k = len(pieces)
    small_piece = Piece(
        small_part, small_inbox, small_own, small_total, ways[0], own_sems.at[k], sends.at[k], recvs.at[k]
    )
    small_piece.send()
    small_piece.sent_at = clock[0]
    pieces.append(small_piece)
    pump()

    shift = cap.bit_length() - 1
    slot_total[...] = jnp.zeros(slot_total.shape, f32)

    def scatter(f, carry):
        wide, hots = [], []
        for k in range(2):
            slot = field[pl.ds(f * 2 + k, 1), :]
            owner = jnp.broadcast_to(jnp.right_shift(slot, shift), (width, events))
            d = d_fields[pl.ds(pl.multiple_of((f * 2 + k) * width, width), width), :].astype(f32)
            wide.append(
                jnp.concatenate([jnp.where(owner == o, d, 0.0).astype(bf16) for o in range(owners)], axis=0)
            )
            hots.append(hot(cap, jnp.bitwise_and(slot, cap - 1)))
        slot_total[...] += lax.dot_general(
            jnp.concatenate(wide, axis=1), jnp.concatenate(hots, axis=1), NT, preferred_element_type=f32
        )
        return carry

    for first in range(0, n_field // 2, 2):
        lax.fori_loop(first, min(first + 2, n_field // 2), scatter, 0)
        pump()

    def spread(o):
        fetch(o).wait()
        behave = jnp.dot(d_pooled[...], counts[lax.rem(o, ahead)], preferred_element_type=f32)
        at = pl.ds(pl.multiple_of(o * width, width), width)
        slot_grad[o] = (slot_total[at, :] + behave).astype(bf16)
        pl.when(o + ahead < owners)(lambda: fetch(o + ahead).start())

    for first in range(0, owners, owners // 8):

        def spread_some(o, carry):
            spread(o)
            return carry

        lax.fori_loop(first, first + owners // 8, spread_some, 0)
        pump()
    me = lax.axis_index("wide") * lax.axis_size("narrow") + lax.axis_index("narrow")
    slot_copies = []
    for d, other, place in everyone_else():
        copy = pltpu.make_async_remote_copy(
            src_ref=slot_grad.at[other], dst_ref=returned.at[me], send_sem=slot_sends.at[d],
            recv_sem=slot_recvs.at[d], device_id=place, device_id_type=MESH)
        copy.start()
        slot_copies.append(copy)
    returned[me] = slot_grad[me]

    while any(not piece.done() for piece in pieces):
        for piece in pieces:
            if not piece.done():
                piece.take()
    for copy in slot_copies:
        copy.wait_recv()
    for copy in slot_copies:
        copy.wait_send()
    for piece in pieces:
        piece.drain()


def learn(fields, pooled, lengths, dense, domains, cotangent, stats, model, field, counts, devices):
    w_in, tower_in, proj_w = model[4], model[12], model[0]
    experts, depth, units = w_in.shape
    width, events = dense.shape
    owners, _, cap = counts.shape
    tower_units = tower_in.shape[2]
    half = units // 2
    shape = Rows(experts, units, depth, tower_units, width)
    n_small = shape.padded(devices)
    blocks = [
        Block(depth, half, devices), Block(half, depth, devices),
        Block(DOMAINS * depth, tower_units, devices), Block(proj_w.shape[0], depth, devices),
    ]
    numbers = (2 * experts, 2 * experts, 1, 1)
    pieces = [(n, b.padded, b.lanes) for n, b in zip(numbers, blocks)]
    steps = 2 * (devices.bit_length() - 1)
    n_pieces = sum(numbers) + 1
    joined = proj_w.shape[0]
    ahead = max(4, min(16, 512 // devices))
    space = lambda *s: pltpu.VMEM(s, f32)
    low = lambda *s: pltpu.VMEM(s, bf16)
    dma = lambda *s: pltpu.SemaphoreType.DMA(s)
    in_specs = [vmem()] * 25
    in_specs[11] = in_specs[13] = in_specs[24] = hbm()
    out = pl.pallas_call(
        functools.partial(learn_kernel, shape, blocks),
        in_specs=in_specs,
        out_specs=[vmem()] * 4 + [hbm()] * 5,
        out_shape=[
            jax.ShapeDtypeStruct((1, events), f32),
            jax.ShapeDtypeStruct((width, events), f32),
            jax.ShapeDtypeStruct((width, events), f32),
            jax.ShapeDtypeStruct((owners, width, cap), bf16),
            jax.ShapeDtypeStruct((n_small, 128), f32),
        ]
        + [jax.ShapeDtypeStruct(s, bf16) for s in pieces],
        scratch_shapes=[
            low(experts, depth, units), low(experts, units, depth), low(joined, events),
            space(events, depth), space(events, depth), space(events, 1), low(events, depth),
            low(depth, events), space(events, 8), low(experts, events, units), low(experts, events, units),
            low(experts, events, depth), space(events, 8), space(events, depth), space(events, depth),
            low(events, depth), low(depth, events), low(DOMAINS, events, tower_units), space(events, depth),
            space(events, 8), low(events, depth), low(events, units), low(width, events), low(GATE_ROWS, depth), low(ahead, events, cap), space(owners * width, cap),
            low(owners, width, cap), space(n_small, 128), space(n_small, 128),
        ]
        + [pltpu.VMEM(s, bf16) for s in pieces] * 2
        + [space(n_small // devices, 128)]
        + [low(n, rows // devices, lanes) for n, rows, lanes in pieces]
        + [dma(experts), dma(experts), dma(ahead), dma(n_pieces), dma(n_pieces, steps), dma(n_pieces, steps), dma(devices), dma(devices)],
        compiler_params=params(collective_id=0, has_side_effects=True),
        name="learn",
    )(fields, pooled, lengths, dense, domains, cotangent, stats, *model, field, counts)
    return out[:5], [b.whole(t, n) for b, t, n in zip(blocks, out[5:], numbers)], shape


def get_row(small, at, n):
    return jnp.concatenate([small[at + c : at + c + 1, :] for c in range(n // 128)], axis=1)


def finish_kernel(shape, line, line_v, group, returned, domains, stats, centered, d_centered, small, *refs):
    more, out, more_out = refs[:4], refs[4], refs[5:9]
    d_dense, b_in, b_out, gain, bias, proj_b, inter_gain, inter_bias, shared_gate, group_gate, tower_in_bias, tower_out, tower_bias = refs[9:22]
    lines, vals = refs[22:]
    step = pl.program_id(0)
    per = out.shape[1] // ROW_CHUNK

    @pl.when(step == 0)
    def _():
        for target, places in (
            (b_in, shape.b_in), (b_out, shape.b_out), (gain, shape.gain), (bias, shape.bias),
            (proj_b, [shape.proj_b]), (inter_gain, [shape.inter_gain]), (inter_bias, [shape.inter_bias]),
            (shared_gate, shape.gates[:SHARED]), (tower_in_bias, shape.tower_in_bias), (tower_out, shape.tower_out),
        ):
            for i, at in enumerate(places):
                target[i : i + 1, :] = get_row(small, at, target.shape[1])
        for i, at in enumerate(shape.gates[SHARED:]):
            group_gate[i // 2, i % 2 : i % 2 + 1, :] = get_row(small, at, group_gate.shape[2])
        tower_bias[...] = small[shape.tower_out_bias : shape.tower_out_bias + 1, : tower_bias.shape[1]]
        which = domains[...]
        sums = small[shape.dense : shape.dense + centered.shape[0], :]
        moments = domain_moments(stats[...])
        scale = by_domain(which, [m[1] for m in moments])
        straight = by_domain(which, [sums[:, d : d + 1] / m[2] for d, m in enumerate(moments)])
        cross = by_domain(which, [sums[:, DOMAINS + d : DOMAINS + d + 1] / m[2] for d, m in enumerate(moments)])
        d_dense[...] = scale * (d_centered[...] - straight - centered[...] * cross)

        def clear(i, carry):
            lines[pl.ds(pl.multiple_of(i * 1024, 1024), 1024), :] = jnp.zeros((1024, 128), f32)
            return carry

        lax.fori_loop(0, lines.shape[0] // 1024, clear, 0)

    width, cap = returned.shape[1:]

    @pl.when(step < ADD_STEPS)
    def _():
        batch = 32
        a = lax.div(lax.broadcasted_iota(i32, (cap, cap), 0), batch)
        near = a == lax.div(lax.broadcasted_iota(i32, (cap, cap), 1), batch)
        each = group.shape[0] // ADD_STEPS

        def prepare(s, slot):
            which, own = jnp.broadcast_to(group[s], (width, cap)), returned[s].astype(f32)
            wide = jnp.concatenate([jnp.where(which == g, own, 0.0) for g in range(8)], axis=0)
            along = jnp.broadcast_to(line_v[s].astype(f32), (cap, cap))
            same = jnp.where(jnp.logical_and(along == along.T, near), 1.0, 0.0).astype(bf16)
            vals[slot] = lax.dot_general(same, wide.astype(bf16), NT, preferred_element_type=f32)

        def add(s, slot):
            for u in range(0, cap, batch):
                places, sums = [], []
                for j in range(u, u + batch):
                    places.append(line[s * cap + j])
                    sums.append(lines[pl.ds(places[-1], 1), :] + vals[slot, j : j + 1, :])
                for place, total in zip(places, sums):
                    lines[pl.ds(place, 1), :] = total

        prepare(step * each, 0)

        def serve(i, carry):
            s = step * each + i * 2
            prepare(s + 1, 1)
            add(s, 0)
            prepare(jnp.minimum(s + 2, group.shape[0] - 1), 0)
            add(s + 1, 1)
            return carry

        lax.fori_loop(0, each // 2, serve, 0)
        for source, target in zip(more, more_out):
            tall, blocks, rows, lanes = source.shape
            for s in range(tall):
                for c in range(blocks):
                    target[s * rows : (s + 1) * rows, c * lanes : (c + 1) * lanes] = source[s, c].astype(f32)

    @pl.when(step >= ADD_STEPS)
    def _():
        def turn(c, carry):
            at = pl.multiple_of(((step - ADD_STEPS) * per + c) * 128, 128)
            turned = lines[pl.ds(at, 128), :].T
            for g in range(8):
                at = pl.multiple_of(c * ROW_CHUNK + g * 128, 128)
                out[:, pl.ds(at, 128)] = turned[g * width : (g + 1) * width]
            return carry

        lax.fori_loop(0, per, turn, 0, unroll=4)


def finish(shape, line, group, returned, domains, stats, centered, d_centered, small, more, rows):
    blocks, width, cap = returned.shape
    events = centered.shape[1]
    experts, units, depth = len(shape.b_in), more[0].shape[1] * more[0].shape[3], more[0].shape[2]
    tower = more[2].shape[1] * more[2].shape[3]
    steps, turns = ADD_STEPS, 4
    early = lambda i: jnp.minimum(i, steps - 1)
    in_more, out_more, shapes = [], [], []
    for x in more:
        tall, parts, r, lanes = x.shape
        if tall > 1:
            in_more.append(pl.BlockSpec((tall // steps, parts, r, lanes), lambda i: (early(i), 0, 0, 0)))
        else:
            in_more.append(pl.BlockSpec((1, parts, r // steps, lanes), lambda i: (0, 0, early(i), 0)))
        out_more.append(pl.BlockSpec((tall * r // steps, parts * lanes), lambda i: (early(i), 0)))
        shapes.append((tall * r, parts * lanes))
    shapes += [(width, events), (experts, units)] + [(experts, depth)] * 3 + [(1, depth)] * 3
    shapes += [(SHARED, depth), (DOMAINS, 2, depth), (DOMAINS, tower), (DOMAINS, tower), (1, DOMAINS)]
    return pl.pallas_call(
        functools.partial(finish_kernel, shape),
        grid=(steps + turns,),
        in_specs=[smem()] + [vmem()] * 8 + in_more,
        out_specs=[pl.BlockSpec((width, rows // turns), lambda i: (0, jnp.maximum(i - steps, 0)))] + out_more + [vmem()] * 13,
        out_shape=[jax.ShapeDtypeStruct(s, f32) for s in [(width, rows)] + shapes],
        scratch_shapes=[pltpu.VMEM((rows // 8, 128), f32), pltpu.VMEM((2, cap, 128), f32)],
        compiler_params=params(),
        name="finish",
    )(line.reshape(-1), line, group, returned, domains, stats, centered, d_centered, small, *more)


def local(
    table,
    dense,
    domains,
    lengths,
    requests,
    counts,
    field_slots,
    behave_slots,
    proj_w,
    proj_b,
    inter_gain,
    inter_bias,
    w_in,
    b_in,
    w_out,
    b_out,
    expert_gain,
    expert_bias,
    shared_gate,
    group_gate,
    tower_in,
    tower_in_bias,
    tower_out,
    tower_out_bias,
    pred_cotangent,
):
    devices = lax.axis_size("wide") * lax.axis_size("narrow")
    capacity = requests.shape[2]
    experts, depth, units = w_in.shape
    counts_of = slot_counts(lengths, behave_slots.reshape(-1, 128), devices, capacity)
    field = field_slots.T
    dense_t, which = dense.T, domains[None]
    fields, pooled, line, group, stats = lookup(
        requests[0], table.T, counts.reshape(-1), field, counts_of, dense_t, which
    )
    model = (
        proj_w, proj_b[None], inter_gain[None], inter_bias[None], w_in, b_in, w_out, b_out, expert_gain, expert_bias,
        shared_gate.T, group_gate.transpose(0, 2, 1), tower_in, tower_in_bias, tower_out, tower_out_bias[None],
    )
    (pred, centered, d_centered, returned, small), totals, shape = learn(
        fields, pooled, lengths, dense_t, which, pred_cotangent[None], stats, model, field, counts_of, devices
    )
    totals[0] = totals[0].reshape(experts, -1, depth, totals[0].shape[3])
    out = finish(shape, line, group, returned, which, stats, centered, d_centered, small, totals, table.shape[0])
    d_table, d_w_in, d_w_out, d_tower_in, d_proj_w, d_dense, d_b_in, d_b_out, d_gain, d_bias = out[:10]
    d_proj_b, d_inter_gain, d_inter_bias, d_shared_gate, d_group_gate, d_tower_in_bias, d_tower_out, d_tower_bias = out[10:]
    return (
        pred[0],
        d_dense.T,
        d_table.T,
        d_proj_w,
        d_proj_b[0],
        d_inter_gain[0],
        d_inter_bias[0],
        d_w_in.reshape(w_in.shape),
        d_b_in,
        d_w_out.reshape(w_out.shape),
        d_b_out,
        d_gain,
        d_bias,
        d_shared_gate.T,
        d_group_gate.transpose(0, 2, 1),
        d_tower_in.reshape(tower_in.shape),
        d_tower_in_bias,
        d_tower_out,
        d_tower_bias[0],
    )


def solution(mesh):
    placed = (
        P(("wide", "narrow"), None),
        P(("wide", "narrow"), None),
        P(("wide", "narrow")),
        P(("wide", "narrow"), None),
        P(("wide", "narrow"), None, None),
        P(("wide", "narrow"), None),
        P(("wide", "narrow"), None),
        P(("wide", "narrow"), None),
        P(),
        P(),
        P(),
        P(),
        P(),
        P(),
        P(),
        P(),
        P(),
        P(),
        P(),
        P(),
        P(),
        P(),
        P(),
        P(),
        P(("wide", "narrow")),
    )
    return jax.shard_map(
        local,
        mesh=mesh,
        in_specs=placed,
        out_specs=(
            P(("wide", "narrow")),
            P(("wide", "narrow"), None),
            P(("wide", "narrow"), None),
            P(),
            P(),
            P(),
            P(),
            P(),
            P(),
            P(),
            P(),
            P(),
            P(),
            P(),
            P(),
            P(),
            P(),
            P(),
            P(),
        ),
        check_vma=False,
    )
```

```python
import functools
import math

import jax
import jax.numpy as jnp
from jax import lax
from jax.experimental import pallas as pl
from jax.experimental.pallas import tpu as pltpu
from jax.sharding import PartitionSpec as P

SHARED = 2
DOMAINS = 2

EPSILON = 1e-05

f32 = jnp.float32
bf16 = jnp.bfloat16
i32 = jnp.int32
MESH = pl.DeviceIdType.MESH
AXES = ("wide", "narrow")
NT = (((1,), (1,)), ((), ()))
TN = (((0,), (0,)), ((), ()))
VMEM_LIMIT = 60 * 1024 * 1024
ROW_CHUNK = 1024
GROUP = 8
SPAN = 6
BUNCH = 4
ADD_STEPS = 4


def vmem():
    return pl.BlockSpec(memory_space=pltpu.VMEM)


def smem():
    return pl.BlockSpec(memory_space=pltpu.SMEM)


def hbm():
    return pl.BlockSpec(memory_space=pl.ANY)


def params(**more):
    return pltpu.CompilerParams(vmem_limit_bytes=VMEM_LIMIT, **more)


def line_of(rows):
    return jnp.left_shift(jnp.right_shift(rows, 10), 7) + jnp.bitwise_and(rows, 127)


def lane_group_of(rows):
    return jnp.bitwise_and(jnp.right_shift(rows, 7), 7)


def identity(n):
    return (lax.broadcasted_iota(i32, (n, n), 0) == lax.broadcasted_iota(i32, (n, n), 1)).astype(bf16)


def hot(rows, index):
    column = lax.broadcasted_iota(i32, (rows, index.shape[1]), 0)
    return jnp.where(column == index, 1.0, 0.0).astype(bf16)


def count_kernel(lengths, behave, counts, sums, done):
    owners, _, cap = counts.shape
    shift = cap.bit_length() - 1
    step = pl.program_id(0)
    place = lax.broadcasted_iota(i32, (SPAN, 128), 0) * 128 + lax.broadcasted_iota(i32, (SPAN, 128), 1)
    last_block = behave.shape[0] - SPAN
    ends = [jnp.where(step == 0, 0, done[0])]
    for i in range(BUNCH * GROUP):
        ends.append(ends[-1] + lengths[0, step * (BUNCH * GROUP) + i])
    done[0] = ends[-1]

    def part(k, m):
        cuts = ends[k * GROUP : (k + 1) * GROUP + 1]
        begin = lax.div(cuts[0], 128) + m * SPAN
        b = jnp.minimum(begin, last_block)
        slot = behave[pl.ds(b, SPAN), :]
        p = place + b * 128
        event = jnp.zeros_like(p)
        for cut in cuts[1:-1]:
            event = event + jnp.where(p >= cut, 1, 0)
        mine = jnp.logical_and(jnp.logical_and(p >= cuts[0], p < cuts[-1]), p >= begin * 128)
        key = jnp.where(mine, jnp.right_shift(slot, shift) * GROUP + event, -1)
        low = jnp.bitwise_and(slot, cap - 1)
        left = jnp.concatenate([hot(owners * GROUP, key[q : q + 1]) for q in range(SPAN)], axis=1)
        right = jnp.concatenate([hot(cap, low[q : q + 1]) for q in range(SPAN)], axis=1)
        return lax.dot_general(left, right, NT, preferred_element_type=f32)

    parts = []
    for k in range(BUNCH):
        sums[k] = part(k, 0)
        first, last = ends[k * GROUP], ends[(k + 1) * GROUP]
        parts.append(lax.div(last - lax.div(first, 128) * 128 + (SPAN * 128 - 1), SPAN * 128))
    most = functools.reduce(jnp.maximum, parts)

    @pl.when(most > 1)
    def _():
        for k in range(BUNCH):

            def more(m, carry):
                sums[k] += part(k, m)
                return carry

            lax.fori_loop(1, parts[k], more, 0)

    for t in range(BUNCH // 2):
        for o in range(owners):
            both = [sums[2 * t + k, o * GROUP : (o + 1) * GROUP, :] for k in range(2)]
            counts[o, t * 2 * GROUP : (t + 1) * 2 * GROUP, :] = jnp.concatenate(both, axis=0).astype(bf16)


def slot_counts(lengths, behave, owners, cap):
    events = lengths.shape[1]
    size = BUNCH * GROUP
    return pl.pallas_call(
        count_kernel,
        grid=(events // size,),
        in_specs=[smem(), vmem()],
        out_specs=pl.BlockSpec((owners, size, cap), lambda i: (0, i, 0)),
        out_shape=jax.ShapeDtypeStruct((owners, events, cap), bf16),
        scratch_shapes=[pltpu.VMEM((BUNCH, owners * GROUP, cap), f32), pltpu.SMEM((1,), i32)],
        compiler_params=params(),
        name="slot_counts",
    )(lengths, behave)


def place_bits():
    return [(axis, b) for axis in AXES for b in range(lax.axis_size(axis).bit_length() - 1)]


def bit_value(bit):
    return jnp.bitwise_and(jnp.right_shift(lax.axis_index(bit[0]), bit[1]), 1)


def across(bit):
    axis, b = bit
    place = {a: lax.axis_index(a) for a in AXES}
    place[axis] = place[axis] + (1 - 2 * bit_value(bit)) * (1 << b)
    return tuple(place[a] for a in AXES)


class Piece:
    def __init__(self, part, inbox, own, total, order, own_sem, sends, recvs):
        self.part, self.inbox, self.own, self.total = part, inbox, own, total
        self.order, self.own_sem, self.sends, self.recvs = order, own_sem, sends, recvs
        self.rows = part.shape[0]
        self.grain = self.rows >> len(order)
        self.offsets, self.copies, self.taken = [0], [], 0

    def at(self, ref, offset, n):
        return ref.at[pl.ds(pl.multiple_of(offset, self.grain), n)]

    def keep(self):
        return pltpu.make_async_copy(self.own, self.at(self.total, self.offsets[-1], self.grain), self.own_sem)

    def send(self):
        k, depth = len(self.copies), len(self.order)
        if k < depth:
            bit, half = self.order[k], self.rows >> (k + 1)
            value, offset = bit_value(bit), self.offsets[k]
            self.offsets.append(offset + value * half)
            source = self.at(self.part, offset + (1 - value) * half, half)
            target = self.inbox.at[pl.ds(self.rows - (self.rows >> k), half)]
        else:
            s = 2 * depth - 1 - k
            bit = self.order[s]
            target = self.at(self.total, self.offsets[s + 1], self.rows >> (s + 1))
            source = self.own if k == depth else target
        copy = pltpu.make_async_remote_copy(
            src_ref=source,
            dst_ref=target,
            send_sem=self.sends.at[k],
            recv_sem=self.recvs.at[k],
            device_id=across(bit),
            device_id_type=MESH,
        )
        copy.start()
        self.copies.append(copy)

    def done(self):
        return self.taken == 2 * len(self.order)

    def take(self):
        k, depth = self.taken, len(self.order)
        self.copies[k].wait_recv()
        self.taken += 1
        if k < depth:
            n, base, offset = self.rows >> (k + 1), self.rows - (self.rows >> k), self.offsets[k + 1]
            chunk = math.gcd(n, 64)

            def add(i, carry):
                at = pl.ds(pl.multiple_of(offset + i * chunk, math.gcd(self.grain, chunk)), chunk)
                came = pl.ds(pl.multiple_of(base + i * chunk, chunk), chunk)
                total = (self.part[at, :].astype(f32) + self.inbox[came, :].astype(f32)).astype(self.part.dtype)
                if k == depth - 1:
                    self.own[pl.ds(pl.multiple_of(i * chunk, chunk), chunk), :] = total
                else:
                    self.part[at, :] = total
                return carry

            lax.fori_loop(0, n // chunk, add, 0)
        if k == depth - 1:
            self.keep().start()
        if k == depth:
            self.keep().wait()
        if not self.done():
            self.send()

    def drain(self):
        for copy in self.copies:
            copy.wait_send()


def peer(d):
    n_wide, n_narrow = (lax.axis_size(a) for a in AXES)
    w, n = (lax.axis_index(a) for a in AXES)
    other = jnp.bitwise_and(w * n_narrow + n + d, n_wide * n_narrow - 1)
    return other, (jnp.right_shift(other, n_narrow.bit_length() - 1), jnp.bitwise_and(other, n_narrow - 1))


def everyone_else():
    for d in range(1, lax.axis_size("wide") * lax.axis_size("narrow")):
        yield (d,) + peer(d)


def greet_all():
    barrier = pltpu.get_barrier_semaphore()
    for _, _, place in everyone_else():
        pl.semaphore_signal(barrier, inc=1, device_id=place, device_id_type=MESH)


def wait_for_all():
    pl.semaphore_wait(pltpu.get_barrier_semaphore(), lax.axis_size("wide") * lax.axis_size("narrow") - 1)


def meet_all():
    greet_all()
    wait_for_all()


def lanes_of(rows, columns, devices):
    lanes = columns
    while lanes > 128 and (rows * (columns // lanes)) % (16 * devices):
        lanes //= 2
    return lanes


ORDERS = "BABGABDABAGBABDABA"


class Block:
    def __init__(self, rows, columns, devices):
        self.rows, self.columns = rows, columns
        self.lanes = lanes_of(rows, columns, devices)
        self.blocks = columns // self.lanes
        self.padded = -(-rows * self.blocks // (16 * devices)) * 16 * devices

    def put(self, piece, value):
        for c in range(self.blocks):
            piece[c * self.rows : (c + 1) * self.rows, :] = value[:, c * self.lanes : (c + 1) * self.lanes]
        extra = self.padded - self.rows * self.blocks
        if extra:
            piece[self.rows * self.blocks :, :] = jnp.zeros((extra, self.lanes), piece.dtype)

    def whole(self, total, n):
        return total[:, : self.rows * self.blocks].reshape(n, self.blocks, self.rows, self.lanes)


def orders():
    if tuple(lax.axis_size(a) for a in AXES) != (8, 4):
        return [place_bits()] * len(ORDERS)
    core, y, x, z0, z1 = ("narrow", 0), ("narrow", 1), ("wide", 0), ("wide", 1), ("wide", 2)
    ways = {
        "A": [core, x, y, z0, z1],
        "B": [core, y, x, z0, z1],
        "D": [core, z0, z1, y, x],
        "G": [core, z0, z1, x, y],
    }
    return [ways[way] for way in ORDERS]


def lookup_kernel(
    requests_in, table, live, field, counts_hbm, dense, domains,
    fields, pooled, line_out, group, stats_out,
    requests, counts, tab, lines, got, line, line_smem, found, rows, slots, stats, stats_in,
    tab_sems, counts_sem, line_sem, ask_sends, ask_recvs, row_sends, row_recvs, stat_sends, stat_recvs,
):
    owners, _, cap = requests.shape
    width = tab.shape[0]
    n_field, events = field.shape
    chunks = tab_sems.shape[0]
    part = tab.shape[1] // chunks
    me = lax.axis_index("wide") * lax.axis_size("narrow") + lax.axis_index("narrow")

    loads = []
    for c in range(chunks):
        at = pl.ds(c * part, part)
        loads.append(pltpu.make_async_copy(table.at[:, at], tab.at[:, at], tab_sems.at[c]))
        loads[-1].start()
    load_counts = pltpu.make_async_copy(counts_hbm, counts, counts_sem)
    load_counts.start()
    for o in range(owners):
        requests[o] = requests_in[o : o + 1, :]
    lane = lax.broadcasted_iota(i32, (width, 128), 1)
    mine = jnp.zeros((width, 128), f32)
    for d in range(DOMAINS):
        here = domains[...] == d
        value = jnp.where(here, dense[...], 0.0)
        one = jnp.broadcast_to(jnp.where(here, 1.0, 0.0), value.shape)
        for k, term in enumerate((value, value * value, one)):
            mine = jnp.where(lane == k * DOMAINS + d, jnp.sum(term, axis=1, keepdims=True), mine)
    stats[...] = mine

    meet_all()

    def ask(d):
        other, place = peer(d)
        return pltpu.make_async_remote_copy(
            src_ref=requests.at[other], dst_ref=line.at[me], send_sem=ask_sends.at[d],
            recv_sem=ask_recvs.at[d], device_id=place, device_id_type=MESH)

    def tell(d):
        _, place = peer(d)
        return pltpu.make_async_remote_copy(
            src_ref=stats, dst_ref=stats_in.at[me], send_sem=stat_sends.at[d],
            recv_sem=stat_recvs.at[d], device_id=place, device_id_type=MESH)

    def answer(d):
        other, place = peer(d)
        return pltpu.make_async_remote_copy(
            src_ref=found.at[other], dst_ref=rows.at[me], send_sem=row_sends.at[d],
            recv_sem=row_recvs.at[d], device_id=place, device_id_type=MESH)

    def each(first, act):
        def step(d, carry):
            act(d)
            return carry

        lax.fori_loop(first, owners, step, 0)

    each(1, lambda d: ask(d).start())
    each(1, lambda d: tell(d).start())
    line[me] = requests[me]
    stats_in[me] = stats[...]

    eye = identity(128)
    for c in range(chunks):
        loads[c].wait()

        def turn(i, carry):
            base = pl.multiple_of(c * part + i * ROW_CHUNK, ROW_CHUNK)
            stack = jnp.concatenate([tab[:, pl.ds(base + g * 128, 128)] for g in range(8)], axis=0)
            at = pl.multiple_of((c * part // ROW_CHUNK + i) * 128, 128)
            lines[pl.ds(at, 128), :] = lax.dot_general(eye, stack, NT, preferred_element_type=f32)
            return carry

        lax.fori_loop(0, part // ROW_CHUNK, turn, 0, unroll=8)

    each(1, lambda d: ask(d).wait_recv())
    group[...] = lane_group_of(line[...])
    line_out[...] = line_of(line[...])
    to_smem = pltpu.make_async_copy(line_out, line_smem, line_sem)
    to_smem.start()
    to_smem.wait()

    def source(d):
        return peer(d)[0]

    def fetch(d):
        s, half = source(d), jnp.bitwise_and(d, 1) * cap
        for j in range(cap):
            got[pl.ds(half + j, 1), :] = lines[pl.ds(line_smem[s, 0, j], 1), :]

    def turn_out(d):
        s, half = source(d), pl.multiple_of(jnp.bitwise_and(d, 1) * cap, cap)
        turned = lax.dot_general(eye, got[pl.ds(half, cap), :].astype(bf16), NT, preferred_element_type=f32)
        which = jnp.broadcast_to(group[s], (width, cap))
        picked = turned[:width]
        for g in range(1, 8):
            picked = jnp.where(which == g, turned[g * width : (g + 1) * width], picked)
        found[s] = picked.astype(bf16)

    fetch(0)

    def serve(d, carry):
        turn_out(d - 1)
        fetch(d)
        pl.when(d > 1)(lambda: answer(d - 1).start())
        return carry

    lax.fori_loop(1, owners, serve, 0)
    turn_out(owners - 1)
    answer(owners - 1).start()
    rows[me] = found[me]
    each(1, lambda d: tell(d).wait_recv())
    total = stats_in[0]
    for o in range(1, owners):
        total = total + stats_in[o]
    stats_out[...] = total

    each(1, lambda d: answer(d).wait_recv())
    shift = cap.bit_length() - 1
    column = lax.broadcasted_iota(i32, (width, cap), 1)
    for o in range(owners):
        slots[o * width : (o + 1) * width, :] = jnp.where(column < live[o], rows[o].astype(f32), 0.0).astype(bf16)

    def one(f, carry):
        slot = field[pl.ds(f, 1), :]
        owner = jnp.broadcast_to(jnp.right_shift(slot, shift), (width, events))
        all_owners = jnp.dot(slots[...], hot(cap, jnp.bitwise_and(slot, cap - 1)), preferred_element_type=f32)
        picked = all_owners[:width]
        for o in range(1, owners):
            picked = jnp.where(owner == o, all_owners[o * width : (o + 1) * width], picked)
        fields[pl.ds(pl.multiple_of(f * width, width), width), :] = picked.astype(bf16)
        return carry

    lax.fori_loop(0, n_field, one, 0, unroll=4)
    load_counts.wait()
    total = jnp.zeros((events, width), f32)
    for o in range(owners):
        total = total + lax.dot_general(counts[o], slots[o * width : (o + 1) * width, :], NT, preferred_element_type=f32)
    pooled[...] = total.T
    each(1, lambda d: ask(d).wait_send())
    each(1, lambda d: tell(d).wait_send())
    each(1, lambda d: answer(d).wait_send())


def lookup(requests, table_t, live, field_t, counts, dense_t, domains):
    owners, cap = requests.shape
    width, rows = table_t.shape
    n_field, events = field_t.shape
    chunks = 6
    dma = pltpu.SemaphoreType.DMA
    return pl.pallas_call(
        lookup_kernel,
        in_specs=[vmem(), hbm(), smem(), vmem(), hbm(), vmem(), vmem()],
        out_specs=[vmem()] * 5,
        out_shape=[
            jax.ShapeDtypeStruct((n_field * width, events), bf16),
            jax.ShapeDtypeStruct((width, events), f32),
            jax.ShapeDtypeStruct((owners, 1, cap), i32),
            jax.ShapeDtypeStruct((owners, 1, cap), i32),
            jax.ShapeDtypeStruct((width, 128), f32),
        ],
        scratch_shapes=[
            pltpu.VMEM((owners, 1, cap), i32),
            pltpu.VMEM((owners, events, cap), bf16),
            pltpu.VMEM((width, rows), bf16),
            pltpu.VMEM((rows // 8, 128), f32),
            pltpu.VMEM((2 * cap, 128), f32),
            pltpu.VMEM((owners, 1, cap), i32),
            pltpu.SMEM((owners, 1, cap), i32),
            pltpu.VMEM((owners, width, cap), bf16),
            pltpu.VMEM((owners, width, cap), bf16),
            pltpu.VMEM((owners * width, cap), bf16),
            pltpu.VMEM((width, 128), f32),
            pltpu.VMEM((owners, width, 128), f32),
            dma((chunks,)),
            dma,
            dma,
        ]
        + [dma((owners,))] * 6,
        compiler_params=params(collective_id=1, has_side_effects=True),
        name="lookup",
    )(requests, table_t, live, field_t, counts, dense_t, domains)


STRIPE = 128
GATE_ROWS = 16
GELU_SCALE = math.sqrt(2.0 / math.pi)
GELU_CUBE = 0.044715


def gelu_and_slope(x):
    square = x * x
    t = jnp.tanh(GELU_SCALE * (x + GELU_CUBE * (square * x)))
    half = 0.5 * (1.0 + t)
    return x * half, half + 0.5 * x * (1.0 - t * t) * (GELU_SCALE * (1.0 + 3.0 * GELU_CUBE * square))


def standardise(values):
    center = values - jnp.mean(values, axis=-1, keepdims=True)
    inverse = lax.rsqrt(jnp.mean(center * center, axis=-1, keepdims=True) + EPSILON)
    return center * inverse, inverse


def standardise_back(d, standard, inverse):
    along = jnp.mean(d * standard, axis=-1, keepdims=True)
    return inverse * (d - jnp.mean(d, axis=-1, keepdims=True) - standard * along)


def loop(n, body):
    def step(i, carry):
        body(i)
        return carry

    lax.fori_loop(0, n, step, 0, unroll=2)


def columns(rows):
    have = rows.shape[0]
    if have < 8:
        rows = jnp.concatenate([rows, jnp.zeros((8 - have, rows.shape[1]), f32)], axis=0)
    return rows.T


def thirds(x):
    high = x.astype(bf16)
    rest = x - high.astype(f32)
    middle = rest.astype(bf16)
    return jnp.concatenate([high, middle, (rest - middle.astype(f32)).astype(bf16)], axis=0)


def domain_moments(stats):
    result = []
    for d in range(DOMAINS):
        count = stats[:, 2 * DOMAINS + d : 2 * DOMAINS + d + 1]
        mean = stats[:, d : d + 1] / count
        variance = stats[:, DOMAINS + d : DOMAINS + d + 1] / count - mean * mean
        result.append((mean, lax.rsqrt(variance + EPSILON), count))
    return result


def by_domain(domains, values):
    picked = values[0]
    for d in range(1, DOMAINS):
        picked = jnp.where(domains == d, values[d], picked)
    return picked


class Rows:
    def __init__(self, experts, units, depth, tower, width):
        self.next = 0
        lines = lambda n: -(-n // 128)
        self.b_in = [self.take(lines(units)) for _ in range(experts)]
        self.b_out, self.gain, self.bias = ([self.take(lines(depth)) for _ in range(experts)] for _ in range(3))
        self.proj_b, self.inter_gain, self.inter_bias = (self.take(lines(depth)) for _ in range(3))
        self.gates = [self.take(lines(depth)) for _ in range(SHARED + 2 * DOMAINS)]
        self.tower_in_bias, self.tower_out = ([self.take(lines(tower)) for _ in range(DOMAINS)] for _ in range(2))
        self.tower_out_bias = self.take(1)
        self.dense = self.take(width)

    def take(self, n):
        at, self.next = self.next, self.next + n
        return at

    def padded(self, devices):
        return -(-self.next // (8 * devices)) * 8 * devices


def put_row(small, at, row):
    for c in range(row.shape[1] // 128):
        small[at + c : at + c + 1, :] = row[:, c * 128 : (c + 1) * 128]


def learn_kernel(
    shape, blocks,
    fields, pooled, lengths, dense, domains, cotangent, stats, proj_w, proj_b, inter_gain, inter_bias,
    w_in_hbm, b_in, w_out_hbm, b_out, expert_gain, expert_bias, shared_gate, group_gate, tower_in, tower_in_bias, tower_out,
    tower_out_bias, field, counts_hbm,
    pred, centered, d_centered, returned, small_total, total_in, total_out, total_tower, total_proj,
    w_in, w_out, joined, pre_slope, pre_standard, pre_inverse, state_low, state_turned, coef,
    active, slope, standard, inverse, work, after, after_low, after_turned, d_tower, d_after, products,
    d_out, d_in, d_pooled, gates, counts, slot_total, slot_grad,
    small_part, small_inbox, part_in, part_out, part_tower, part_proj, inbox_in, inbox_out, inbox_tower, inbox_proj,
    small_own, own_in, own_out, own_tower, own_proj, in_sems, out_sems, count_sems, own_sems, sends, recvs, slot_sends, slot_recvs,
):
    experts, depth, units = w_in.shape
    width, events = dense.shape
    n_field = field.shape[0]
    owners, _, cap = slot_grad.shape
    tower_units = tower_in.shape[2]
    greet_all()
    for x in range(experts):
        pltpu.make_async_copy(w_in_hbm.at[x], w_in.at[x], in_sems.at[x]).start()
        pltpu.make_async_copy(w_out_hbm.at[x], w_out.at[x], out_sems.at[x]).start()

    which = domains[...]
    length = lengths[...].astype(f32)
    rows = [shared_gate[...].astype(f32)] + [group_gate[d].astype(f32) for d in range(DOMAINS)]
    have = SHARED + 2 * DOMAINS
    gates[...] = jnp.concatenate(rows + [jnp.zeros((GATE_ROWS - have, depth), f32)], axis=0).astype(bf16)
    moments = domain_moments(stats[...])
    mean, scale = (by_domain(which, [m[i] for m in moments]) for i in range(2))
    centered[...] = (dense[...] - mean) * scale
    joined[: n_field * width, :] = fields[...]
    joined[n_field * width : (n_field + 1) * width, :] = (pooled[...] / length).astype(bf16)
    joined[(n_field + 1) * width :, :] = centered[...].astype(bf16)
    joined_rows, d_state, d_fields = d_in.at[:, : joined.shape[0]], after, joined
    joined_rows[...] = joined[...].T
    quarter = 256

    def project(c):
        at = pl.ds(pl.multiple_of(c * quarter, quarter), quarter)
        work[:, at] = jnp.dot(joined_rows[...], proj_w[:, at], preferred_element_type=f32) + proj_b[:, at]

    loop(depth // quarter, project)

    def stripe(i):
        return pl.ds(pl.multiple_of(i * STRIPE, STRIPE), STRIPE)

    def start_state(i):
        at = stripe(i)
        value, pre_slope[at, :] = gelu_and_slope(work[at, :])
        pre_standard[at, :], pre_inverse[at, :] = standardise(value)
        state = pre_standard[at, :] * inter_gain[...] + inter_bias[...]
        after[at, :] = state
        state_low[at, :] = state.astype(bf16)

    loop(events // STRIPE, start_state)
    state_turned[...] = state_low[...].T
    logits = lax.dot_general(gates[...], state_low[...], NT, preferred_element_type=f32)

    def softmax_pair(a, b):
        top = jnp.maximum(a, b)
        a, b = jnp.exp(a - top), jnp.exp(b - top)
        return a / (a + b), b / (a + b)

    share = softmax_pair(logits[0:1], logits[1:2])
    group_logits = [
        by_domain(which, [logits[SHARED + 2 * d + i : SHARED + 2 * d + i + 1] for d in range(DOMAINS)]) for i in range(2)
    ]
    level = softmax_pair(*group_logits)
    here = [jnp.where(which == d, 1.0, 0.0) for d in range(DOMAINS)]
    weights = [level[0] * share[0], level[0] * share[1]] + [level[1] * here[d] for d in range(DOMAINS)]
    weight_columns = columns(jnp.concatenate(weights, axis=0))
    coef[...] = weight_columns

    def expert_forward(x):
        pltpu.make_async_copy(w_in_hbm.at[x], w_in.at[x], in_sems.at[x]).wait()

        def enter(c):
            at = pl.ds(pl.multiple_of(c * quarter, quarter), quarter)
            pre = jnp.dot(state_low[...], w_in[x, :, at], preferred_element_type=f32) + b_in[x : x + 1, at]
            value, rise = gelu_and_slope(pre)
            active[x, :, at] = value.astype(bf16)
            slope[x, :, at] = rise.astype(bf16)

        loop(units // quarter, enter)
        pltpu.make_async_copy(w_out_hbm.at[x], w_out.at[x], out_sems.at[x]).wait()

        def leave(c):
            at = pl.ds(pl.multiple_of(c * quarter, quarter), quarter)
            work[:, at] = jnp.dot(active[x], w_out[x, :, at], preferred_element_type=f32) + b_out[x : x + 1, at]

        loop(depth // quarter, leave)

        def mix(i):
            at = stripe(i)
            value, inverse[at, x : x + 1] = standardise(work[at, :])
            standard[x, at, :] = value.astype(bf16)
            after[at, :] += coef[at, x : x + 1] * (value * expert_gain[x : x + 1, :] + expert_bias[x : x + 1, :])

        loop(events // STRIPE, mix)

    for x in range(experts):
        expert_forward(x)
    after_low[...] = after[...].astype(bf16)
    after_turned[...] = after_low[...].T

    here_columns = columns(jnp.concatenate(here + [cotangent[...]], axis=0))
    logit = jnp.zeros((events, 1), f32)
    for d in range(DOMAINS):
        pre = jnp.dot(after_low[...], tower_in[d], preferred_element_type=f32) + tower_in_bias[d : d + 1, :]
        value, rise = gelu_and_slope(pre)
        work[:, d * tower_units : (d + 1) * tower_units] = value
        d_after[:, d * tower_units : (d + 1) * tower_units] = rise
        head = jnp.sum(value * tower_out[d : d + 1, :], axis=1, keepdims=True) + tower_out_bias[:, d : d + 1]
        logit = logit + here_columns[:, d : d + 1] * head
    chance = 1.0 / (1.0 + jnp.exp(-logit))
    d_logit = here_columns[:, DOMAINS : DOMAINS + 1] * chance * (1.0 - chance)
    pred[...] = jnp.broadcast_to(chance, (events, 8)).T[0:1, :]
    lane = lax.broadcasted_iota(i32, (1, 128), 1)
    bias_row = jnp.zeros((1, 128), f32)
    for d in range(DOMAINS):
        at = slice(d * tower_units, (d + 1) * tower_units)
        mine = d_logit * here_columns[:, d : d + 1]
        put_row(small_part, shape.tower_out[d], jnp.sum(mine * work[:, at], axis=0, keepdims=True))
        bias_row = jnp.where(lane == d, jnp.sum(mine, axis=0, keepdims=True), bias_row)
        low = (mine * tower_out[d : d + 1, :] * d_after[:, at]).astype(bf16)
        d_tower[d] = low
        put_row(small_part, shape.tower_in_bias[d], jnp.sum(low.astype(f32), axis=0, keepdims=True))
    small_part[shape.tower_out_bias : shape.tower_out_bias + 1, :] = bias_row

    wait_for_all()
    ways = orders()
    pieces, clock = [], [0]

    def pump():
        for piece in pieces:
            if not piece.done() and piece.sent_at < clock[0] - 2:
                piece.take()
                piece.sent_at = clock[0]
        clock[0] += 1

    def send(block, parts, inboxes, owns, totals, i, value):
        k = len(pieces)
        block.put(parts.at[i], value)
        piece = Piece(
            parts.at[i], inboxes.at[i], owns.at[i], totals.at[i], ways[k], own_sems.at[k], sends.at[k], recvs.at[k]
        )
        piece.send()
        piece.sent_at = clock[0]
        pieces.append(piece)

    towers = [jnp.dot(after_turned[...], d_tower[d], preferred_element_type=f32).astype(bf16) for d in range(DOMAINS)]
    send(blocks[2], part_tower, inbox_tower, own_tower, total_tower, 0, jnp.concatenate(towers, axis=0))
    d_after[...] = sum(
        lax.dot_general(d_tower[d], tower_in[d], NT, preferred_element_type=f32) for d in range(DOMAINS)
    )
    d_state[...] = d_after[...]

    products[...] = jnp.zeros(products.shape, f32)
    zero = jnp.zeros((1, depth), f32)
    half = units // 2
    for x in range(experts):

        def unmix(i, sums):
            at = stripe(i)
            d, value = d_after[at, :], standard[x, at, :].astype(f32)
            products[at, x : x + 1] = jnp.sum(d * (value * expert_gain[x : x + 1, :] + expert_bias[x : x + 1, :]), axis=1, keepdims=True)
            d = coef[at, x : x + 1] * d
            low = standardise_back(d * expert_gain[x : x + 1, :], value, inverse[at, x : x + 1]).astype(bf16)
            d_out[at, :] = low
            terms = (d * value, d, low.astype(f32))
            return tuple(s + jnp.sum(t, axis=0, keepdims=True) for s, t in zip(sums, terms))

        for place, row in zip((shape.gain[x], shape.bias[x], shape.b_out[x]),
                              lax.fori_loop(0, events // STRIPE, unmix, (zero,) * 3, unroll=2)):
            put_row(small_part, place, row)
        pump()
        for h in range(2):
            value = lax.dot_general(active[x, :, h * half : (h + 1) * half], d_out[...], TN, preferred_element_type=f32)
            send(blocks[1], part_out, inbox_out, own_out, total_out, 2 * x + h, value.astype(bf16))

        def unenter(c):
            at = pl.ds(pl.multiple_of(c * quarter, quarter), quarter)
            d = lax.dot_general(d_out[...], w_out[x, at, :], NT, preferred_element_type=f32)
            low = (d * slope[x, :, at].astype(f32)).astype(bf16)
            d_in[:, at] = low
            row = jnp.sum(low.astype(f32), axis=0, keepdims=True)
            for q in range(quarter // 128):
                small_part[pl.ds(shape.b_in[x] + c * (quarter // 128) + q, 1), :] = row[:, q * 128 : (q + 1) * 128]

        loop(units // quarter, unenter)
        for h in range(2):
            value = jnp.dot(state_turned[...], d_in[:, h * half : (h + 1) * half], preferred_element_type=f32)
            send(blocks[0], part_in, inbox_in, own_in, total_in, 2 * x + h, value.astype(bf16))

        def unstate(c):
            at = pl.ds(pl.multiple_of(c * quarter, quarter), quarter)
            d_state[:, at] += lax.dot_general(d_in[...], w_in[x, at, :], NT, preferred_element_type=f32)

        loop(depth // quarter, unstate)
        pump()

    ahead = counts.shape[0]

    def fetch(o):
        slot = o % ahead if isinstance(o, int) else lax.rem(o, ahead)
        return pltpu.make_async_copy(counts_hbm.at[o], counts.at[slot], count_sems.at[slot])

    for o in range(ahead):
        fetch(o).start()
    q = products[...].T
    q = [q[x : x + 1] for x in range(experts)]
    d_level = (share[0] * q[0] + share[1] * q[1], by_domain(which, q[SHARED:]))
    mean_share = share[0] * q[0] + share[1] * q[1]
    d_share = [level[0] * share[s] * (q[s] - mean_share) for s in range(SHARED)]
    mean_level = level[0] * d_level[0] + level[1] * d_level[1]
    d_group = [level[i] * (d_level[i] - mean_level) for i in range(2)]
    rows = d_share + [d_group[i] * here[d] for d in range(DOMAINS) for i in range(2)]
    d_logits = jnp.concatenate(rows + [jnp.zeros((GATE_ROWS - len(rows), events), f32)], axis=0)
    split = thirds(d_logits)
    gate_sums = jnp.dot(split, state_low[...], preferred_element_type=f32)
    gate_sums = sum(gate_sums[i * GATE_ROWS : (i + 1) * GATE_ROWS] for i in range(3))
    for i, place in enumerate(shape.gates):
        put_row(small_part, place, gate_sums[i : i + 1])
    gates_thrice = jnp.concatenate([gates[...]] * 3, axis=0)
    d_state[...] += lax.dot_general(split, gates_thrice, TN, preferred_element_type=f32)

    def unstart(i, sums):
        at = stripe(i)
        d, value = d_state[at, :], pre_standard[at, :]
        low = (standardise_back(d * inter_gain[...], value, pre_inverse[at, :]) * pre_slope[at, :]).astype(bf16)
        d_out[at, :] = low
        terms = (d * value, d, low.astype(f32))
        return tuple(s + jnp.sum(t, axis=0, keepdims=True) for s, t in zip(sums, terms))

    for place, row in zip((shape.inter_gain, shape.inter_bias, shape.proj_b),
                          lax.fori_loop(0, events // STRIPE, unstart, (zero,) * 3, unroll=2)):
        put_row(small_part, place, row)
    value = jnp.dot(joined[...], d_out[...], preferred_element_type=f32)
    send(blocks[3], part_proj, inbox_proj, own_proj, total_proj, 0, value.astype(bf16))
    n_all = n_field * width
    d_fields[:n_all, :] = lax.dot_general(proj_w[:n_all, :], d_out[...], NT, preferred_element_type=f32).astype(bf16)
    tail = lax.dot_general(proj_w[n_all:, :], d_out[...], NT, preferred_element_type=f32)
    d_pooled[...] = (tail[:width] / length).astype(bf16)
    d_centered[...] = tail[width:]
    lanes = lax.broadcasted_iota(i32, (width, 128), 1)
    sums = jnp.zeros((width, 128), f32)
    for d in range(DOMAINS):
        mine = jnp.where(which == d, tail[width:], 0.0)
        for k, term in enumerate((mine, mine * centered[...])):
            sums = jnp.where(lanes == k * DOMAINS + d, jnp.sum(term, axis=1, keepdims=True), sums)
    small_part[shape.dense : shape.dense + width, :] = sums
    if small_part.shape[0] > shape.next:
        small_part[shape.next :, :] = jnp.zeros((small_part.shape[0] - shape.next, 128), f32)
    k = len(pieces)
    small_piece = Piece(
        small_part, small_inbox, small_own, small_total, ways[0], own_sems.at[k], sends.at[k], recvs.at[k]
    )
    small_piece.send()
    small_piece.sent_at = clock[0]
    pieces.append(small_piece)
    pump()

    shift = cap.bit_length() - 1
    slot_total[...] = jnp.zeros(slot_total.shape, f32)

    def scatter(f, carry):
        wide, hots = [], []
        for k in range(2):
            slot = field[pl.ds(f * 2 + k, 1), :]
            owner = jnp.broadcast_to(jnp.right_shift(slot, shift), (width, events))
            d = d_fields[pl.ds(pl.multiple_of((f * 2 + k) * width, width), width), :].astype(f32)
            wide.append(
                jnp.concatenate([jnp.where(owner == o, d, 0.0).astype(bf16) for o in range(owners)], axis=0)
            )
            hots.append(hot(cap, jnp.bitwise_and(slot, cap - 1)))
        slot_total[...] += lax.dot_general(
            jnp.concatenate(wide, axis=1), jnp.concatenate(hots, axis=1), NT, preferred_element_type=f32
        )
        return carry

    for first in range(0, n_field // 2, 2):
        lax.fori_loop(first, min(first + 2, n_field // 2), scatter, 0)
        pump()

    def spread(o):
        fetch(o).wait()
        behave = jnp.dot(d_pooled[...], counts[lax.rem(o, ahead)], preferred_element_type=f32)
        at = pl.ds(pl.multiple_of(o * width, width), width)
        slot_grad[o] = (slot_total[at, :] + behave).astype(bf16)
        pl.when(o + ahead < owners)(lambda: fetch(o + ahead).start())

    for first in range(0, owners, owners // 8):

        def spread_some(o, carry):
            spread(o)
            return carry

        lax.fori_loop(first, first + owners // 8, spread_some, 0)
        pump()
    me = lax.axis_index("wide") * lax.axis_size("narrow") + lax.axis_index("narrow")
    slot_copies = []
    for d, other, place in everyone_else():
        copy = pltpu.make_async_remote_copy(
            src_ref=slot_grad.at[other], dst_ref=returned.at[me], send_sem=slot_sends.at[d],
            recv_sem=slot_recvs.at[d], device_id=place, device_id_type=MESH)
        copy.start()
        slot_copies.append(copy)
    returned[me] = slot_grad[me]

    while any(not piece.done() for piece in pieces):
        for piece in pieces:
            if not piece.done():
                piece.take()
    for copy in slot_copies:
        copy.wait_recv()
    for copy in slot_copies:
        copy.wait_send()
    for piece in pieces:
        piece.drain()


def learn(fields, pooled, lengths, dense, domains, cotangent, stats, model, field, counts, devices):
    w_in, tower_in, proj_w = model[4], model[12], model[0]
    experts, depth, units = w_in.shape
    width, events = dense.shape
    owners, _, cap = counts.shape
    tower_units = tower_in.shape[2]
    half = units // 2
    shape = Rows(experts, units, depth, tower_units, width)
    n_small = shape.padded(devices)
    blocks = [
        Block(depth, half, devices), Block(half, depth, devices),
        Block(DOMAINS * depth, tower_units, devices), Block(proj_w.shape[0], depth, devices),
    ]
    numbers = (2 * experts, 2 * experts, 1, 1)
    pieces = [(n, b.padded, b.lanes) for n, b in zip(numbers, blocks)]
    steps = 2 * (devices.bit_length() - 1)
    n_pieces = sum(numbers) + 1
    joined = proj_w.shape[0]
    ahead = max(4, min(16, 512 // devices))
    space = lambda *s: pltpu.VMEM(s, f32)
    low = lambda *s: pltpu.VMEM(s, bf16)
    dma = lambda *s: pltpu.SemaphoreType.DMA(s)
    in_specs = [vmem()] * 25
    in_specs[11] = in_specs[13] = in_specs[24] = hbm()
    out = pl.pallas_call(
        functools.partial(learn_kernel, shape, blocks),
        in_specs=in_specs,
        out_specs=[vmem()] * 4 + [hbm()] * 5,
        out_shape=[
            jax.ShapeDtypeStruct((1, events), f32),
            jax.ShapeDtypeStruct((width, events), f32),
            jax.ShapeDtypeStruct((width, events), f32),
            jax.ShapeDtypeStruct((owners, width, cap), bf16),
            jax.ShapeDtypeStruct((n_small, 128), f32),
        ]
        + [jax.ShapeDtypeStruct(s, bf16) for s in pieces],
        scratch_shapes=[
            low(experts, depth, units), low(experts, units, depth), low(joined, events),
            space(events, depth), space(events, depth), space(events, 1), low(events, depth),
            low(depth, events), space(events, 8), low(experts, events, units), low(experts, events, units),
            low(experts, events, depth), space(events, 8), space(events, depth), space(events, depth),
            low(events, depth), low(depth, events), low(DOMAINS, events, tower_units), space(events, depth),
            space(events, 8), low(events, depth), low(events, units), low(width, events), low(GATE_ROWS, depth), low(ahead, events, cap), space(owners * width, cap),
            low(owners, width, cap), space(n_small, 128), space(n_small, 128),
        ]
        + [pltpu.VMEM(s, bf16) for s in pieces] * 2
        + [space(n_small // devices, 128)]
        + [low(n, rows // devices, lanes) for n, rows, lanes in pieces]
        + [dma(experts), dma(experts), dma(ahead), dma(n_pieces), dma(n_pieces, steps), dma(n_pieces, steps), dma(devices), dma(devices)],
        compiler_params=params(collective_id=0, has_side_effects=True),
        name="learn",
    )(fields, pooled, lengths, dense, domains, cotangent, stats, *model, field, counts)
    return out[:5], [b.whole(t, n) for b, t, n in zip(blocks, out[5:], numbers)], shape


def get_row(small, at, n):
    return jnp.concatenate([small[at + c : at + c + 1, :] for c in range(n // 128)], axis=1)


def finish_kernel(shape, line, line_v, group, returned, domains, stats, centered, d_centered, small, *refs):
    more, out, more_out = refs[:4], refs[4], refs[5:9]
    d_dense, b_in, b_out, gain, bias, proj_b, inter_gain, inter_bias, shared_gate, group_gate, tower_in_bias, tower_out, tower_bias = refs[9:22]
    lines, vals = refs[22:]
    step = pl.program_id(0)
    per = out.shape[1] // ROW_CHUNK

    @pl.when(step == 0)
    def _():
        for target, places in (
            (b_in, shape.b_in), (b_out, shape.b_out), (gain, shape.gain), (bias, shape.bias),
            (proj_b, [shape.proj_b]), (inter_gain, [shape.inter_gain]), (inter_bias, [shape.inter_bias]),
            (shared_gate, shape.gates[:SHARED]), (tower_in_bias, shape.tower_in_bias), (tower_out, shape.tower_out),
        ):
            for i, at in enumerate(places):
                target[i : i + 1, :] = get_row(small, at, target.shape[1])
        for i, at in enumerate(shape.gates[SHARED:]):
            group_gate[i // 2, i % 2 : i % 2 + 1, :] = get_row(small, at, group_gate.shape[2])
        tower_bias[...] = small[shape.tower_out_bias : shape.tower_out_bias + 1, : tower_bias.shape[1]]
        which = domains[...]
        sums = small[shape.dense : shape.dense + centered.shape[0], :]
        moments = domain_moments(stats[...])
        scale = by_domain(which, [m[1] for m in moments])
        straight = by_domain(which, [sums[:, d : d + 1] / m[2] for d, m in enumerate(moments)])
        cross = by_domain(which, [sums[:, DOMAINS + d : DOMAINS + d + 1] / m[2] for d, m in enumerate(moments)])
        d_dense[...] = scale * (d_centered[...] - straight - centered[...] * cross)

        def clear(i, carry):
            lines[pl.ds(pl.multiple_of(i * 1024, 1024), 1024), :] = jnp.zeros((1024, 128), f32)
            return carry

        lax.fori_loop(0, lines.shape[0] // 1024, clear, 0)

    width, cap = returned.shape[1:]

    @pl.when(step < ADD_STEPS)
    def _():
        batch = 32
        a = lax.div(lax.broadcasted_iota(i32, (cap, cap), 0), batch)
        near = a == lax.div(lax.broadcasted_iota(i32, (cap, cap), 1), batch)
        each = group.shape[0] // ADD_STEPS

        def prepare(s, slot):
            which, own = jnp.broadcast_to(group[s], (width, cap)), returned[s].astype(f32)
            wide = jnp.concatenate([jnp.where(which == g, own, 0.0) for g in range(8)], axis=0)
            along = jnp.broadcast_to(line_v[s].astype(f32), (cap, cap))
            same = jnp.where(jnp.logical_and(along == along.T, near), 1.0, 0.0).astype(bf16)
            vals[slot] = lax.dot_general(same, wide.astype(bf16), NT, preferred_element_type=f32)

        def add(s, slot):
            for u in range(0, cap, batch):
                places, sums = [], []
                for j in range(u, u + batch):
                    places.append(line[s * cap + j])
                    sums.append(lines[pl.ds(places[-1], 1), :] + vals[slot, j : j + 1, :])
                for place, total in zip(places, sums):
                    lines[pl.ds(place, 1), :] = total

        prepare(step * each, 0)

        def serve(i, carry):
            s = step * each + i * 2
            prepare(s + 1, 1)
            add(s, 0)
            prepare(jnp.minimum(s + 2, group.shape[0] - 1), 0)
            add(s + 1, 1)
            return carry

        lax.fori_loop(0, each // 2, serve, 0)
        for source, target in zip(more, more_out):
            tall, blocks, rows, lanes = source.shape
            for s in range(tall):
                for c in range(blocks):
                    target[s * rows : (s + 1) * rows, c * lanes : (c + 1) * lanes] = source[s, c].astype(f32)

    @pl.when(step >= ADD_STEPS)
    def _():
        def turn(c, carry):
            at = pl.multiple_of(((step - ADD_STEPS) * per + c) * 128, 128)
            turned = lines[pl.ds(at, 128), :].T
            for g in range(8):
                at = pl.multiple_of(c * ROW_CHUNK + g * 128, 128)
                out[:, pl.ds(at, 128)] = turned[g * width : (g + 1) * width]
            return carry

        lax.fori_loop(0, per, turn, 0, unroll=12)


def finish(shape, line, group, returned, domains, stats, centered, d_centered, small, more, rows):
    blocks, width, cap = returned.shape
    events = centered.shape[1]
    experts, units, depth = len(shape.b_in), more[0].shape[1] * more[0].shape[3], more[0].shape[2]
    tower = more[2].shape[1] * more[2].shape[3]
    steps, turns = ADD_STEPS, 4
    early = lambda i: jnp.minimum(i, steps - 1)
    in_more, out_more, shapes = [], [], []
    for x in more:
        tall, parts, r, lanes = x.shape
        if tall > 1:
            in_more.append(pl.BlockSpec((tall // steps, parts, r, lanes), lambda i: (early(i), 0, 0, 0)))
        else:
            in_more.append(pl.BlockSpec((1, parts, r // steps, lanes), lambda i: (0, 0, early(i), 0)))
        out_more.append(pl.BlockSpec((tall * r // steps, parts * lanes), lambda i: (early(i), 0)))
        shapes.append((tall * r, parts * lanes))
    shapes += [(width, events), (experts, units)] + [(experts, depth)] * 3 + [(1, depth)] * 3
    shapes += [(SHARED, depth), (DOMAINS, 2, depth), (DOMAINS, tower), (DOMAINS, tower), (1, DOMAINS)]
    return pl.pallas_call(
        functools.partial(finish_kernel, shape),
        grid=(steps + turns,),
        in_specs=[smem()] + [vmem()] * 8 + in_more,
        out_specs=[pl.BlockSpec((width, rows // turns), lambda i: (0, jnp.maximum(i - steps, 0)))] + out_more + [vmem()] * 13,
        out_shape=[jax.ShapeDtypeStruct(s, f32) for s in [(width, rows)] + shapes],
        scratch_shapes=[pltpu.VMEM((rows // 8, 128), f32), pltpu.VMEM((2, cap, 128), f32)],
        compiler_params=params(),
        name="finish",
    )(line.reshape(-1), line, group, returned, domains, stats, centered, d_centered, small, *more)


def local(
    table,
    dense,
    domains,
    lengths,
    requests,
    counts,
    field_slots,
    behave_slots,
    proj_w,
    proj_b,
    inter_gain,
    inter_bias,
    w_in,
    b_in,
    w_out,
    b_out,
    expert_gain,
    expert_bias,
    shared_gate,
    group_gate,
    tower_in,
    tower_in_bias,
    tower_out,
    tower_out_bias,
    pred_cotangent,
):
    devices = lax.axis_size("wide") * lax.axis_size("narrow")
    capacity = requests.shape[2]
    experts, depth, units = w_in.shape
    counts_of = slot_counts(lengths, behave_slots.reshape(-1, 128), devices, capacity)
    field = field_slots.T
    dense_t, which = dense.T, domains[None]
    fields, pooled, line, group, stats = lookup(
        requests[0], table.T, counts.reshape(-1), field, counts_of, dense_t, which
    )
    model = (
        proj_w, proj_b[None], inter_gain[None], inter_bias[None], w_in, b_in, w_out, b_out, expert_gain, expert_bias,
        shared_gate.T, group_gate.transpose(0, 2, 1), tower_in, tower_in_bias, tower_out, tower_out_bias[None],
    )
    (pred, centered, d_centered, returned, small), totals, shape = learn(
        fields, pooled, lengths, dense_t, which, pred_cotangent[None], stats, model, field, counts_of, devices
    )
    totals[0] = totals[0].reshape(experts, -1, depth, totals[0].shape[3])
    out = finish(shape, line, group, returned, which, stats, centered, d_centered, small, totals, table.shape[0])
    d_table, d_w_in, d_w_out, d_tower_in, d_proj_w, d_dense, d_b_in, d_b_out, d_gain, d_bias = out[:10]
    d_proj_b, d_inter_gain, d_inter_bias, d_shared_gate, d_group_gate, d_tower_in_bias, d_tower_out, d_tower_bias = out[10:]
    return (
        pred[0],
        d_dense.T,
        d_table.T,
        d_proj_w,
        d_proj_b[0],
        d_inter_gain[0],
        d_inter_bias[0],
        d_w_in.reshape(w_in.shape),
        d_b_in,
        d_w_out.reshape(w_out.shape),
        d_b_out,
        d_gain,
        d_bias,
        d_shared_gate.T,
        d_group_gate.transpose(0, 2, 1),
        d_tower_in.reshape(tower_in.shape),
        d_tower_in_bias,
        d_tower_out,
        d_tower_bias[0],
    )


def solution(mesh):
    placed = (
        P(("wide", "narrow"), None),
        P(("wide", "narrow"), None),
        P(("wide", "narrow")),
        P(("wide", "narrow"), None),
        P(("wide", "narrow"), None, None),
        P(("wide", "narrow"), None),
        P(("wide", "narrow"), None),
        P(("wide", "narrow"), None),
        P(),
        P(),
        P(),
        P(),
        P(),
        P(),
        P(),
        P(),
        P(),
        P(),
        P(),
        P(),
        P(),
        P(),
        P(),
        P(),
        P(("wide", "narrow")),
    )
    return jax.shard_map(
        local,
        mesh=mesh,
        in_specs=placed,
        out_specs=(
            P(("wide", "narrow")),
            P(("wide", "narrow"), None),
            P(("wide", "narrow"), None),
            P(),
            P(),
            P(),
            P(),
            P(),
            P(),
            P(),
            P(),
            P(),
            P(),
            P(),
            P(),
            P(),
            P(),
            P(),
            P(),
        ),
        check_vma=False,
    )
```

```python
import functools
import math

import jax
import jax.numpy as jnp
from jax import lax
from jax.experimental import pallas as pl
from jax.experimental.pallas import tpu as pltpu
from jax.sharding import PartitionSpec as P

SHARED = 2
DOMAINS = 2

EPSILON = 1e-05

f32 = jnp.float32
bf16 = jnp.bfloat16
i32 = jnp.int32
MESH = pl.DeviceIdType.MESH
AXES = ("wide", "narrow")
NT = (((1,), (1,)), ((), ()))
TN = (((0,), (0,)), ((), ()))
VMEM_LIMIT = 60 * 1024 * 1024
ROW_CHUNK = 1024
GROUP = 8
SPAN = 6
BUNCH = 4
ADD_STEPS = 4


def vmem():
    return pl.BlockSpec(memory_space=pltpu.VMEM)


def smem():
    return pl.BlockSpec(memory_space=pltpu.SMEM)


def hbm():
    return pl.BlockSpec(memory_space=pl.ANY)


def params(**more):
    return pltpu.CompilerParams(vmem_limit_bytes=VMEM_LIMIT, **more)


def line_of(rows):
    return jnp.left_shift(jnp.right_shift(rows, 10), 7) + jnp.bitwise_and(rows, 127)


def lane_group_of(rows):
    return jnp.bitwise_and(jnp.right_shift(rows, 7), 7)


def identity(n):
    return (lax.broadcasted_iota(i32, (n, n), 0) == lax.broadcasted_iota(i32, (n, n), 1)).astype(bf16)


def hot(rows, index):
    column = lax.broadcasted_iota(i32, (rows, index.shape[1]), 0)
    return jnp.where(column == index, 1.0, 0.0).astype(bf16)


def count_kernel(lengths, behave, counts, sums, done):
    owners, _, cap = counts.shape
    shift = cap.bit_length() - 1
    step = pl.program_id(0)
    place = lax.broadcasted_iota(i32, (SPAN, 128), 0) * 128 + lax.broadcasted_iota(i32, (SPAN, 128), 1)
    last_block = behave.shape[0] - SPAN
    ends = [jnp.where(step == 0, 0, done[0])]
    for i in range(BUNCH * GROUP):
        ends.append(ends[-1] + lengths[0, step * (BUNCH * GROUP) + i])
    done[0] = ends[-1]

    def part(k, m):
        cuts = ends[k * GROUP : (k + 1) * GROUP + 1]
        begin = lax.div(cuts[0], 128) + m * SPAN
        b = jnp.minimum(begin, last_block)
        slot = behave[pl.ds(b, SPAN), :]
        p = place + b * 128
        event = jnp.zeros_like(p)
        for cut in cuts[1:-1]:
            event = event + jnp.where(p >= cut, 1, 0)
        mine = jnp.logical_and(jnp.logical_and(p >= cuts[0], p < cuts[-1]), p >= begin * 128)
        key = jnp.where(mine, jnp.right_shift(slot, shift) * GROUP + event, -1)
        low = jnp.bitwise_and(slot, cap - 1)
        left = jnp.concatenate([hot(owners * GROUP, key[q : q + 1]) for q in range(SPAN)], axis=1)
        right = jnp.concatenate([hot(cap, low[q : q + 1]) for q in range(SPAN)], axis=1)
        return lax.dot_general(left, right, NT, preferred_element_type=f32)

    parts = []
    for k in range(BUNCH):
        sums[k] = part(k, 0)
        first, last = ends[k * GROUP], ends[(k + 1) * GROUP]
        parts.append(lax.div(last - lax.div(first, 128) * 128 + (SPAN * 128 - 1), SPAN * 128))
    most = functools.reduce(jnp.maximum, parts)

    @pl.when(most > 1)
    def _():
        for k in range(BUNCH):

            def more(m, carry):
                sums[k] += part(k, m)
                return carry

            lax.fori_loop(1, parts[k], more, 0)

    for t in range(BUNCH // 2):
        for o in range(owners):
            both = [sums[2 * t + k, o * GROUP : (o + 1) * GROUP, :] for k in range(2)]
            counts[o, t * 2 * GROUP : (t + 1) * 2 * GROUP, :] = jnp.concatenate(both, axis=0).astype(bf16)


def slot_counts(lengths, behave, owners, cap):
    events = lengths.shape[1]
    size = BUNCH * GROUP
    return pl.pallas_call(
        count_kernel,
        grid=(events // size,),
        in_specs=[smem(), vmem()],
        out_specs=pl.BlockSpec((owners, size, cap), lambda i: (0, i, 0)),
        out_shape=jax.ShapeDtypeStruct((owners, events, cap), bf16),
        scratch_shapes=[pltpu.VMEM((BUNCH, owners * GROUP, cap), f32), pltpu.SMEM((1,), i32)],
        compiler_params=params(),
        name="slot_counts",
    )(lengths, behave)


def place_bits():
    return [(axis, b) for axis in AXES for b in range(lax.axis_size(axis).bit_length() - 1)]


def bit_value(bit):
    return jnp.bitwise_and(jnp.right_shift(lax.axis_index(bit[0]), bit[1]), 1)


def across(bit):
    axis, b = bit
    place = {a: lax.axis_index(a) for a in AXES}
    place[axis] = place[axis] + (1 - 2 * bit_value(bit)) * (1 << b)
    return tuple(place[a] for a in AXES)


class Piece:
    def __init__(self, part, inbox, own, total, order, own_sem, sends, recvs):
        self.part, self.inbox, self.own, self.total = part, inbox, own, total
        self.order, self.own_sem, self.sends, self.recvs = order, own_sem, sends, recvs
        self.rows = part.shape[0]
        self.grain = self.rows >> len(order)
        self.offsets, self.copies, self.taken = [0], [], 0

    def at(self, ref, offset, n):
        return ref.at[pl.ds(pl.multiple_of(offset, self.grain), n)]

    def keep(self):
        return pltpu.make_async_copy(self.own, self.at(self.total, self.offsets[-1], self.grain), self.own_sem)

    def send(self):
        k, depth = len(self.copies), len(self.order)
        if k < depth:
            bit, half = self.order[k], self.rows >> (k + 1)
            value, offset = bit_value(bit), self.offsets[k]
            self.offsets.append(offset + value * half)
            source = self.at(self.part, offset + (1 - value) * half, half)
            target = self.inbox.at[pl.ds(self.rows - (self.rows >> k), half)]
        else:
            s = 2 * depth - 1 - k
            bit = self.order[s]
            target = self.at(self.total, self.offsets[s + 1], self.rows >> (s + 1))
            source = self.own if k == depth else target
        copy = pltpu.make_async_remote_copy(
            src_ref=source,
            dst_ref=target,
            send_sem=self.sends.at[k],
            recv_sem=self.recvs.at[k],
            device_id=across(bit),
            device_id_type=MESH,
        )
        copy.start()
        self.copies.append(copy)

    def done(self):
        return self.taken == 2 * len(self.order)

    def take(self):
        k, depth = self.taken, len(self.order)
        self.copies[k].wait_recv()
        self.taken += 1
        if k < depth:
            n, base, offset = self.rows >> (k + 1), self.rows - (self.rows >> k), self.offsets[k + 1]
            chunk = math.gcd(n, 64)

            def add(i, carry):
                at = pl.ds(pl.multiple_of(offset + i * chunk, math.gcd(self.grain, chunk)), chunk)
                came = pl.ds(pl.multiple_of(base + i * chunk, chunk), chunk)
                total = (self.part[at, :].astype(f32) + self.inbox[came, :].astype(f32)).astype(self.part.dtype)
                if k == depth - 1:
                    self.own[pl.ds(pl.multiple_of(i * chunk, chunk), chunk), :] = total
                else:
                    self.part[at, :] = total
                return carry

            lax.fori_loop(0, n // chunk, add, 0)
        if k == depth - 1:
            self.keep().start()
        if k == depth:
            self.keep().wait()
        if not self.done():
            self.send()

    def drain(self):
        for copy in self.copies:
            copy.wait_send()


def peer(d):
    n_wide, n_narrow = (lax.axis_size(a) for a in AXES)
    w, n = (lax.axis_index(a) for a in AXES)
    other = jnp.bitwise_and(w * n_narrow + n + d, n_wide * n_narrow - 1)
    return other, (jnp.right_shift(other, n_narrow.bit_length() - 1), jnp.bitwise_and(other, n_narrow - 1))


def everyone_else():
    for d in range(1, lax.axis_size("wide") * lax.axis_size("narrow")):
        yield (d,) + peer(d)


def greet_all():
    barrier = pltpu.get_barrier_semaphore()
    for _, _, place in everyone_else():
        pl.semaphore_signal(barrier, inc=1, device_id=place, device_id_type=MESH)


def wait_for_all():
    pl.semaphore_wait(pltpu.get_barrier_semaphore(), lax.axis_size("wide") * lax.axis_size("narrow") - 1)


def meet_all():
    greet_all()
    wait_for_all()


def lanes_of(rows, columns, devices):
    lanes = columns
    while lanes > 128 and (rows * (columns // lanes)) % (16 * devices):
        lanes //= 2
    return lanes


ORDERS = "BABGABDABAGBABDABA"


class Block:
    def __init__(self, rows, columns, devices):
        self.rows, self.columns = rows, columns
        self.lanes = lanes_of(rows, columns, devices)
        self.blocks = columns // self.lanes
        self.padded = -(-rows * self.blocks // (16 * devices)) * 16 * devices

    def put(self, piece, value):
        for c in range(self.blocks):
            piece[c * self.rows : (c + 1) * self.rows, :] = value[:, c * self.lanes : (c + 1) * self.lanes]
        extra = self.padded - self.rows * self.blocks
        if extra:
            piece[self.rows * self.blocks :, :] = jnp.zeros((extra, self.lanes), piece.dtype)

    def whole(self, total, n):
        return total[:, : self.rows * self.blocks].reshape(n, self.blocks, self.rows, self.lanes)


def orders():
    if tuple(lax.axis_size(a) for a in AXES) != (8, 4):
        return [place_bits()] * len(ORDERS)
    core, y, x, z0, z1 = ("narrow", 0), ("narrow", 1), ("wide", 0), ("wide", 1), ("wide", 2)
    ways = {
        "A": [core, x, y, z0, z1],
        "B": [core, y, x, z0, z1],
        "D": [core, z0, z1, y, x],
        "G": [core, z0, z1, x, y],
    }
    return [ways[way] for way in ORDERS]


def lookup_kernel(
    requests_in, table, live, field, counts_hbm, dense, domains,
    fields, pooled, line_out, group, stats_out,
    requests, counts, tab, lines, got, line, line_smem, found, rows, slots, stats, stats_in,
    tab_sems, counts_sem, line_sem, ask_sends, ask_recvs, row_sends, row_recvs, stat_sends, stat_recvs,
):
    owners, _, cap = requests.shape
    width = tab.shape[0]
    n_field, events = field.shape
    chunks = tab_sems.shape[0]
    part = tab.shape[1] // chunks
    me = lax.axis_index("wide") * lax.axis_size("narrow") + lax.axis_index("narrow")

    loads = []
    for c in range(chunks):
        at = pl.ds(c * part, part)
        loads.append(pltpu.make_async_copy(table.at[:, at], tab.at[:, at], tab_sems.at[c]))
        loads[-1].start()
    load_counts = pltpu.make_async_copy(counts_hbm, counts, counts_sem)
    for o in range(owners):
        requests[o] = requests_in[o : o + 1, :]
    lane = lax.broadcasted_iota(i32, (width, 128), 1)
    mine = jnp.zeros((width, 128), f32)
    for d in range(DOMAINS):
        here = domains[...] == d
        value = jnp.where(here, dense[...], 0.0)
        one = jnp.broadcast_to(jnp.where(here, 1.0, 0.0), value.shape)
        for k, term in enumerate((value, value * value, one)):
            mine = jnp.where(lane == k * DOMAINS + d, jnp.sum(term, axis=1, keepdims=True), mine)
    stats[...] = mine

    meet_all()

    def ask(d):
        other, place = peer(d)
        return pltpu.make_async_remote_copy(
            src_ref=requests.at[other], dst_ref=line.at[me], send_sem=ask_sends.at[d],
            recv_sem=ask_recvs.at[d], device_id=place, device_id_type=MESH)

    def tell(d):
        _, place = peer(d)
        return pltpu.make_async_remote_copy(
            src_ref=stats, dst_ref=stats_in.at[me], send_sem=stat_sends.at[d],
            recv_sem=stat_recvs.at[d], device_id=place, device_id_type=MESH)

    def answer(d):
        other, place = peer(d)
        return pltpu.make_async_remote_copy(
            src_ref=found.at[other], dst_ref=rows.at[me], send_sem=row_sends.at[d],
            recv_sem=row_recvs.at[d], device_id=place, device_id_type=MESH)

    def each(first, act):
        def step(d, carry):
            act(d)
            return carry

        lax.fori_loop(first, owners, step, 0)

    each(1, lambda d: ask(d).start())
    each(1, lambda d: tell(d).start())
    line[me] = requests[me]
    stats_in[me] = stats[...]

    eye = identity(128)
    for c in range(chunks):
        loads[c].wait()

        def turn(i, carry):
            base = pl.multiple_of(c * part + i * ROW_CHUNK, ROW_CHUNK)
            stack = jnp.concatenate([tab[:, pl.ds(base + g * 128, 128)] for g in range(8)], axis=0)
            at = pl.multiple_of((c * part // ROW_CHUNK + i) * 128, 128)
            lines[pl.ds(at, 128), :] = lax.dot_general(eye, stack, NT, preferred_element_type=f32)
            return carry

        lax.fori_loop(0, part // ROW_CHUNK, turn, 0, unroll=8)

    load_counts.start()
    each(1, lambda d: ask(d).wait_recv())
    group[...] = lane_group_of(line[...])
    line_out[...] = line_of(line[...])
    to_smem = pltpu.make_async_copy(line_out, line_smem, line_sem)
    to_smem.start()
    to_smem.wait()

    def source(d):
        return peer(d)[0]

    def fetch(d):
        s, half = source(d), jnp.bitwise_and(d, 1) * cap
        for j in range(cap):
            got[pl.ds(half + j, 1), :] = lines[pl.ds(line_smem[s, 0, j], 1), :]

    def turn_out(d):
        s, half = source(d), pl.multiple_of(jnp.bitwise_and(d, 1) * cap, cap)
        turned = lax.dot_general(eye, got[pl.ds(half, cap), :].astype(bf16), NT, preferred_element_type=f32)
        which = jnp.broadcast_to(group[s], (width, cap))
        picked = turned[:width]
        for g in range(1, 8):
            picked = jnp.where(which == g, turned[g * width : (g + 1) * width], picked)
        found[s] = picked.astype(bf16)

    fetch(0)

    def serve(d, carry):
        turn_out(d - 1)
        fetch(d)
        pl.when(d > 1)(lambda: answer(d - 1).start())
        return carry

    lax.fori_loop(1, owners, serve, 0)
    turn_out(owners - 1)
    answer(owners - 1).start()
    rows[me] = found[me]
    each(1, lambda d: tell(d).wait_recv())
    total = stats_in[0]
    for o in range(1, owners):
        total = total + stats_in[o]
    stats_out[...] = total

    each(1, lambda d: answer(d).wait_recv())
    shift = cap.bit_length() - 1
    column = lax.broadcasted_iota(i32, (width, cap), 1)
    for o in range(owners):
        slots[o * width : (o + 1) * width, :] = jnp.where(column < live[o], rows[o].astype(f32), 0.0).astype(bf16)

    def one(f, carry):
        slot = field[pl.ds(f, 1), :]
        owner = jnp.broadcast_to(jnp.right_shift(slot, shift), (width, events))
        all_owners = jnp.dot(slots[...], hot(cap, jnp.bitwise_and(slot, cap - 1)), preferred_element_type=f32)
        picked = all_owners[:width]
        for o in range(1, owners):
            picked = jnp.where(owner == o, all_owners[o * width : (o + 1) * width], picked)
        fields[pl.ds(pl.multiple_of(f * width, width), width), :] = picked.astype(bf16)
        return carry

    lax.fori_loop(0, n_field, one, 0, unroll=4)
    load_counts.wait()
    total = jnp.zeros((events, width), f32)
    for o in range(owners):
        total = total + lax.dot_general(counts[o], slots[o * width : (o + 1) * width, :], NT, preferred_element_type=f32)
    pooled[...] = total.T
    each(1, lambda d: ask(d).wait_send())
    each(1, lambda d: tell(d).wait_send())
    each(1, lambda d: answer(d).wait_send())


def lookup(requests, table_t, live, field_t, counts, dense_t, domains):
    owners, cap = requests.shape
    width, rows = table_t.shape
    n_field, events = field_t.shape
    chunks = 6
    dma = pltpu.SemaphoreType.DMA
    return pl.pallas_call(
        lookup_kernel,
        in_specs=[vmem(), hbm(), smem(), vmem(), hbm(), vmem(), vmem()],
        out_specs=[vmem()] * 5,
        out_shape=[
            jax.ShapeDtypeStruct((n_field * width, events), bf16),
            jax.ShapeDtypeStruct((width, events), f32),
            jax.ShapeDtypeStruct((owners, 1, cap), i32),
            jax.ShapeDtypeStruct((owners, 1, cap), i32),
            jax.ShapeDtypeStruct((width, 128), f32),
        ],
        scratch_shapes=[
            pltpu.VMEM((owners, 1, cap), i32),
            pltpu.VMEM((owners, events, cap), bf16),
            pltpu.VMEM((width, rows), bf16),
            pltpu.VMEM((rows // 8, 128), f32),
            pltpu.VMEM((2 * cap, 128), f32),
            pltpu.VMEM((owners, 1, cap), i32),
            pltpu.SMEM((owners, 1, cap), i32),
            pltpu.VMEM((owners, width, cap), bf16),
            pltpu.VMEM((owners, width, cap), bf16),
            pltpu.VMEM((owners * width, cap), bf16),
            pltpu.VMEM((width, 128), f32),
            pltpu.VMEM((owners, width, 128), f32),
            dma((chunks,)),
            dma,
            dma,
        ]
        + [dma((owners,))] * 6,
        compiler_params=params(collective_id=1, has_side_effects=True),
        name="lookup",
    )(requests, table_t, live, field_t, counts, dense_t, domains)


STRIPE = 128
GATE_ROWS = 16
GELU_SCALE = math.sqrt(2.0 / math.pi)
GELU_CUBE = 0.044715


def gelu_and_slope(x):
    square = x * x
    t = jnp.tanh(GELU_SCALE * (x + GELU_CUBE * (square * x)))
    half = 0.5 * (1.0 + t)
    return x * half, half + 0.5 * x * (1.0 - t * t) * (GELU_SCALE * (1.0 + 3.0 * GELU_CUBE * square))


def standardise(values):
    center = values - jnp.mean(values, axis=-1, keepdims=True)
    inverse = lax.rsqrt(jnp.mean(center * center, axis=-1, keepdims=True) + EPSILON)
    return center * inverse, inverse


def standardise_back(d, standard, inverse):
    along = jnp.mean(d * standard, axis=-1, keepdims=True)
    return inverse * (d - jnp.mean(d, axis=-1, keepdims=True) - standard * along)


def loop(n, body):
    def step(i, carry):
        body(i)
        return carry

    lax.fori_loop(0, n, step, 0, unroll=2)


def columns(rows):
    have = rows.shape[0]
    if have < 8:
        rows = jnp.concatenate([rows, jnp.zeros((8 - have, rows.shape[1]), f32)], axis=0)
    return rows.T


def thirds(x):
    high = x.astype(bf16)
    rest = x - high.astype(f32)
    middle = rest.astype(bf16)
    return jnp.concatenate([high, middle, (rest - middle.astype(f32)).astype(bf16)], axis=0)


def domain_moments(stats):
    result = []
    for d in range(DOMAINS):
        count = stats[:, 2 * DOMAINS + d : 2 * DOMAINS + d + 1]
        mean = stats[:, d : d + 1] / count
        variance = stats[:, DOMAINS + d : DOMAINS + d + 1] / count - mean * mean
        result.append((mean, lax.rsqrt(variance + EPSILON), count))
    return result


def by_domain(domains, values):
    picked = values[0]
    for d in range(1, DOMAINS):
        picked = jnp.where(domains == d, values[d], picked)
    return picked


class Rows:
    def __init__(self, experts, units, depth, tower, width):
        self.next = 0
        lines = lambda n: -(-n // 128)
        self.b_in = [self.take(lines(units)) for _ in range(experts)]
        self.b_out, self.gain, self.bias = ([self.take(lines(depth)) for _ in range(experts)] for _ in range(3))
        self.proj_b, self.inter_gain, self.inter_bias = (self.take(lines(depth)) for _ in range(3))
        self.gates = [self.take(lines(depth)) for _ in range(SHARED + 2 * DOMAINS)]
        self.tower_in_bias, self.tower_out = ([self.take(lines(tower)) for _ in range(DOMAINS)] for _ in range(2))
        self.tower_out_bias = self.take(1)
        self.dense = self.take(width)

    def take(self, n):
        at, self.next = self.next, self.next + n
        return at

    def padded(self, devices):
        return -(-self.next // (8 * devices)) * 8 * devices


def put_row(small, at, row):
    for c in range(row.shape[1] // 128):
        small[at + c : at + c + 1, :] = row[:, c * 128 : (c + 1) * 128]


def learn_kernel(
    shape, blocks,
    fields, pooled, lengths, dense, domains, cotangent, stats, proj_w, proj_b, inter_gain, inter_bias,
    w_in_hbm, b_in, w_out_hbm, b_out, expert_gain, expert_bias, shared_gate, group_gate, tower_in, tower_in_bias, tower_out,
    tower_out_bias, field, counts_hbm,
    pred, centered, d_centered, returned, small_total, total_in, total_out, total_tower, total_proj,
    w_in, w_out, joined, pre_slope, pre_standard, pre_inverse, state_low, state_turned, coef,
    active, slope, standard, inverse, work, after, after_low, after_turned, d_tower, d_after, products,
    d_out, d_in, d_pooled, gates, counts, slot_total, slot_grad,
    small_part, small_inbox, part_in, part_out, part_tower, part_proj, inbox_in, inbox_out, inbox_tower, inbox_proj,
    small_own, own_in, own_out, own_tower, own_proj, in_sems, out_sems, count_sems, own_sems, sends, recvs, slot_sends, slot_recvs,
):
    experts, depth, units = w_in.shape
    width, events = dense.shape
    n_field = field.shape[0]
    owners, _, cap = slot_grad.shape
    tower_units = tower_in.shape[2]
    greet_all()
    for x in range(experts):
        pltpu.make_async_copy(w_in_hbm.at[x], w_in.at[x], in_sems.at[x]).start()
        pltpu.make_async_copy(w_out_hbm.at[x], w_out.at[x], out_sems.at[x]).start()

    which = domains[...]
    length = lengths[...].astype(f32)
    rows = [shared_gate[...].astype(f32)] + [group_gate[d].astype(f32) for d in range(DOMAINS)]
    have = SHARED + 2 * DOMAINS
    gates[...] = jnp.concatenate(rows + [jnp.zeros((GATE_ROWS - have, depth), f32)], axis=0).astype(bf16)
    moments = domain_moments(stats[...])
    mean, scale = (by_domain(which, [m[i] for m in moments]) for i in range(2))
    centered[...] = (dense[...] - mean) * scale
    joined[: n_field * width, :] = fields[...]
    joined[n_field * width : (n_field + 1) * width, :] = (pooled[...] / length).astype(bf16)
    joined[(n_field + 1) * width :, :] = centered[...].astype(bf16)
    joined_rows, d_state, d_fields = d_in.at[:, : joined.shape[0]], after, joined
    joined_rows[...] = joined[...].T
    quarter = 256

    def project(c):
        at = pl.ds(pl.multiple_of(c * quarter, quarter), quarter)
        work[:, at] = jnp.dot(joined_rows[...], proj_w[:, at], preferred_element_type=f32) + proj_b[:, at]

    loop(depth // quarter, project)

    def stripe(i):
        return pl.ds(pl.multiple_of(i * STRIPE, STRIPE), STRIPE)

    def start_state(i):
        at = stripe(i)
        value, pre_slope[at, :] = gelu_and_slope(work[at, :])
        pre_standard[at, :], pre_inverse[at, :] = standardise(value)
        state = pre_standard[at, :] * inter_gain[...] + inter_bias[...]
        after[at, :] = state
        state_low[at, :] = state.astype(bf16)

    loop(events // STRIPE, start_state)
    state_turned[...] = state_low[...].T
    logits = lax.dot_general(gates[...], state_low[...], NT, preferred_element_type=f32)

    def softmax_pair(a, b):
        top = jnp.maximum(a, b)
        a, b = jnp.exp(a - top), jnp.exp(b - top)
        return a / (a + b), b / (a + b)

    share = softmax_pair(logits[0:1], logits[1:2])
    group_logits = [
        by_domain(which, [logits[SHARED + 2 * d + i : SHARED + 2 * d + i + 1] for d in range(DOMAINS)]) for i in range(2)
    ]
    level = softmax_pair(*group_logits)
    here = [jnp.where(which == d, 1.0, 0.0) for d in range(DOMAINS)]
    weights = [level[0] * share[0], level[0] * share[1]] + [level[1] * here[d] for d in range(DOMAINS)]
    weight_columns = columns(jnp.concatenate(weights, axis=0))
    coef[...] = weight_columns

    def expert_forward(x):
        pltpu.make_async_copy(w_in_hbm.at[x], w_in.at[x], in_sems.at[x]).wait()

        def enter(c):
            at = pl.ds(pl.multiple_of(c * quarter, quarter), quarter)
            pre = jnp.dot(state_low[...], w_in[x, :, at], preferred_element_type=f32) + b_in[x : x + 1, at]
            value, rise = gelu_and_slope(pre)
            active[x, :, at] = value.astype(bf16)
            slope[x, :, at] = rise.astype(bf16)

        loop(units // quarter, enter)
        pltpu.make_async_copy(w_out_hbm.at[x], w_out.at[x], out_sems.at[x]).wait()

        def leave(c):
            at = pl.ds(pl.multiple_of(c * quarter, quarter), quarter)
            work[:, at] = jnp.dot(active[x], w_out[x, :, at], preferred_element_type=f32) + b_out[x : x + 1, at]

        loop(depth // quarter, leave)

        def mix(i):
            at = stripe(i)
            value, inverse[at, x : x + 1] = standardise(work[at, :])
            standard[x, at, :] = value.astype(bf16)
            after[at, :] += coef[at, x : x + 1] * (value * expert_gain[x : x + 1, :] + expert_bias[x : x + 1, :])

        loop(events // STRIPE, mix)

    for x in range(experts):
        expert_forward(x)
    after_low[...] = after[...].astype(bf16)
    after_turned[...] = after_low[...].T

    here_columns = columns(jnp.concatenate(here + [cotangent[...]], axis=0))
    logit = jnp.zeros((events, 1), f32)
    for d in range(DOMAINS):
        pre = jnp.dot(after_low[...], tower_in[d], preferred_element_type=f32) + tower_in_bias[d : d + 1, :]
        value, rise = gelu_and_slope(pre)
        work[:, d * tower_units : (d + 1) * tower_units] = value
        d_after[:, d * tower_units : (d + 1) * tower_units] = rise
        head = jnp.sum(value * tower_out[d : d + 1, :], axis=1, keepdims=True) + tower_out_bias[:, d : d + 1]
        logit = logit + here_columns[:, d : d + 1] * head
    chance = 1.0 / (1.0 + jnp.exp(-logit))
    d_logit = here_columns[:, DOMAINS : DOMAINS + 1] * chance * (1.0 - chance)
    pred[...] = jnp.broadcast_to(chance, (events, 8)).T[0:1, :]
    lane = lax.broadcasted_iota(i32, (1, 128), 1)
    bias_row = jnp.zeros((1, 128), f32)
    for d in range(DOMAINS):
        at = slice(d * tower_units, (d + 1) * tower_units)
        mine = d_logit * here_columns[:, d : d + 1]
        put_row(small_part, shape.tower_out[d], jnp.sum(mine * work[:, at], axis=0, keepdims=True))
        bias_row = jnp.where(lane == d, jnp.sum(mine, axis=0, keepdims=True), bias_row)
        low = (mine * tower_out[d : d + 1, :] * d_after[:, at]).astype(bf16)
        d_tower[d] = low
        put_row(small_part, shape.tower_in_bias[d], jnp.sum(low.astype(f32), axis=0, keepdims=True))
    small_part[shape.tower_out_bias : shape.tower_out_bias + 1, :] = bias_row

    wait_for_all()
    ways = orders()
    pieces, clock = [], [0]

    def pump():
        for piece in pieces:
            if not piece.done() and piece.sent_at < clock[0] - 2:
                piece.take()
                piece.sent_at = clock[0]
        clock[0] += 1

    def send(block, parts, inboxes, owns, totals, i, value):
        k = len(pieces)
        block.put(parts.at[i], value)
        piece = Piece(
            parts.at[i], inboxes.at[i], owns.at[i], totals.at[i], ways[k], own_sems.at[k], sends.at[k], recvs.at[k]
        )
        piece.send()
        piece.sent_at = clock[0]
        pieces.append(piece)

    towers = [jnp.dot(after_turned[...], d_tower[d], preferred_element_type=f32).astype(bf16) for d in range(DOMAINS)]
    send(blocks[2], part_tower, inbox_tower, own_tower, total_tower, 0, jnp.concatenate(towers, axis=0))
    d_after[...] = sum(
        lax.dot_general(d_tower[d], tower_in[d], NT, preferred_element_type=f32) for d in range(DOMAINS)
    )
    d_state[...] = d_after[...]

    products[...] = jnp.zeros(products.shape, f32)
    zero = jnp.zeros((1, depth), f32)
    half = units // 2
    for x in range(experts):

        def unmix(i, sums):
            at = stripe(i)
            d, value = d_after[at, :], standard[x, at, :].astype(f32)
            products[at, x : x + 1] = jnp.sum(d * (value * expert_gain[x : x + 1, :] + expert_bias[x : x + 1, :]), axis=1, keepdims=True)
            d = coef[at, x : x + 1] * d
            low = standardise_back(d * expert_gain[x : x + 1, :], value, inverse[at, x : x + 1]).astype(bf16)
            d_out[at, :] = low
            terms = (d * value, d, low.astype(f32))
            return tuple(s + jnp.sum(t, axis=0, keepdims=True) for s, t in zip(sums, terms))

        for place, row in zip((shape.gain[x], shape.bias[x], shape.b_out[x]),
                              lax.fori_loop(0, events // STRIPE, unmix, (zero,) * 3, unroll=2)):
            put_row(small_part, place, row)
        pump()
        for h in range(2):
            value = lax.dot_general(active[x, :, h * half : (h + 1) * half], d_out[...], TN, preferred_element_type=f32)
            send(blocks[1], part_out, inbox_out, own_out, total_out, 2 * x + h, value.astype(bf16))

        def unenter(c):
            at = pl.ds(pl.multiple_of(c * quarter, quarter), quarter)
            d = lax.dot_general(d_out[...], w_out[x, at, :], NT, preferred_element_type=f32)
            low = (d * slope[x, :, at].astype(f32)).astype(bf16)
            d_in[:, at] = low
            row = jnp.sum(low.astype(f32), axis=0, keepdims=True)
            for q in range(quarter // 128):
                small_part[pl.ds(shape.b_in[x] + c * (quarter // 128) + q, 1), :] = row[:, q * 128 : (q + 1) * 128]

        loop(units // quarter, unenter)
        for h in range(2):
            value = jnp.dot(state_turned[...], d_in[:, h * half : (h + 1) * half], preferred_element_type=f32)
            send(blocks[0], part_in, inbox_in, own_in, total_in, 2 * x + h, value.astype(bf16))

        def unstate(c):
            at = pl.ds(pl.multiple_of(c * quarter, quarter), quarter)
            d_state[:, at] += lax.dot_general(d_in[...], w_in[x, at, :], NT, preferred_element_type=f32)

        loop(depth // quarter, unstate)
        pump()

    ahead = counts.shape[0]

    def fetch(o):
        slot = o % ahead if isinstance(o, int) else lax.rem(o, ahead)
        return pltpu.make_async_copy(counts_hbm.at[o], counts.at[slot], count_sems.at[slot])

    for o in range(ahead):
        fetch(o).start()
    q = products[...].T
    q = [q[x : x + 1] for x in range(experts)]
    d_level = (share[0] * q[0] + share[1] * q[1], by_domain(which, q[SHARED:]))
    mean_share = share[0] * q[0] + share[1] * q[1]
    d_share = [level[0] * share[s] * (q[s] - mean_share) for s in range(SHARED)]
    mean_level = level[0] * d_level[0] + level[1] * d_level[1]
    d_group = [level[i] * (d_level[i] - mean_level) for i in range(2)]
    rows = d_share + [d_group[i] * here[d] for d in range(DOMAINS) for i in range(2)]
    d_logits = jnp.concatenate(rows + [jnp.zeros((GATE_ROWS - len(rows), events), f32)], axis=0)
    split = thirds(d_logits)
    gate_sums = jnp.dot(split, state_low[...], preferred_element_type=f32)
    gate_sums = sum(gate_sums[i * GATE_ROWS : (i + 1) * GATE_ROWS] for i in range(3))
    for i, place in enumerate(shape.gates):
        put_row(small_part, place, gate_sums[i : i + 1])
    gates_thrice = jnp.concatenate([gates[...]] * 3, axis=0)
    d_state[...] += lax.dot_general(split, gates_thrice, TN, preferred_element_type=f32)

    def unstart(i, sums):
        at = stripe(i)
        d, value = d_state[at, :], pre_standard[at, :]
        low = (standardise_back(d * inter_gain[...], value, pre_inverse[at, :]) * pre_slope[at, :]).astype(bf16)
        d_out[at, :] = low
        terms = (d * value, d, low.astype(f32))
        return tuple(s + jnp.sum(t, axis=0, keepdims=True) for s, t in zip(sums, terms))

    for place, row in zip((shape.inter_gain, shape.inter_bias, shape.proj_b),
                          lax.fori_loop(0, events // STRIPE, unstart, (zero,) * 3, unroll=2)):
        put_row(small_part, place, row)
    value = jnp.dot(joined[...], d_out[...], preferred_element_type=f32)
    send(blocks[3], part_proj, inbox_proj, own_proj, total_proj, 0, value.astype(bf16))
    n_all = n_field * width
    d_fields[:n_all, :] = lax.dot_general(proj_w[:n_all, :], d_out[...], NT, preferred_element_type=f32).astype(bf16)
    tail = lax.dot_general(proj_w[n_all:, :], d_out[...], NT, preferred_element_type=f32)
    d_pooled[...] = (tail[:width] / length).astype(bf16)
    d_centered[...] = tail[width:]
    lanes = lax.broadcasted_iota(i32, (width, 128), 1)
    sums = jnp.zeros((width, 128), f32)
    for d in range(DOMAINS):
        mine = jnp.where(which == d, tail[width:], 0.0)
        for k, term in enumerate((mine, mine * centered[...])):
            sums = jnp.where(lanes == k * DOMAINS + d, jnp.sum(term, axis=1, keepdims=True), sums)
    small_part[shape.dense : shape.dense + width, :] = sums
    if small_part.shape[0] > shape.next:
        small_part[shape.next :, :] = jnp.zeros((small_part.shape[0] - shape.next, 128), f32)
    k = len(pieces)
    small_piece = Piece(
        small_part, small_inbox, small_own, small_total, ways[0], own_sems.at[k], sends.at[k], recvs.at[k]
    )
    small_piece.send()
    small_piece.sent_at = clock[0]
    pieces.append(small_piece)
    pump()

    shift = cap.bit_length() - 1
    slot_total[...] = jnp.zeros(slot_total.shape, f32)

    def scatter(f, carry):
        wide, hots = [], []
        for k in range(2):
            slot = field[pl.ds(f * 2 + k, 1), :]
            owner = jnp.broadcast_to(jnp.right_shift(slot, shift), (width, events))
            d = d_fields[pl.ds(pl.multiple_of((f * 2 + k) * width, width), width), :].astype(f32)
            wide.append(
                jnp.concatenate([jnp.where(owner == o, d, 0.0).astype(bf16) for o in range(owners)], axis=0)
            )
            hots.append(hot(cap, jnp.bitwise_and(slot, cap - 1)))
        slot_total[...] += lax.dot_general(
            jnp.concatenate(wide, axis=1), jnp.concatenate(hots, axis=1), NT, preferred_element_type=f32
        )
        return carry

    for first in range(0, n_field // 2, 2):
        lax.fori_loop(first, min(first + 2, n_field // 2), scatter, 0)
        pump()

    def spread(o):
        fetch(o).wait()
        behave = jnp.dot(d_pooled[...], counts[lax.rem(o, ahead)], preferred_element_type=f32)
        at = pl.ds(pl.multiple_of(o * width, width), width)
        slot_grad[o] = (slot_total[at, :] + behave).astype(bf16)
        pl.when(o + ahead < owners)(lambda: fetch(o + ahead).start())

    for first in range(0, owners, owners // 8):

        def spread_some(o, carry):
            spread(o)
            return carry

        lax.fori_loop(first, first + owners // 8, spread_some, 0)
        pump()
    me = lax.axis_index("wide") * lax.axis_size("narrow") + lax.axis_index("narrow")
    slot_copies = []
    for d, other, place in everyone_else():
        copy = pltpu.make_async_remote_copy(
            src_ref=slot_grad.at[other], dst_ref=returned.at[me], send_sem=slot_sends.at[d],
            recv_sem=slot_recvs.at[d], device_id=place, device_id_type=MESH)
        copy.start()
        slot_copies.append(copy)
    returned[me] = slot_grad[me]

    while any(not piece.done() for piece in pieces):
        for piece in pieces:
            if not piece.done():
                piece.take()
    for copy in slot_copies:
        copy.wait_recv()
    for copy in slot_copies:
        copy.wait_send()
    for piece in pieces:
        piece.drain()


def learn(fields, pooled, lengths, dense, domains, cotangent, stats, model, field, counts, devices):
    w_in, tower_in, proj_w = model[4], model[12], model[0]
    experts, depth, units = w_in.shape
    width, events = dense.shape
    owners, _, cap = counts.shape
    tower_units = tower_in.shape[2]
    half = units // 2
    shape = Rows(experts, units, depth, tower_units, width)
    n_small = shape.padded(devices)
    blocks = [
        Block(depth, half, devices), Block(half, depth, devices),
        Block(DOMAINS * depth, tower_units, devices), Block(proj_w.shape[0], depth, devices),
    ]
    numbers = (2 * experts, 2 * experts, 1, 1)
    pieces = [(n, b.padded, b.lanes) for n, b in zip(numbers, blocks)]
    steps = 2 * (devices.bit_length() - 1)
    n_pieces = sum(numbers) + 1
    joined = proj_w.shape[0]
    ahead = max(4, min(16, 512 // devices))
    space = lambda *s: pltpu.VMEM(s, f32)
    low = lambda *s: pltpu.VMEM(s, bf16)
    dma = lambda *s: pltpu.SemaphoreType.DMA(s)
    in_specs = [vmem()] * 25
    in_specs[11] = in_specs[13] = in_specs[24] = hbm()
    out = pl.pallas_call(
        functools.partial(learn_kernel, shape, blocks),
        in_specs=in_specs,
        out_specs=[vmem()] * 4 + [hbm()] * 5,
        out_shape=[
            jax.ShapeDtypeStruct((1, events), f32),
            jax.ShapeDtypeStruct((width, events), f32),
            jax.ShapeDtypeStruct((width, events), f32),
            jax.ShapeDtypeStruct((owners, width, cap), bf16),
            jax.ShapeDtypeStruct((n_small, 128), f32),
        ]
        + [jax.ShapeDtypeStruct(s, bf16) for s in pieces],
        scratch_shapes=[
            low(experts, depth, units), low(experts, units, depth), low(joined, events),
            space(events, depth), space(events, depth), space(events, 1), low(events, depth),
            low(depth, events), space(events, 8), low(experts, events, units), low(experts, events, units),
            low(experts, events, depth), space(events, 8), space(events, depth), space(events, depth),
            low(events, depth), low(depth, events), low(DOMAINS, events, tower_units), space(events, depth),
            space(events, 8), low(events, depth), low(events, units), low(width, events), low(GATE_ROWS, depth), low(ahead, events, cap), space(owners * width, cap),
            low(owners, width, cap), space(n_small, 128), space(n_small, 128),
        ]
        + [pltpu.VMEM(s, bf16) for s in pieces] * 2
        + [space(n_small // devices, 128)]
        + [low(n, rows // devices, lanes) for n, rows, lanes in pieces]
        + [dma(experts), dma(experts), dma(ahead), dma(n_pieces), dma(n_pieces, steps), dma(n_pieces, steps), dma(devices), dma(devices)],
        compiler_params=params(collective_id=0, has_side_effects=True),
        name="learn",
    )(fields, pooled, lengths, dense, domains, cotangent, stats, *model, field, counts)
    return out[:5], [b.whole(t, n) for b, t, n in zip(blocks, out[5:], numbers)], shape


def get_row(small, at, n):
    return jnp.concatenate([small[at + c : at + c + 1, :] for c in range(n // 128)], axis=1)


def finish_kernel(shape, line, line_v, group, returned, domains, stats, centered, d_centered, small, *refs):
    more, out, more_out = refs[:4], refs[4], refs[5:9]
    d_dense, b_in, b_out, gain, bias, proj_b, inter_gain, inter_bias, shared_gate, group_gate, tower_in_bias, tower_out, tower_bias = refs[9:22]
    lines, vals = refs[22:]
    step = pl.program_id(0)
    per = out.shape[1] // ROW_CHUNK

    @pl.when(step == 0)
    def _():
        for target, places in (
            (b_in, shape.b_in), (b_out, shape.b_out), (gain, shape.gain), (bias, shape.bias),
            (proj_b, [shape.proj_b]), (inter_gain, [shape.inter_gain]), (inter_bias, [shape.inter_bias]),
            (shared_gate, shape.gates[:SHARED]), (tower_in_bias, shape.tower_in_bias), (tower_out, shape.tower_out),
        ):
            for i, at in enumerate(places):
                target[i : i + 1, :] = get_row(small, at, target.shape[1])
        for i, at in enumerate(shape.gates[SHARED:]):
            group_gate[i // 2, i % 2 : i % 2 + 1, :] = get_row(small, at, group_gate.shape[2])
        tower_bias[...] = small[shape.tower_out_bias : shape.tower_out_bias + 1, : tower_bias.shape[1]]
        which = domains[...]
        sums = small[shape.dense : shape.dense + centered.shape[0], :]
        moments = domain_moments(stats[...])
        scale = by_domain(which, [m[1] for m in moments])
        straight = by_domain(which, [sums[:, d : d + 1] / m[2] for d, m in enumerate(moments)])
        cross = by_domain(which, [sums[:, DOMAINS + d : DOMAINS + d + 1] / m[2] for d, m in enumerate(moments)])
        d_dense[...] = scale * (d_centered[...] - straight - centered[...] * cross)

        def clear(i, carry):
            lines[pl.ds(pl.multiple_of(i * 1024, 1024), 1024), :] = jnp.zeros((1024, 128), f32)
            return carry

        lax.fori_loop(0, lines.shape[0] // 1024, clear, 0)

    width, cap = returned.shape[1:]

    @pl.when(step < ADD_STEPS)
    def _():
        batch = 32
        a = lax.div(lax.broadcasted_iota(i32, (cap, cap), 0), batch)
        near = a == lax.div(lax.broadcasted_iota(i32, (cap, cap), 1), batch)
        each = group.shape[0] // ADD_STEPS

        def prepare(s, slot):
            which, own = jnp.broadcast_to(group[s], (width, cap)), returned[s].astype(f32)
            wide = jnp.concatenate([jnp.where(which == g, own, 0.0) for g in range(8)], axis=0)
            along = jnp.broadcast_to(line_v[s].astype(f32), (cap, cap))
            same = jnp.where(jnp.logical_and(along == along.T, near), 1.0, 0.0).astype(bf16)
            vals[slot] = lax.dot_general(same, wide.astype(bf16), NT, preferred_element_type=f32)

        def add(s, slot):
            for u in range(0, cap, batch):
                places, sums = [], []
                for j in range(u, u + batch):
                    places.append(line[s * cap + j])
                    sums.append(lines[pl.ds(places[-1], 1), :] + vals[slot, j : j + 1, :])
                for place, total in zip(places, sums):
                    lines[pl.ds(place, 1), :] = total

        prepare(step * each, 0)

        def serve(i, carry):
            s = step * each + i * 2
            prepare(s + 1, 1)
            add(s, 0)
            prepare(jnp.minimum(s + 2, group.shape[0] - 1), 0)
            add(s + 1, 1)
            return carry

        lax.fori_loop(0, each // 2, serve, 0)
        for source, target in zip(more, more_out):
            tall, blocks, rows, lanes = source.shape
            for s in range(tall):
                for c in range(blocks):
                    target[s * rows : (s + 1) * rows, c * lanes : (c + 1) * lanes] = source[s, c].astype(f32)

    @pl.when(step >= ADD_STEPS)
    def _():
        def turn(c, carry):
            at = pl.multiple_of(((step - ADD_STEPS) * per + c) * 128, 128)
            turned = lines[pl.ds(at, 128), :].T
            for g in range(8):
                at = pl.multiple_of(c * ROW_CHUNK + g * 128, 128)
                out[:, pl.ds(at, 128)] = turned[g * width : (g + 1) * width]
            return carry

        lax.fori_loop(0, per, turn, 0, unroll=24)


def finish(shape, line, group, returned, domains, stats, centered, d_centered, small, more, rows):
    blocks, width, cap = returned.shape
    events = centered.shape[1]
    experts, units, depth = len(shape.b_in), more[0].shape[1] * more[0].shape[3], more[0].shape[2]
    tower = more[2].shape[1] * more[2].shape[3]
    steps, turns = ADD_STEPS, 4
    early = lambda i: jnp.minimum(i, steps - 1)
    in_more, out_more, shapes = [], [], []
    for x in more:
        tall, parts, r, lanes = x.shape
        if tall > 1:
            in_more.append(pl.BlockSpec((tall // steps, parts, r, lanes), lambda i: (early(i), 0, 0, 0)))
        else:
            in_more.append(pl.BlockSpec((1, parts, r // steps, lanes), lambda i: (0, 0, early(i), 0)))
        out_more.append(pl.BlockSpec((tall * r // steps, parts * lanes), lambda i: (early(i), 0)))
        shapes.append((tall * r, parts * lanes))
    shapes += [(width, events), (experts, units)] + [(experts, depth)] * 3 + [(1, depth)] * 3
    shapes += [(SHARED, depth), (DOMAINS, 2, depth), (DOMAINS, tower), (DOMAINS, tower), (1, DOMAINS)]
    return pl.pallas_call(
        functools.partial(finish_kernel, shape),
        grid=(steps + turns,),
        in_specs=[smem()] + [vmem()] * 8 + in_more,
        out_specs=[pl.BlockSpec((width, rows // turns), lambda i: (0, jnp.maximum(i - steps, 0)))] + out_more + [vmem()] * 13,
        out_shape=[jax.ShapeDtypeStruct(s, f32) for s in [(width, rows)] + shapes],
        scratch_shapes=[pltpu.VMEM((rows // 8, 128), f32), pltpu.VMEM((2, cap, 128), f32)],
        compiler_params=params(),
        name="finish",
    )(line.reshape(-1), line, group, returned, domains, stats, centered, d_centered, small, *more)


def local(
    table,
    dense,
    domains,
    lengths,
    requests,
    counts,
    field_slots,
    behave_slots,
    proj_w,
    proj_b,
    inter_gain,
    inter_bias,
    w_in,
    b_in,
    w_out,
    b_out,
    expert_gain,
    expert_bias,
    shared_gate,
    group_gate,
    tower_in,
    tower_in_bias,
    tower_out,
    tower_out_bias,
    pred_cotangent,
):
    devices = lax.axis_size("wide") * lax.axis_size("narrow")
    capacity = requests.shape[2]
    experts, depth, units = w_in.shape
    counts_of = slot_counts(lengths, behave_slots.reshape(-1, 128), devices, capacity)
    field = field_slots.T
    dense_t, which = dense.T, domains[None]
    fields, pooled, line, group, stats = lookup(
        requests[0], table.T, counts.reshape(-1), field, counts_of, dense_t, which
    )
    model = (
        proj_w, proj_b[None], inter_gain[None], inter_bias[None], w_in, b_in, w_out, b_out, expert_gain, expert_bias,
        shared_gate.T, group_gate.transpose(0, 2, 1), tower_in, tower_in_bias, tower_out, tower_out_bias[None],
    )
    (pred, centered, d_centered, returned, small), totals, shape = learn(
        fields, pooled, lengths, dense_t, which, pred_cotangent[None], stats, model, field, counts_of, devices
    )
    totals[0] = totals[0].reshape(experts, -1, depth, totals[0].shape[3])
    out = finish(shape, line, group, returned, which, stats, centered, d_centered, small, totals, table.shape[0])
    d_table, d_w_in, d_w_out, d_tower_in, d_proj_w, d_dense, d_b_in, d_b_out, d_gain, d_bias = out[:10]
    d_proj_b, d_inter_gain, d_inter_bias, d_shared_gate, d_group_gate, d_tower_in_bias, d_tower_out, d_tower_bias = out[10:]
    return (
        pred[0],
        d_dense.T,
        d_table.T,
        d_proj_w,
        d_proj_b[0],
        d_inter_gain[0],
        d_inter_bias[0],
        d_w_in.reshape(w_in.shape),
        d_b_in,
        d_w_out.reshape(w_out.shape),
        d_b_out,
        d_gain,
        d_bias,
        d_shared_gate.T,
        d_group_gate.transpose(0, 2, 1),
        d_tower_in.reshape(tower_in.shape),
        d_tower_in_bias,
        d_tower_out,
        d_tower_bias[0],
    )


def solution(mesh):
    placed = (
        P(("wide", "narrow"), None),
        P(("wide", "narrow"), None),
        P(("wide", "narrow")),
        P(("wide", "narrow"), None),
        P(("wide", "narrow"), None, None),
        P(("wide", "narrow"), None),
        P(("wide", "narrow"), None),
        P(("wide", "narrow"), None),
        P(),
        P(),
        P(),
        P(),
        P(),
        P(),
        P(),
        P(),
        P(),
        P(),
        P(),
        P(),
        P(),
        P(),
        P(),
        P(),
        P(("wide", "narrow")),
    )
    return jax.shard_map(
        local,
        mesh=mesh,
        in_specs=placed,
        out_specs=(
            P(("wide", "narrow")),
            P(("wide", "narrow"), None),
            P(("wide", "narrow"), None),
            P(),
            P(),
            P(),
            P(),
            P(),
            P(),
            P(),
            P(),
            P(),
            P(),
            P(),
            P(),
            P(),
            P(),
            P(),
            P(),
        ),
        check_vma=False,
    )
```
